256 devices in a mesh: dp: 32 (over x, z_hi, core), seq: 8 (over z_lo, y).
Axes of the slice: x: 4, y: 4, z: 8 (z_hi: 4, z_lo: 2; z = z_hi * 2 + z_lo), core: 2. Of those that a mesh axis runs over, the one named last changes fastest.
Arguments:
- normed: bfloat16 [32, 2048, 1536], P('dp', 'seq'), may hold values from -6 to 6
- w_query: bfloat16 [1536, 512], replicated, may hold values from -1.5 to 1.5
- w_key: bfloat16 [1536, 128], replicated, may hold values from -1.5 to 1.5
- w_value: bfloat16 [1536, 128], replicated, may hold values from -0.15625 to 0.15625
- w_out: bfloat16 [1536, 512], replicated, may hold values from -0.25 to 0.25
- cotangent: bfloat16 [32, 2048, 1536], P('dp', 'seq'), may hold values from -6 to 6
Outputs:
- branch: bfloat16 [32, 2048, 1536], P('dp', 'seq')
- grad_query: float32 [1536, 512], P(('dp', 'seq'))
- grad_key: float32 [1536, 128], P(('dp', 'seq'))
- grad_value: float32 [1536, 128], P(('dp', 'seq'))
- grad_out: float32 [1536, 512], P(('dp', 'seq'))
The draws below stay inside these ranges and needn't reach their ends.
All inputs are finite; a program needn't handle non-finite values.
Results may differ from the reference program's by a relative error of at most 0.006.
The reference program's roundings to bfloat16 on the way (of `queries`, `probs_b`, `attended`, `d_att`, `d_scores` and `d_query`) count: a program that leaves them out, or rounds other values in their place, can miss the bound.
Values may be sent and summed in bfloat16 or wider, within the bound.
No kernel may reach another device: no remote copies, remote signals or barrier semaphores. Data moves between devices by JAX's collectives and lax.ppermute only.
A program may use at most 64 MiB of HBM per device.

```python
import jax
import jax.numpy as jnp
from jax import lax

D = 1536
HEADS = 4
HD = 128
INNER = 512
SEQ_LEN = 2048
EXAMPLES = 32


def query_table(key):
    return jax.random.uniform(key, (D, HEADS * HD), jnp.float32, -1.0, 1.0) * (3.0 / D) ** 0.5


def draw_w_query(key, part):
    table = query_table(key)
    return table.astype(jnp.bfloat16)


def draw_w_key(key, part):
    key = jax.random.fold_in(key, 12)
    fresh = jax.random.uniform(key, (D, HD), jnp.float32, -1.0, 1.0) * (3.0 / D) ** 0.5
    return fresh.astype(jnp.bfloat16)


def levels(key, extent, cuts, smallest, top_value):
    def one(axis_at, parts):
        steps = jax.random.uniform(jax.random.fold_in(jax.random.fold_in(key, 6), axis_at), (parts,), jnp.float32, smallest / len(cuts), top_value / len(cuts))
        return jnp.repeat(jnp.exp(steps), extent[axis_at] // parts).reshape((-1,) + (1,) * (len(extent) - axis_at - 1))

    gain = one(*cuts[0])
    for cut in cuts[1:]:
        gain = gain * one(*cut)
    return gain


def bell_draw(own_key, shape, spread, reach, shards=(), held_as=jnp.bfloat16):
    gain = levels(own_key, shape, shards, -0.22, 0.18) if shards else 1.0
    drawn = jax.random.normal(own_key, shape, jnp.float32) * spread * gain
    return jnp.minimum(jnp.maximum(drawn, -reach), reach).astype(held_as)


def setup_inputs(seed: int = 0) -> dict:
    key_of = jax.random.split(jax.random.key(seed), 7)
    normed = bell_draw(key_of[0], (EXAMPLES, SEQ_LEN, D), 1.0, 6.0, ((0, 32), (1, 8)))
    w_query = draw_w_query(jax.random.fold_in(key_of[6], 71), 0)
    w_key = draw_w_key(jax.random.fold_in(key_of[6], 71), 0)
    w_value = bell_draw(key_of[3], (D, HD), D ** -0.5, 0.15625)
    w_out = bell_draw(key_of[4], (D, INNER), INNER ** -0.5, 0.25)
    cotangent = bell_draw(key_of[5], (EXAMPLES, SEQ_LEN, D), 1.0, 6.0, ((0, 32), (1, 8)))
    return dict(normed=normed, w_query=w_query, w_key=w_key, w_value=w_value, w_out=w_out, cotangent=cotangent)


def contract_rows(left, right):
    return lax.dot_general(left, right, (((0,), (0,)), ((), ())), preferred_element_type=jnp.float32)


def contract_rows_exact(left, right):
    return lax.dot_general(left.astype(jnp.float32), right, (((0,), (0,)), ((), ())),
                           precision=lax.Precision.HIGHEST, preferred_element_type=jnp.float32)


def one_example(hidden, grads_in, w_query, w_key, w_value, w_out):
    length = hidden.shape[0]
    scale = HD ** -0.5
    queries = jnp.dot(hidden, w_query, preferred_element_type=jnp.float32).astype(jnp.bfloat16)
    keys = jnp.dot(hidden, w_key, preferred_element_type=jnp.float32).astype(jnp.bfloat16)
    values = jnp.dot(hidden, w_value, preferred_element_type=jnp.float32).astype(jnp.bfloat16)
    query_rows = queries.reshape(length * HEADS, HD)
    scores = jnp.dot(query_rows, keys.T, preferred_element_type=jnp.float32) * scale
    shifted = jnp.exp(scores - jnp.max(scores, axis=1, keepdims=True))
    probs = shifted / jnp.sum(shifted, axis=1, keepdims=True)
    probs_b = probs.astype(jnp.bfloat16)
    attended = jnp.dot(probs_b, values, preferred_element_type=jnp.float32).astype(jnp.bfloat16).reshape(length, HEADS * HD)
    branch = lax.dot_general(attended, w_out, (((1,), (1,)), ((), ())), preferred_element_type=jnp.float32).astype(jnp.bfloat16)
    d_att = jnp.dot(grads_in, w_out, preferred_element_type=jnp.float32).astype(jnp.bfloat16).reshape(length * HEADS, HD)
    d_probs = jnp.dot(d_att, values.T, preferred_element_type=jnp.float32)
    delta = jnp.sum(d_probs * probs, axis=1, keepdims=True)
    d_scores = (probs * (d_probs - delta)).astype(jnp.bfloat16)
    d_query = (jnp.dot(d_scores, keys, preferred_element_type=jnp.float32) * scale).astype(jnp.bfloat16).reshape(length, HEADS * HD)
    d_key = contract_rows(d_scores, query_rows) * scale
    d_value = contract_rows(probs_b, d_att)
    grad_query = contract_rows(hidden, d_query)
    grad_out = contract_rows(grads_in, attended)
    grad_key = contract_rows_exact(hidden, d_key)
    grad_value = contract_rows_exact(hidden, d_value)
    return branch, (grad_query, grad_key, grad_value, grad_out)


def reference(normed, w_query, w_key, w_value, w_out, cotangent):
    def step(totals, item):
        branch, grads = one_example(item[0], item[1], w_query, w_key, w_value, w_out)
        return tuple(a + b for a, b in zip(totals, grads)), branch

    start = (jnp.zeros((D, HEADS * HD), jnp.float32), jnp.zeros((D, HD), jnp.float32),
             jnp.zeros((D, HD), jnp.float32), jnp.zeros((D, HEADS * HD), jnp.float32))
    totals, branch = lax.scan(step, start, (normed, cotangent))
    return branch, totals[0], totals[1], totals[2], totals[3]
```

```python
import jax
import jax.numpy as jnp
import numpy as np
from jax import lax
from jax.experimental import pallas as pl
from jax.experimental.pallas import tpu as pltpu
from jax.sharding import PartitionSpec as P

HEADS = 4
HD = 128
SCALE = HD ** (-0.5)
LOG2_E = 1.4426950408889634
AXES = ("dp", "seq")
MIB = 1024 * 1024


def place(x, y, z, core):
    return x * 64 + (z >> 1) * 16 + core * 8 + (z & 1) * 4 + y


YZ_GROUPS = [[place(x, y, z, c) for y in range(4) for z in range(8)] for x in range(4) for c in range(2)]
ROW_ORDER = np.concatenate(
    [
        np.arange(6) + 6 * place(x, y, z, c)
        for c in range(2)
        for x in range(4)
        for y in range(4)
        for z in range(8)
    ]
)


def dot(left, right, dims):
    return lax.dot_general(left, right, (dims, ((), ())), preferred_element_type=jnp.float32)


def exchange(value, mask):
    return lax.ppermute(value, AXES, [(i, i ^ mask) for i in range(256)])


def from_other_core(value):
    return exchange(value, 8)


def exponent(values):
    top = jnp.max(jnp.max(jnp.abs(values), axis=0, keepdims=True), axis=1, keepdims=True)
    return jnp.ceil(jnp.log2(jnp.maximum(top, 1e-30))) - 13.0


def unscaled(ref, block, values, exponents):
    return ref[block, values, :] * jnp.exp2(ref[block, exponents, :])


def attention_kernel(q_ref, da_ref, k_ref, v_ref, factor_ref, copy_ref, dkv_ref):
    step = pl.program_id(0)
    keys = k_ref[...]
    values = v_ref[...]
    bf = jnp.bfloat16
    heads = range(q_ref.shape[1] // HD)
    q = [q_ref[:, h * HD : (h + 1) * HD] for h in heads]
    da = [da_ref[:, h * HD : (h + 1) * HD] for h in heads]

    def softmax(scores):
        shifted = jnp.exp2((scores - jnp.max(scores, axis=1, keepdims=True)) * (SCALE * LOG2_E))
        return shifted * (1.0 / jnp.sum(shifted, axis=1, keepdims=True))

    def store(side, h, value):
        factor_ref[side, :, h * HD : (h + 1) * HD] = value
        copy_ref[side, :, h * HD : (h + 1) * HD] = value

    scores = [dot(q[h], keys, ((1,), (1,))) for h in heads]
    probs, probs_b, d_probs, d_scores = [], [], [], []
    for h in heads:
        probs.append(softmax(scores[h]))
        probs_b.append(probs[h].astype(bf))
        d_probs.append(dot(da[h], values, ((1,), (1,))))
    d_value = None
    for h in heads:
        store(1, h, dot(probs_b[h], values, ((1,), (0,))).astype(bf))
        term = dot(da[h], probs_b[h], ((0,), (0,)))
        d_value = term if d_value is None else d_value + term
        delta = jnp.sum(d_probs[h] * probs[h], axis=1, keepdims=True)
        d_scores.append((probs[h] * (d_probs[h] - delta)).astype(bf))
    d_key = None
    for h in heads:
        store(0, h, (dot(d_scores[h], keys, ((1,), (0,))) * SCALE).astype(bf))
        term = dot(q[h], d_scores[h], ((0,), (0,)))
        d_key = term if d_key is None else d_key + term
    blocks, _, tokens = dkv_ref.shape

    @pl.when(step == 0)
    def _():
        for b in range(blocks):
            dkv_ref[b, :HD, :] = d_key[:, b * tokens : (b + 1) * tokens]
            dkv_ref[b, HD : 2 * HD, :] = d_value[:, b * tokens : (b + 1) * tokens]

    @pl.when(step != 0)
    def _():
        for b in range(blocks):
            dkv_ref[b, :HD, :] += d_key[:, b * tokens : (b + 1) * tokens]
            dkv_ref[b, HD : 2 * HD, :] += d_value[:, b * tokens : (b + 1) * tokens]

    @pl.when(step == pl.num_programs(0) - 1)
    def _():
        for i, scale in enumerate((SCALE, 1.0)):
            rows = pl.ds(i * HD, HD)
            top = jnp.abs(dkv_ref[0, rows, :])
            for b in range(1, blocks):
                top = jnp.maximum(top, jnp.abs(dkv_ref[b, rows, :]))
            power = exponent(top * scale)
            factor = jnp.exp2(-power) * scale
            for b in range(blocks):
                dkv_ref[b, rows, :] = dkv_ref[b, rows, :] * factor
                dkv_ref[b, pl.ds(2 * HD + 8 * i, 8), :] = jnp.broadcast_to(power, (8, tokens))


def attention(queries, d_att, keys_values):
    tokens, inner = queries.shape
    length = keys_values.shape[0]
    by_pair = pl.BlockSpec((tokens, 2 * HD), lambda j: (0, j))
    terms = (length // tokens, 2 * HD + 16, tokens)
    return pl.pallas_call(
        attention_kernel,
        grid=(HEADS // 2,),
        in_specs=[
            by_pair,
            by_pair,
            pl.BlockSpec((length, HD), lambda j: (0, 0)),
            pl.BlockSpec((length, HD), lambda j: (0, 1)),
        ],
        out_specs=[
            pl.BlockSpec((2, tokens, 2 * HD), lambda j: (0, 0, j)),
            pl.BlockSpec((2, tokens, 2 * HD), lambda j: (0, 0, j)),
            pl.BlockSpec(terms, lambda j: (0, 0, 0)),
        ],
        out_shape=[
            jax.ShapeDtypeStruct((2, tokens, inner), jnp.bfloat16),
            jax.ShapeDtypeStruct((2, tokens, inner), jnp.bfloat16),
            jax.ShapeDtypeStruct(terms, jnp.float32),
        ],
        compiler_params=pltpu.CompilerParams(vmem_limit_bytes=32 * MIB),
        cost_estimate=pl.CostEstimate(
            flops=12 * tokens * inner * length, bytes_accessed=4 << 20, transcendentals=tokens * HEADS * length
        ),
        name="attention",
    )(queries, d_att, keys_values, keys_values)


def store_scaled(product, out_ref, first, cols, mask):
    power = exponent(product)
    scaled = product * jnp.exp2(-power)
    receivers, padded, _ = out_ref.shape
    rows = padded - 8
    for i in range(receivers):
        out_ref[i ^ mask, :rows, pl.ds(first, cols)] = scaled[i * rows : (i + 1) * rows]
        out_ref[i, rows:, pl.ds(first, cols)] = jnp.broadcast_to(power, (8, cols))


def wide_kernel(x_ref, mine_ref, theirs_ref, own_ref, other_ref, out_ref):
    product = dot(mine_ref[0], own_ref[0], ((1,), (0,))) + dot(theirs_ref[0], other_ref[0], ((1,), (0,)))
    store_scaled(product, out_ref, 0, product.shape[1], x_ref[0])


def wide_products(x, mine, theirs, own, other):
    _, rows, tokens = mine.shape
    inner = own.shape[2]
    side = pl.BlockSpec((1, rows, tokens), lambda i, x: (i, 0, 0))
    factor = pl.BlockSpec((1, tokens, inner), lambda i, x: (i, 0, 0))
    return pl.pallas_call(
        wide_kernel,
        grid_spec=pltpu.PrefetchScalarGridSpec(
            num_scalar_prefetch=1,
            grid=(2,),
            in_specs=[side, side, factor, factor],
            out_specs=pl.BlockSpec((4, rows // 4 + 8, inner), lambda i, x: (0, 0, i)),
        ),
        out_shape=jax.ShapeDtypeStruct((4, rows // 4 + 8, 2 * inner), jnp.float32),
        compiler_params=pltpu.CompilerParams(vmem_limit_bytes=16 * MIB),
        cost_estimate=pl.CostEstimate(flops=8 * rows * tokens * inner, bytes_accessed=5 << 20, transcendentals=0),
        name="wide",
    )(x.reshape(1), mine, theirs, own, other)


def narrow_kernel(x_ref, mine_ref, theirs_ref, own_ref, other_ref, out_ref):
    product = None
    for side_ref, terms_ref in ((mine_ref, own_ref), (theirs_ref, other_ref)):
        side = side_ref[0]
        rest = terms_ref[...]
        for _ in range(3):
            piece = rest.astype(jnp.bfloat16)
            rest = rest - piece.astype(jnp.float32)
            term = dot(side, piece, ((1,), (1,)))
            product = term if product is None else product + term
    for i in range(2):
        store_scaled(product[:, i * HD : (i + 1) * HD], out_ref, i * HD, HD, x_ref[0])


def narrow_products(x, mine, theirs, own, other):
    _, rows, tokens = mine.shape
    cols = own.shape[0]
    side = pl.BlockSpec((1, rows, tokens), lambda i, x: (0, 0, 0))
    whole = pl.BlockSpec((cols, tokens), lambda i, x: (0, 0))
    shape = (4, rows // 4 + 8, cols)
    return pl.pallas_call(
        narrow_kernel,
        grid_spec=pltpu.PrefetchScalarGridSpec(
            num_scalar_prefetch=1,
            grid=(1,),
            in_specs=[side, side, whole, whole],
            out_specs=pl.BlockSpec(shape, lambda i, x: (0, 0, 0)),
        ),
        out_shape=jax.ShapeDtypeStruct(shape, jnp.float32),
        compiler_params=pltpu.CompilerParams(vmem_limit_bytes=16 * MIB),
        cost_estimate=pl.CostEstimate(flops=1, bytes_accessed=1, transcendentals=0),
        name="narrow",
    )(x.reshape(1), mine, theirs, own, other)


def own_terms_kernel(terms_ref, out_ref):
    for i in range(2):
        rows, powers = pl.ds(i * HD, HD), pl.ds(2 * HD + 8 * i, 1)
        total = unscaled(terms_ref, 0, rows, powers)
        for b in range(1, terms_ref.shape[0]):
            total = total + unscaled(terms_ref, b, rows, powers)
        out_ref[rows, :] = total


def own_terms(terms):
    return pl.pallas_call(
        own_terms_kernel,
        out_shape=jax.ShapeDtypeStruct((2 * HD, terms.shape[2]), jnp.float32),
        compiler_params=pltpu.CompilerParams(vmem_limit_bytes=8 * MIB),
        cost_estimate=pl.CostEstimate(flops=1, bytes_accessed=1, transcendentals=0),
        name="own_terms",
    )(terms)


def after_x_kernel(wide_ref, wide_got_ref, narrow_ref, narrow_got_ref, out_ref, total_ref):
    receivers = out_ref.shape[0]
    rows = total_ref.shape[0]
    first = 0
    for i, (own_ref, got_ref, start, cols) in enumerate(
        (
            (wide_ref, wide_got_ref, 0, 4 * HD),
            (wide_ref, wide_got_ref, 4 * HD, 4 * HD),
            (narrow_ref, narrow_got_ref, 0, HD),
            (narrow_ref, narrow_got_ref, HD, HD),
        )
    ):
        sent = [(own_ref, 0)] + [(got_ref, m) for m in range(3)]
        here = pl.ds(start, cols)
        powers = [ref[m, rows : rows + 1, here] for ref, m in sent]
        top = jnp.maximum(jnp.maximum(powers[0], powers[1]), jnp.maximum(powers[2], powers[3])) + 2.0
        total = sum(ref[m, :rows, here] * jnp.exp2(power - top) for (ref, m), power in zip(sent, powers))
        total_ref[:, pl.ds(first, cols)] = total
        out_ref[:, 60 + i, :] = jnp.broadcast_to(top[:, :HD], (receivers, HD))
        first += cols
    for k in range(receivers):
        for j in range(10):
            out_ref[k, 6 * j : 6 * j + 6, :] = total_ref[6 * k : 6 * k + 6, j * HD : (j + 1) * HD]


def after_x(wide, wide_got, narrow, narrow_got):
    _, padded, wide_cols = wide.shape
    narrow_cols = narrow.shape[2]
    rows = padded - 8
    shape = (rows // 6, 64, HD)
    spec = lambda count, cols: pl.BlockSpec((count, padded, cols), lambda i: (0, 0, 0))
    return pl.pallas_call(
        after_x_kernel,
        grid=(1,),
        in_specs=[spec(1, wide_cols), spec(3, wide_cols), spec(1, narrow_cols), spec(3, narrow_cols)],
        out_specs=pl.BlockSpec(shape, lambda i: (0, 0, 0)),
        out_shape=jax.ShapeDtypeStruct(shape, jnp.float32),
        scratch_shapes=[pltpu.VMEM((rows, wide_cols + narrow_cols), jnp.float32)],
        compiler_params=pltpu.CompilerParams(vmem_limit_bytes=16 * MIB),
        name="after_x",
    )(wide, wide_got, narrow, narrow_got)


def last_sum_kernel(got_ref, query_ref, out_ref, key_ref, value_ref):
    first = 0
    for i, ref in enumerate((query_ref, out_ref, key_ref, value_ref)):
        tiles = ref.shape[1] // HD
        rows = pl.ds(first, 6 * tiles)
        total = unscaled(got_ref, 0, rows, pl.ds(60 + i, 1))
        for b in range(1, got_ref.shape[0]):
            total = total + unscaled(got_ref, b, rows, pl.ds(60 + i, 1))
        for j in range(tiles):
            ref[:, j * HD : (j + 1) * HD] = total[6 * j : 6 * j + 6]
        first += 6 * tiles


def last_sum(got):
    shape = lambda cols: jax.ShapeDtypeStruct((6, cols), jnp.float32)
    return pl.pallas_call(
        last_sum_kernel,
        out_shape=[shape(4 * HD), shape(4 * HD), shape(HD), shape(HD)],
        compiler_params=pltpu.CompilerParams(vmem_limit_bytes=8 * MIB),
        name="last_sum",
    )(got)


def local(normed, w_query, w_key, w_value, w_out, cotangent):
    hidden = normed[0]
    grads_in = cotangent[0]
    tokens, width = hidden.shape
    bf, half = jnp.bfloat16, jnp.float16
    dp = lax.axis_index("dp")
    x, core = dp >> 3, dp & 1
    f32 = jnp.float32

    own = dot(hidden, jnp.concatenate([w_key, w_value], axis=1), ((1,), (0,))).astype(bf)
    gathered = lax.all_to_all(jnp.broadcast_to(own, (8,) + own.shape), "seq", 0, 0, tiled=True)

    queries = dot(hidden, w_query, ((1,), (0,))).astype(bf)
    d_att = dot(grads_in, w_out, ((1,), (0,))).astype(bf)
    pick = (jnp.asarray(ROW_ORDER)[:, None] == jnp.arange(width)[None, :]).astype(bf)
    sides = jnp.stack([dot(pick, side, ((1,), (1,))).astype(bf) for side in (hidden, grads_in)])
    sides = sides.reshape(2, 2, width // 2, tokens)
    mine = lax.dynamic_index_in_dim(sides, core, 1, keepdims=False)
    theirs = from_other_core(lax.dynamic_index_in_dim(sides, 1 - core, 1, keepdims=False))
    queries, d_att, mine, theirs = lax.optimization_barrier((queries, d_att, mine, theirs))

    factors, factors_sent, terms = attention(queries, d_att, gathered.reshape(8 * tokens, 2 * HD))
    terms = lax.all_to_all(terms.astype(half), "seq", 0, 0, tiled=True)
    wide = wide_products(x, mine, theirs, factors, from_other_core(factors_sent))
    sent = [wide[m].astype(half) for m in (1, 2, 3)]
    got = [exchange(block, m << 6) for m, block in zip((1, 2, 3), sent)]
    branch = dot(factors[1], w_out, ((1,), (1,))).astype(bf)

    terms, _ = lax.optimization_barrier((terms, sent))
    d_kv = own_terms(terms.astype(f32))
    narrow = narrow_products(x, mine, theirs, d_kv, from_other_core(d_kv))
    narrow_sent = [narrow[m].astype(half) for m in (1, 2, 3)]
    got, _ = lax.optimization_barrier((got, narrow_sent))
    narrow_got = [exchange(block, m << 6) for m, block in zip((1, 2, 3), narrow_sent)]

    part = after_x(wide, jnp.stack(got).astype(f32), narrow, jnp.stack(narrow_got).astype(f32))
    part = lax.all_to_all(part.astype(half), AXES, 0, 0, axis_index_groups=YZ_GROUPS, tiled=True)
    grad_query, grad_out, grad_key, grad_value = last_sum(part.astype(f32))
    return branch[None], grad_query, grad_key, grad_value, grad_out


def solution(mesh):
    return jax.shard_map(
        local,
        mesh=mesh,
        in_specs=(P("dp", "seq", None), P(), P(), P(), P(), P("dp", "seq", None)),
        out_specs=(
            P("dp", "seq", None),
            P(("dp", "seq"), None),
            P(("dp", "seq"), None),
            P(("dp", "seq"), None),
            P(("dp", "seq"), None),
        ),
        check_vma=False,
    )
```

```python
import jax
import jax.numpy as jnp
import numpy as np
from jax import lax
from jax.experimental import pallas as pl
from jax.experimental.pallas import tpu as pltpu
from jax.sharding import PartitionSpec as P

HEADS = 4
HD = 128
SCALE = HD ** (-0.5)
LOG2_E = 1.4426950408889634
AXES = ("dp", "seq")
MIB = 1024 * 1024


def place(x, y, z, core):
    return x * 64 + (z >> 1) * 16 + core * 8 + (z & 1) * 4 + y


YZ_GROUPS = [[place(x, y, z, c) for y in range(4) for z in range(8)] for x in range(4) for c in range(2)]
ROW_ORDER = np.concatenate(
    [
        np.arange(6) + 6 * place(x, y, z, c)
        for c in range(2)
        for x in range(4)
        for y in range(4)
        for z in range(8)
    ]
)


def dot(left, right, dims):
    return lax.dot_general(left, right, (dims, ((), ())), preferred_element_type=jnp.float32)


def exchange(value, mask):
    return lax.ppermute(value, AXES, [(i, i ^ mask) for i in range(256)])


def from_other_core(value):
    return exchange(value, 8)


def exponent(values):
    top = jnp.max(jnp.max(jnp.abs(values), axis=0, keepdims=True), axis=1, keepdims=True)
    return jnp.ceil(jnp.log2(jnp.maximum(top, 1e-30))) - 13.0


def unscaled(ref, block, values, exponents):
    return ref[block, values, :] * jnp.exp2(ref[block, exponents, :])


def project_kernel(hidden_ref, w_key_ref, w_value_ref, out_ref):
    hidden = hidden_ref[...]
    for i, ref in enumerate((w_key_ref, w_value_ref)):
        block = dot(hidden, ref[...], ((1,), (0,))).astype(jnp.bfloat16)
        for b in range(out_ref.shape[0]):
            out_ref[b, :, i * HD : (i + 1) * HD] = block


def project(hidden, w_key, w_value):
    hidden, w_key, w_value = (pltpu.with_memory_space_constraint(v, pltpu.HBM) for v in (hidden, w_key, w_value))
    return pl.pallas_call(
        project_kernel,
        out_shape=jax.ShapeDtypeStruct((8, hidden.shape[0], 2 * HD), jnp.bfloat16),
        compiler_params=pltpu.CompilerParams(vmem_limit_bytes=16 * MIB),
        name="project",
    )(hidden, w_key, w_value)


def attention_kernel(q_ref, da_ref, k_ref, v_ref, factor_ref, dkv_ref):
    step = pl.program_id(0)
    keys = k_ref[...]
    values = v_ref[...]
    bf = jnp.bfloat16
    heads = range(q_ref.shape[1] // HD)
    q = [q_ref[:, h * HD : (h + 1) * HD] for h in heads]
    da = [da_ref[:, h * HD : (h + 1) * HD] for h in heads]

    def softmax(scores):
        shifted = jnp.exp2((scores - jnp.max(scores, axis=1, keepdims=True)) * (SCALE * LOG2_E))
        return shifted * (1.0 / jnp.sum(shifted, axis=1, keepdims=True))

    def store(side, h, value):
        factor_ref[side, :, h * HD : (h + 1) * HD] = value

    scores = [dot(q[h], keys, ((1,), (1,))) for h in heads]
    probs, probs_b, d_probs, d_scores = [], [], [], []
    for h in heads:
        probs.append(softmax(scores[h]))
        probs_b.append(probs[h].astype(bf))
        d_probs.append(dot(da[h], values, ((1,), (1,))))
    d_value = None
    for h in heads:
        store(1, h, dot(probs_b[h], values, ((1,), (0,))).astype(bf))
        term = dot(da[h], probs_b[h], ((0,), (0,)))
        d_value = term if d_value is None else d_value + term
        delta = jnp.sum(d_probs[h] * probs[h], axis=1, keepdims=True)
        d_scores.append((probs[h] * (d_probs[h] - delta)).astype(bf))
    d_key = None
    for h in heads:
        store(0, h, (dot(d_scores[h], keys, ((1,), (0,))) * SCALE).astype(bf))
        term = dot(q[h], d_scores[h], ((0,), (0,)))
        d_key = term if d_key is None else d_key + term
    blocks, _, tokens = dkv_ref.shape

    @pl.when(step == 0)
    def _():
        for b in range(blocks):
            dkv_ref[b, :HD, :] = d_key[:, b * tokens : (b + 1) * tokens]
            dkv_ref[b, HD : 2 * HD, :] = d_value[:, b * tokens : (b + 1) * tokens]

    @pl.when(step != 0)
    def _():
        for b in range(blocks):
            dkv_ref[b, :HD, :] += d_key[:, b * tokens : (b + 1) * tokens]
            dkv_ref[b, HD : 2 * HD, :] += d_value[:, b * tokens : (b + 1) * tokens]

    @pl.when(step == pl.num_programs(0) - 1)
    def _():
        for i, scale in enumerate((SCALE, 1.0)):
            rows = pl.ds(i * HD, HD)
            top = jnp.abs(dkv_ref[0, rows, :])
            for b in range(1, blocks):
                top = jnp.maximum(top, jnp.abs(dkv_ref[b, rows, :]))
            power = exponent(top * scale)
            factor = jnp.exp2(-power) * scale
            for b in range(blocks):
                dkv_ref[b, rows, :] = dkv_ref[b, rows, :] * factor
                dkv_ref[b, pl.ds(2 * HD + 8 * i, 8), :] = jnp.broadcast_to(power, (8, tokens))


def attention(queries, d_att, keys_values):
    tokens, inner = queries.shape
    length = keys_values.shape[0]
    by_pair = pl.BlockSpec((tokens, 2 * HD), lambda j: (0, j))
    terms = (length // tokens, 2 * HD + 16, tokens)
    return pl.pallas_call(
        attention_kernel,
        grid=(HEADS // 2,),
        in_specs=[
            by_pair,
            by_pair,
            pl.BlockSpec((length, HD), lambda j: (0, 0)),
            pl.BlockSpec((length, HD), lambda j: (0, 1)),
        ],
        out_specs=[
            pl.BlockSpec((2, tokens, 2 * HD), lambda j: (0, 0, j)),
            pl.BlockSpec(terms, lambda j: (0, 0, 0)),
        ],
        out_shape=[
            pltpu.HBM((2, tokens, inner), jnp.bfloat16),
            jax.ShapeDtypeStruct(terms, jnp.float32),
        ],
        compiler_params=pltpu.CompilerParams(vmem_limit_bytes=32 * MIB),
        cost_estimate=pl.CostEstimate(
            flops=12 * tokens * inner * length, bytes_accessed=4 << 20, transcendentals=tokens * HEADS * length
        ),
        name="attention",
    )(queries, d_att, keys_values, keys_values)


def store_scaled(product, out_ref, first, cols, mask):
    power = exponent(product)
    scaled = product * jnp.exp2(-power)
    receivers, padded, _ = out_ref.shape
    rows = padded - 8
    for i in range(receivers):
        out_ref[i ^ mask, :rows, pl.ds(first, cols)] = scaled[i * rows : (i + 1) * rows]
        out_ref[i, rows:, pl.ds(first, cols)] = jnp.broadcast_to(power, (8, cols))


def scaled_rows(values, out_ref, first):
    power = exponent(values)
    rows = values.shape[0]
    out_ref[0, first : first + rows, :] = values * jnp.exp2(-power)
    out_ref[0, first + rows :, :] = jnp.broadcast_to(power, (8, values.shape[1]))


def wide_kernel(x_ref, mine_ref, theirs_ref, own_ref, other_ref, keep_ref, send_ref, product_ref):
    product = dot(mine_ref[0], own_ref[0], ((1,), (0,))) + dot(theirs_ref[0], other_ref[0], ((1,), (0,)))
    product_ref[...] = product
    power = exponent(product)
    factor = jnp.exp2(-power)
    first = 1 + 2 * pl.program_id(0)
    rows = keep_ref.shape[2]
    block = lambda mask: product_ref[pl.ds(pl.multiple_of((x_ref[0] ^ mask) * rows, 8), rows), :]
    keep_ref[0, 0] = block(0)
    keep_ref[0, 1] = block(4 - first)
    send_ref[0, :rows] = block(first) * factor
    send_ref[0, rows : 2 * rows] = block(2) * factor
    send_ref[0, 2 * rows :] = jnp.broadcast_to(power, (8, product.shape[1]))


def wide_products(x, mine, theirs, own, other):
    _, rows, tokens = mine.shape
    inner = own.shape[2]
    side = pl.BlockSpec((1, rows, tokens), lambda i, x: (i, 0, 0))
    factor = pl.BlockSpec((1, tokens, inner), lambda i, x: (i, 0, 0))
    return pl.pallas_call(
        wide_kernel,
        grid_spec=pltpu.PrefetchScalarGridSpec(
            num_scalar_prefetch=1,
            grid=(2,),
            in_specs=[side, side, factor, factor],
            out_specs=[
                pl.BlockSpec((1, 2, rows // 4, inner), lambda i, x: (i, 0, 0, 0)),
                pl.BlockSpec((1, rows // 2 + 8, inner), lambda i, x: (i, 0, 0)),
            ],
            scratch_shapes=[pltpu.VMEM((rows, inner), jnp.float32)],
        ),
        out_shape=[
            pltpu.HBM((2, 2, rows // 4, inner), jnp.float32),
            jax.ShapeDtypeStruct((2, rows // 2 + 8, inner), jnp.float32),
        ],
        compiler_params=pltpu.CompilerParams(vmem_limit_bytes=16 * MIB),
        cost_estimate=pl.CostEstimate(flops=8 * rows * tokens * inner, bytes_accessed=5 << 20, transcendentals=0),
        name="wide",
    )(x.reshape(1), mine, theirs, own, other)


def middle_kernel(keep_ref, got_ref, total_ref, send_ref):
    rows = keep_ref.shape[2]
    powers = pl.ds(2 * rows, 1)
    total_ref[0] = keep_ref[0, 0] + unscaled(got_ref, 0, pl.ds(0, rows), powers)
    scaled_rows(keep_ref[0, 1] + unscaled(got_ref, 0, pl.ds(rows, rows), powers), send_ref, 0)


def middle(keep, got):
    _, _, rows, cols = keep.shape
    shapes = (rows, rows + 8)
    return pl.pallas_call(
        middle_kernel,
        grid=(2,),
        in_specs=[
            pl.BlockSpec((1, 2, rows, cols), lambda i: (i, 0, 0, 0)),
            pl.BlockSpec((1, 2 * rows + 8, cols), lambda i: (i, 0, 0)),
        ],
        out_specs=[pl.BlockSpec((1, r, cols), lambda i: (i, 0, 0)) for r in shapes],
        out_shape=[
            pltpu.HBM((2, rows, cols), jnp.float32),
            jax.ShapeDtypeStruct((2, rows + 8, cols), jnp.float32),
        ],
        compiler_params=pltpu.CompilerParams(vmem_limit_bytes=16 * MIB),
        cost_estimate=pl.CostEstimate(flops=1, bytes_accessed=1, transcendentals=0),
        name="middle",
    )(keep, got)


def narrow_kernel(x_ref, mine_ref, theirs_ref, own_ref, other_ref, out_ref):
    product = None
    for side_ref, terms_ref in ((mine_ref, own_ref), (theirs_ref, other_ref)):
        side = side_ref[0]
        rest = terms_ref[...]
        for _ in range(3):
            piece = rest.astype(jnp.bfloat16)
            rest = rest - piece.astype(jnp.float32)
            term = dot(side, piece, ((1,), (1,)))
            product = term if product is None else product + term
    for i in range(2):
        store_scaled(product[:, i * HD : (i + 1) * HD], out_ref, i * HD, HD, x_ref[0])


def narrow_products(x, mine, theirs, own, other):
    _, rows, tokens = mine.shape
    cols = own.shape[0]
    side = pl.BlockSpec((1, rows, tokens), lambda i, x: (0, 0, 0))
    whole = pl.BlockSpec((cols, tokens), lambda i, x: (0, 0))
    shape = (4, rows // 4 + 8, cols)
    return pl.pallas_call(
        narrow_kernel,
        grid_spec=pltpu.PrefetchScalarGridSpec(
            num_scalar_prefetch=1,
            grid=(1,),
            in_specs=[side, side, whole, whole],
            out_specs=pl.BlockSpec(shape, lambda i, x: (0, 0, 0)),
        ),
        out_shape=jax.ShapeDtypeStruct(shape, jnp.float32),
        compiler_params=pltpu.CompilerParams(vmem_limit_bytes=16 * MIB),
        cost_estimate=pl.CostEstimate(flops=1, bytes_accessed=1, transcendentals=0),
        name="narrow",
    )(x.reshape(1), mine, theirs, own, other)


def own_terms_kernel(terms_ref, out_ref):
    for i in range(2):
        rows, powers = pl.ds(i * HD, HD), pl.ds(2 * HD + 8 * i, 1)
        total = unscaled(terms_ref, 0, rows, powers)
        for b in range(1, terms_ref.shape[0]):
            total = total + unscaled(terms_ref, b, rows, powers)
        out_ref[rows, :] = total


def own_terms(terms):
    return pl.pallas_call(
        own_terms_kernel,
        out_shape=jax.ShapeDtypeStruct((2 * HD, terms.shape[2]), jnp.float32),
        compiler_params=pltpu.CompilerParams(vmem_limit_bytes=8 * MIB),
        cost_estimate=pl.CostEstimate(flops=1, bytes_accessed=1, transcendentals=0),
        name="own_terms",
    )(terms)


def after_x_kernel(wide_ref, wide_got_ref, narrow_ref, narrow_got_ref, out_ref, total_ref):
    receivers = out_ref.shape[0]
    rows, cols = wide_ref.shape[1:]
    for i in range(2):
        power = wide_got_ref[i, rows : rows + 1, :]
        total = wide_ref[i] + wide_got_ref[i, :rows, :] * jnp.exp2(power)
        top = exponent(total)
        total_ref[:, pl.ds(i * cols, cols)] = total * jnp.exp2(-top)
        out_ref[:, 60 + i, :] = jnp.broadcast_to(top, (receivers, HD))
    for i in range(2):
        here = pl.ds(i * HD, HD)
        total = unscaled(narrow_ref, 0, pl.ds(0, rows), pl.ds(rows, 1))[:, i * HD : (i + 1) * HD]
        for m in range(3):
            total = total + narrow_got_ref[m, :rows, here] * jnp.exp2(narrow_got_ref[m, rows : rows + 1, here])
        top = exponent(total)
        total_ref[:, pl.ds(2 * cols + i * HD, HD)] = total * jnp.exp2(-top)
        out_ref[:, 62 + i, :] = jnp.broadcast_to(top, (receivers, HD))
    for k in range(receivers):
        for j in range(10):
            out_ref[k, 6 * j : 6 * j + 6, :] = total_ref[6 * k : 6 * k + 6, j * HD : (j + 1) * HD]


def after_x(wide, wide_got, narrow, narrow_got):
    _, rows, wide_cols = wide.shape
    narrow_cols = narrow.shape[2]
    shape = (rows // 6, 64, HD)
    spec = lambda *sizes: pl.BlockSpec(sizes, lambda i: (0, 0, 0))
    return pl.pallas_call(
        after_x_kernel,
        grid=(1,),
        in_specs=[
            spec(2, rows, wide_cols),
            spec(2, rows + 8, wide_cols),
            spec(1, rows + 8, narrow_cols),
            spec(3, rows + 8, narrow_cols),
        ],
        out_specs=spec(*shape),
        out_shape=jax.ShapeDtypeStruct(shape, jnp.float32),
        scratch_shapes=[pltpu.VMEM((rows, 2 * wide_cols + narrow_cols), jnp.float32)],
        compiler_params=pltpu.CompilerParams(vmem_limit_bytes=16 * MIB),
        name="after_x",
    )(wide, wide_got, narrow, narrow_got)


def last_sum_kernel(got_ref, query_ref, out_ref, key_ref, value_ref):
    first = 0
    for i, ref in enumerate((query_ref, out_ref, key_ref, value_ref)):
        tiles = ref.shape[1] // HD
        rows = pl.ds(first, 6 * tiles)
        total = unscaled(got_ref, 0, rows, pl.ds(60 + i, 1))
        for b in range(1, got_ref.shape[0]):
            total = total + unscaled(got_ref, b, rows, pl.ds(60 + i, 1))
        for j in range(tiles):
            ref[:, j * HD : (j + 1) * HD] = total[6 * j : 6 * j + 6]
        first += 6 * tiles


def last_sum(got):
    shape = lambda cols: jax.ShapeDtypeStruct((6, cols), jnp.float32)
    return pl.pallas_call(
        last_sum_kernel,
        out_shape=[shape(4 * HD), shape(4 * HD), shape(HD), shape(HD)],
        compiler_params=pltpu.CompilerParams(vmem_limit_bytes=8 * MIB),
        name="last_sum",
    )(got)


def local(normed, w_query, w_key, w_value, w_out, cotangent):
    hidden = normed[0]
    grads_in = cotangent[0]
    tokens, width = hidden.shape
    bf, half = jnp.bfloat16, jnp.float16
    dp = lax.axis_index("dp")
    x, core = dp >> 3, dp & 1
    f32 = jnp.float32

    gathered = lax.all_to_all(project(hidden, w_key, w_value), "seq", 0, 0, tiled=True)

    queries = dot(hidden, w_query, ((1,), (0,))).astype(bf)
    d_att = dot(grads_in, w_out, ((1,), (0,))).astype(bf)
    pick = (jnp.asarray(ROW_ORDER)[:, None] == jnp.arange(width)[None, :]).astype(bf)
    sides = jnp.stack([dot(pick, side, ((1,), (1,))).astype(bf) for side in (hidden, grads_in)])
    sides = sides.reshape(2, 2, width // 2, tokens)
    mine = lax.dynamic_index_in_dim(sides, core, 1, keepdims=False)
    theirs = from_other_core(lax.dynamic_index_in_dim(sides, 1 - core, 1, keepdims=False))
    queries, d_att, mine, theirs = lax.optimization_barrier((queries, d_att, mine, theirs))

    queries, d_att = (pltpu.with_memory_space_constraint(v, pltpu.HBM) for v in (queries, d_att))
    factors, terms = attention(queries, d_att, gathered.reshape(8 * tokens, 2 * HD))
    terms = lax.all_to_all(terms.astype(half), "seq", 0, 0, tiled=True)
    keep, send = wide_products(x, mine, theirs, factors, from_other_core(factors))
    send = send.astype(half)
    got = [exchange(send[0], 1 << 6), exchange(send[1], 3 << 6)]
    branch = dot(factors[1], w_out, ((1,), (1,))).astype(bf)

    terms, _ = lax.optimization_barrier((terms, send))
    terms, got = lax.optimization_barrier((terms.astype(f32), got))
    d_kv = own_terms(terms)
    narrow = narrow_products(x, mine, theirs, d_kv, from_other_core(d_kv))
    narrow_sent = [narrow[m].astype(half) for m in (1, 2, 3)]
    narrow_got = [exchange(block, m << 6) for m, block in zip((1, 2, 3), narrow_sent)]
    wide, send = middle(keep, jnp.stack(got).astype(f32))
    send = send.astype(half)
    got = [exchange(send[0], 3 << 6), exchange(send[1], 1 << 6)]

    part = after_x(wide, jnp.stack(got).astype(f32), narrow, jnp.stack(narrow_got).astype(f32))
    part = lax.all_to_all(part.astype(half), AXES, 0, 0, axis_index_groups=YZ_GROUPS, tiled=True)
    grad_query, grad_out, grad_key, grad_value = last_sum(part.astype(f32))
    return branch[None], grad_query, grad_key, grad_value, grad_out


def solution(mesh):
    return jax.shard_map(
        local,
        mesh=mesh,
        in_specs=(P("dp", "seq", None), P(), P(), P(), P(), P("dp", "seq", None)),
        out_specs=(
            P("dp", "seq", None),
            P(("dp", "seq"), None),
            P(("dp", "seq"), None),
            P(("dp", "seq"), None),
            P(("dp", "seq"), None),
        ),
        check_vma=False,
    )
```

```python
import functools

import jax
import jax.numpy as jnp
from jax import lax
from jax.experimental import pallas as pl
from jax.experimental.pallas import tpu as pltpu
from jax.sharding import PartitionSpec as P

HEADS = 4
HD = 128
SCALE = HD ** (-0.5)
LOG2_E = 1.4426950408889634
AXES = ("dp", "seq")
MIB = 1024 * 1024


def place(x, y, z, core):
    return x * 64 + (z >> 1) * 16 + core * 8 + (z & 1) * 4 + y


Z_HI_GROUPS = [
    [place(x, y, 2 * z + low, c) for z in range(4)] for x in range(4) for y in range(4) for low in range(2) for c in range(2)
]


def dot(left, right, dims):
    return lax.dot_general(left, right, (dims, ((), ())), preferred_element_type=jnp.float32)


def exchange(value, mask):
    return lax.ppermute(value, AXES, [(i, i ^ mask) for i in range(256)])


def from_other_core(value):
    return exchange(value, 8)


def exponent(values):
    top = jnp.max(jnp.max(jnp.abs(values), axis=0, keepdims=True), axis=1, keepdims=True)
    return jnp.ceil(jnp.log2(jnp.maximum(top, 1e-30))) - 13.0


def unscaled(ref, block, values, exponents):
    return ref[block, values, :] * jnp.exp2(ref[block, exponents, :])


def project_kernel(hidden_ref, w_key_ref, w_value_ref, out_ref):
    hidden = hidden_ref[...]
    for i, ref in enumerate((w_key_ref, w_value_ref)):
        block = dot(hidden, ref[...], ((1,), (0,))).astype(jnp.bfloat16)
        for b in range(out_ref.shape[0]):
            out_ref[b, :, i * HD : (i + 1) * HD] = block


def project(hidden, w_key, w_value):
    hidden, w_key, w_value = (pltpu.with_memory_space_constraint(v, pltpu.HBM) for v in (hidden, w_key, w_value))
    return pl.pallas_call(
        project_kernel,
        out_shape=jax.ShapeDtypeStruct((8, hidden.shape[0], 2 * HD), jnp.bfloat16),
        compiler_params=pltpu.CompilerParams(vmem_limit_bytes=16 * MIB),
        name="project",
    )(hidden, w_key, w_value)


def turn_kernel(pieces, place_ref, side_ref, *refs):
    turned_ref = refs[-1]
    turned_ref[...] = side_ref[...].T
    for ref, (far, masks) in zip(refs, pieces):
        for i, mask in enumerate(masks):
            for z_hi in range(4):
                start = 384 * (place_ref[0] ^ mask) + 96 * z_hi + 48 * (place_ref[1] ^ far)
                first = 192 * i + 48 * z_hi
                ref[first : first + 48, :] = turned_ref[pl.ds(pl.multiple_of(start, 16), 48), :]


def turn(place, side, pieces):
    tokens, width = side.shape
    shapes = [(len(masks) * width // 8, tokens) for _, masks in pieces]
    return pl.pallas_call(
        functools.partial(turn_kernel, pieces),
        grid_spec=pltpu.PrefetchScalarGridSpec(
            num_scalar_prefetch=1,
            grid=(1,),
            in_specs=[pl.BlockSpec((tokens, width), lambda i, place: (0, 0))],
            out_specs=[pl.BlockSpec(shape, lambda i, place: (0, 0)) for shape in shapes],
            scratch_shapes=[pltpu.VMEM((width, tokens), side.dtype)],
        ),
        out_shape=[jax.ShapeDtypeStruct(shape, side.dtype) for shape in shapes],
        compiler_params=pltpu.CompilerParams(vmem_limit_bytes=12 * MIB),
        name="turn",
    )(place, side)


def attention_kernel(q_ref, da_ref, k_ref, v_ref, d_query_ref, attended_ref, dkv_ref):
    step = pl.program_id(0)
    keys = k_ref[...]
    values = v_ref[...]
    bf = jnp.bfloat16
    heads = range(q_ref.shape[1] // HD)
    q = [q_ref[:, h * HD : (h + 1) * HD] for h in heads]
    da = [da_ref[:, h * HD : (h + 1) * HD] for h in heads]

    def softmax(scores):
        shifted = jnp.exp2((scores - jnp.max(scores, axis=1, keepdims=True)) * (SCALE * LOG2_E))
        return shifted * (1.0 / jnp.sum(shifted, axis=1, keepdims=True))

    scores = [dot(q[h], keys, ((1,), (1,))) for h in heads]
    probs, probs_b, d_probs, d_scores = [], [], [], []
    for h in heads:
        probs.append(softmax(scores[h]))
        probs_b.append(probs[h].astype(bf))
        d_probs.append(dot(da[h], values, ((1,), (1,))))
    d_value = None
    for h in heads:
        attended_ref[:, h * HD : (h + 1) * HD] = dot(probs_b[h], values, ((1,), (0,))).astype(bf)
        term = dot(da[h], probs_b[h], ((0,), (0,)))
        d_value = term if d_value is None else d_value + term
        delta = jnp.sum(d_probs[h] * probs[h], axis=1, keepdims=True)
        d_scores.append((probs[h] * (d_probs[h] - delta)).astype(bf))
    d_key = None
    for h in heads:
        d_query_ref[:, h * HD : (h + 1) * HD] = (dot(d_scores[h], keys, ((1,), (0,))) * SCALE).astype(bf)
        term = dot(q[h], d_scores[h], ((0,), (0,)))
        d_key = term if d_key is None else d_key + term
    blocks, _, tokens = dkv_ref.shape

    @pl.when(step == 0)
    def _():
        for b in range(blocks):
            dkv_ref[b, :HD, :] = d_key[:, b * tokens : (b + 1) * tokens]
            dkv_ref[b, HD : 2 * HD, :] = d_value[:, b * tokens : (b + 1) * tokens]

    @pl.when(step != 0)
    def _():
        for b in range(blocks):
            dkv_ref[b, :HD, :] += d_key[:, b * tokens : (b + 1) * tokens]
            dkv_ref[b, HD : 2 * HD, :] += d_value[:, b * tokens : (b + 1) * tokens]

    @pl.when(step == pl.num_programs(0) - 1)
    def _():
        for i, scale in enumerate((SCALE, 1.0)):
            rows = pl.ds(i * HD, HD)
            top = jnp.abs(dkv_ref[0, rows, :])
            for b in range(1, blocks):
                top = jnp.maximum(top, jnp.abs(dkv_ref[b, rows, :]))
            power = exponent(top * scale)
            factor = jnp.exp2(-power) * scale
            for b in range(blocks):
                dkv_ref[b, rows, :] = dkv_ref[b, rows, :] * factor
                dkv_ref[b, pl.ds(2 * HD + 8 * i, 8), :] = jnp.broadcast_to(power, (8, tokens))


def attention(queries, d_att, keys_values):
    tokens, inner = queries.shape
    length = keys_values.shape[0]
    by_pair = pl.BlockSpec((tokens, 2 * HD), lambda j: (0, j))
    terms = (length // tokens, 2 * HD + 16, tokens)
    return pl.pallas_call(
        attention_kernel,
        grid=(HEADS // 2,),
        in_specs=[
            by_pair,
            by_pair,
            pl.BlockSpec((length, HD), lambda j: (0, 0)),
            pl.BlockSpec((length, HD), lambda j: (0, 1)),
        ],
        out_specs=[
            by_pair,
            by_pair,
            pl.BlockSpec(terms, lambda j: (0, 0, 0)),
        ],
        out_shape=[
            pltpu.HBM((tokens, inner), jnp.bfloat16),
            pltpu.HBM((tokens, inner), jnp.bfloat16),
            jax.ShapeDtypeStruct(terms, jnp.float32),
        ],
        compiler_params=pltpu.CompilerParams(vmem_limit_bytes=32 * MIB),
        cost_estimate=pl.CostEstimate(
            flops=12 * tokens * inner * length, bytes_accessed=4 << 20, transcendentals=tokens * HEADS * length
        ),
        name="attention",
    )(queries, d_att, keys_values, keys_values)


def store_scaled(values, ref):
    power = exponent(values)
    ref[:-8, :] = values * jnp.exp2(-power)
    ref[-8:, :] = jnp.broadcast_to(power, (8, values.shape[1]))


def wide_kernel(*refs):
    keep_ref, *send_refs = refs[16:]
    rows, cols = keep_ref.shape[0], send_refs[0].shape[1]
    for i in range(2):
        product = None
        for side_ref, factor_ref in zip(refs[8 * i : 8 * i + 4], refs[8 * i + 4 : 8 * i + 8]):
            term = dot(side_ref[: 2 * rows], factor_ref[...], ((1,), (0,)))
            product = term if product is None else product + term
        keep_ref[:, i * cols : (i + 1) * cols] = product[:rows]
        store_scaled(product[rows:], send_refs[i])


def wide_products(query, out):
    rows = out[0].shape[0] // 2
    cols = out[4].shape[1]
    query, out = (v[:4] + [pltpu.with_memory_space_constraint(f, pltpu.HBM) for f in v[4:]] for v in (query, out))
    return pl.pallas_call(
        wide_kernel,
        out_shape=[
            pltpu.HBM((rows, 2 * cols), jnp.float32),
            jax.ShapeDtypeStruct((rows + 8, cols), jnp.float32),
            jax.ShapeDtypeStruct((rows + 8, cols), jnp.float32),
        ],
        compiler_params=pltpu.CompilerParams(vmem_limit_bytes=20 * MIB),
        cost_estimate=pl.CostEstimate(flops=1 << 30, bytes_accessed=5 << 20, transcendentals=0),
        name="wide",
    )(*query, *out)


def narrow_kernel(mine_ref, theirs_ref, own_ref, other_ref, keep_ref, three_ref, one_ref, two_ref):
    product = None
    for side_ref, terms_ref in ((mine_ref, own_ref), (theirs_ref, other_ref)):
        side = side_ref[...]
        rest = terms_ref[...]
        for _ in range(2):
            piece = rest.astype(jnp.bfloat16)
            rest = rest - piece.astype(jnp.float32)
            term = dot(side, piece, ((1,), (1,)))
            product = term if product is None else product + term
    rows = keep_ref.shape[0]
    keep_ref[...] = product[:rows]
    powers = [jnp.broadcast_to(exponent(product[:, i * HD : (i + 1) * HD]), (8, HD)) for i in range(2)]
    power = jnp.concatenate(powers, axis=1)
    factor = jnp.exp2(-power[:1])
    for i, ref in enumerate((three_ref, one_ref, two_ref)):
        ref[:rows, :] = product[(i + 1) * rows : (i + 2) * rows] * factor
        ref[rows:, :] = power


def narrow_products(mine, theirs, own, other):
    rows = mine.shape[0] // 4
    cols = own.shape[0]
    sent = jax.ShapeDtypeStruct((rows + 8, cols), jnp.float32)
    return pl.pallas_call(
        narrow_kernel,
        out_shape=[pltpu.HBM((rows, cols), jnp.float32), sent, sent, sent],
        compiler_params=pltpu.CompilerParams(vmem_limit_bytes=16 * MIB),
        cost_estimate=pl.CostEstimate(flops=1, bytes_accessed=1, transcendentals=0),
        name="narrow",
    )(mine, theirs, own, other)


def own_terms_kernel(terms_ref, out_ref):
    for i in range(2):
        rows, powers = pl.ds(i * HD, HD), pl.ds(2 * HD + 8 * i, 1)
        total = unscaled(terms_ref, 0, rows, powers)
        for b in range(1, terms_ref.shape[0]):
            total = total + unscaled(terms_ref, b, rows, powers)
        out_ref[rows, :] = total


def own_terms(terms):
    return pl.pallas_call(
        own_terms_kernel,
        out_shape=jax.ShapeDtypeStruct((2 * HD, terms.shape[2]), jnp.float32),
        compiler_params=pltpu.CompilerParams(vmem_limit_bytes=8 * MIB),
        cost_estimate=pl.CostEstimate(flops=1, bytes_accessed=1, transcendentals=0),
        name="own_terms",
    )(terms)


def after_x_kernel(wide_ref, wide_got_ref, narrow_ref, narrow_got_ref, out_ref, total_ref):
    rows = wide_ref.shape[0]
    cols = 4 * HD
    scaled = lambda ref, i, here: ref[i, :rows, here] * jnp.exp2(ref[i, rows : rows + 1, here])
    for i, (first, width) in enumerate(((0, cols), (cols, cols), (2 * cols, HD), (2 * cols + HD, HD))):
        if i < 2:
            total = wide_ref[:, first : first + width] + scaled(wide_got_ref, i, pl.ds(0, cols))
        else:
            here = pl.ds(first - 2 * cols, HD)
            total = narrow_ref[:, here]
            for m in range(3):
                total = total + scaled(narrow_got_ref, m, here)
        top = exponent(total)
        total_ref[:, first : first + width] = total * jnp.exp2(-top)
        out_ref[:, 240 + i, :] = jnp.broadcast_to(top, (out_ref.shape[0], HD))
    out_ref[:, 244:, :] = jnp.zeros((out_ref.shape[0], 4, HD), jnp.float32)
    for k in range(out_ref.shape[0]):
        for j in range(10):
            for z_hi in range(4):
                to, start = 24 * j + 6 * z_hi, 48 * z_hi + 6 * k
                out_ref[k, to : to + 6, :] = total_ref[start : start + 6, j * HD : (j + 1) * HD]


def after_x(wide, wide_got, narrow, narrow_got):
    rows, cols = wide.shape
    shape = (rows // 24, 248, HD)
    return pl.pallas_call(
        after_x_kernel,
        out_shape=jax.ShapeDtypeStruct(shape, jnp.float32),
        scratch_shapes=[pltpu.VMEM((rows, cols + narrow.shape[1]), jnp.float32)],
        compiler_params=pltpu.CompilerParams(vmem_limit_bytes=16 * MIB),
        name="after_x",
    )(wide, wide_got, narrow, narrow_got)


def after_seq_kernel(got_ref, out_ref, total_ref):
    for i, (first, count) in enumerate(((0, 96), (96, 96), (192, 24), (216, 24))):
        rows = pl.ds(first, count)
        total = unscaled(got_ref, 0, rows, pl.ds(240 + i, 1))
        for b in range(1, got_ref.shape[0]):
            total = total + unscaled(got_ref, b, rows, pl.ds(240 + i, 1))
        total_ref[rows, :] = total
    for k in range(4):
        for j in range(10):
            out_ref[k, 6 * j : 6 * j + 6, :] = total_ref[24 * j + 6 * k : 24 * j + 6 * k + 6, :]
        out_ref[k, 60:, :] = jnp.zeros((4, HD), jnp.float32)


def after_seq(got):
    return pl.pallas_call(
        after_seq_kernel,
        out_shape=jax.ShapeDtypeStruct((4, 64, HD), jnp.float32),
        scratch_shapes=[pltpu.VMEM((240, HD), jnp.float32)],
        compiler_params=pltpu.CompilerParams(vmem_limit_bytes=8 * MIB),
        name="after_seq",
    )(got)


def last_sum_kernel(got_ref, query_ref, out_ref, key_ref, value_ref):
    total = (got_ref[0] + got_ref[1]) + (got_ref[2] + got_ref[3])
    first = 0
    for ref in (query_ref, out_ref, key_ref, value_ref):
        for j in range(ref.shape[1] // HD):
            ref[:, j * HD : (j + 1) * HD] = total[first : first + 6]
            first += 6


def last_sum(got):
    shape = lambda cols: jax.ShapeDtypeStruct((6, cols), jnp.float32)
    return pl.pallas_call(
        last_sum_kernel,
        out_shape=[shape(4 * HD), shape(4 * HD), shape(HD), shape(HD)],
        compiler_params=pltpu.CompilerParams(vmem_limit_bytes=8 * MIB),
        name="last_sum",
    )(got)


def local(normed, w_query, w_key, w_value, w_out, cotangent):
    hidden = normed[0]
    grads_in = cotangent[0]
    tokens = hidden.shape[0]
    bf, half = jnp.bfloat16, jnp.float16
    dp = lax.axis_index("dp")
    x, core = dp >> 3, dp & 1
    f32 = jnp.float32

    gathered = lax.all_to_all(project(hidden, w_key, w_value), "seq", 0, 0, tiled=True)

    queries = dot(hidden, w_query, ((1,), (0,))).astype(bf)
    d_att = dot(grads_in, w_out, ((1,), (0,))).astype(bf)
    place_now = jnp.stack([x, core])
    h, h_core, *h_far = turn(place_now, hidden, ((0, (0, 3, 1, 2)), (1, (0, 3, 1, 2)), (0, (1, 2)), (1, (1, 2))))
    g, g_core, *g_far = turn(place_now, grads_in, ((0, (0, 1)), (1, (0, 1)), (0, (3, 2)), (1, (3, 2))))
    h_from = [exchange(h_far[0], 1 << 6), exchange(h_far[1], (1 << 6) | 8)]
    g_from = [exchange(g_far[0], 3 << 6), exchange(g_far[1], (3 << 6) | 8)]
    h_core, g_core = from_other_core(h_core), from_other_core(g_core)

    queries, d_att = (pltpu.with_memory_space_constraint(v, pltpu.HBM) for v in (queries, d_att))
    d_query, attended, terms = attention(queries, d_att, gathered.reshape(8 * tokens, 2 * HD))
    terms, d_query, attended, h_from, g_from, h_core, g_core = lax.optimization_barrier(
        (terms, d_query, attended, h_from, g_from, h_core, g_core)
    )
    terms = lax.all_to_all(terms.astype(half), "seq", 0, 0, tiled=True)

    def factors(own, first):
        beside = exchange(own, first << 6)
        return [own, from_other_core(own), beside, from_other_core(beside)]

    keep, *sent = wide_products(
        [h, h_core, *h_from] + factors(d_query, 1),
        [g, g_core, *g_from] + factors(attended, 3),
    )
    sent = [block.astype(half) for block in sent]
    wide_got = [exchange(block, m << 6) for m, block in zip((3, 1), sent)]
    branch = dot(attended, w_out, ((1,), (1,))).astype(bf)

    terms, _, branch = lax.optimization_barrier((terms, sent, branch))
    d_kv = own_terms(terms.astype(f32))
    narrow, *sent = narrow_products(h, h_core, d_kv, from_other_core(d_kv))
    narrow_got = [exchange(block.astype(half), m << 6) for m, block in zip((3, 1, 2), sent)]

    part = after_x(keep, jnp.stack(wide_got).astype(f32), narrow, jnp.stack(narrow_got).astype(f32))
    part = after_seq(lax.all_to_all(part.astype(half), "seq", 0, 0, tiled=True).astype(f32))
    part = lax.all_to_all(part, AXES, 0, 0, axis_index_groups=Z_HI_GROUPS, tiled=True)
    grad_query, grad_out, grad_key, grad_value = last_sum(part)
    return branch[None], grad_query, grad_key, grad_value, grad_out


def solution(mesh):
    return jax.shard_map(
        local,
        mesh=mesh,
        in_specs=(P("dp", "seq", None), P(), P(), P(), P(), P("dp", "seq", None)),
        out_specs=(
            P("dp", "seq", None),
            P(("dp", "seq"), None),
            P(("dp", "seq"), None),
            P(("dp", "seq"), None),
            P(("dp", "seq"), None),
        ),
        check_vma=False,
    )
```

```python
import functools

import jax
import jax.numpy as jnp
from jax import lax
from jax.experimental import pallas as pl
from jax.experimental.pallas import tpu as pltpu
from jax.sharding import PartitionSpec as P

HEADS = 4
HD = 128
SCALE = HD ** (-0.5)
LOG2_E = 1.4426950408889634
AXES = ("dp", "seq")
MIB = 1024 * 1024


def place(x, y, z, core):
    return x * 64 + (z >> 1) * 16 + core * 8 + (z & 1) * 4 + y


Z_HI_GROUPS = [
    [place(x, y, 2 * z + low, c) for z in range(4)] for x in range(4) for y in range(4) for low in range(2) for c in range(2)
]


def dot(left, right, dims):
    return lax.dot_general(left, right, (dims, ((), ())), preferred_element_type=jnp.float32)


def exchange(value, mask):
    return lax.ppermute(value, AXES, [(i, i ^ mask) for i in range(256)])


def from_other_core(value):
    return exchange(value, 8)


def exponent(values):
    top = jnp.max(jnp.max(jnp.abs(values), axis=0, keepdims=True), axis=1, keepdims=True)
    return jnp.ceil(jnp.log2(jnp.maximum(top, 1e-30))) - 13.0


def unscaled(ref, block, values, exponents):
    return ref[block, values, :] * jnp.exp2(ref[block, exponents, :])


def project_kernel(hidden_ref, w_key_ref, w_value_ref, out_ref):
    hidden = hidden_ref[...]
    for i, ref in enumerate((w_key_ref, w_value_ref)):
        block = dot(hidden, ref[...], ((1,), (0,))).astype(jnp.bfloat16)
        for b in range(out_ref.shape[0]):
            out_ref[b, :, i * HD : (i + 1) * HD] = block


def project(hidden, w_key, w_value):
    hidden, w_key, w_value = (pltpu.with_memory_space_constraint(v, pltpu.HBM) for v in (hidden, w_key, w_value))
    return pl.pallas_call(
        project_kernel,
        out_shape=jax.ShapeDtypeStruct((8, hidden.shape[0], 2 * HD), jnp.bfloat16),
        compiler_params=pltpu.CompilerParams(vmem_limit_bytes=16 * MIB),
        name="project",
    )(hidden, w_key, w_value)


def turn_kernel(pieces, place_ref, side_ref, *refs):
    turned_ref = refs[-1]
    turned_ref[...] = side_ref[...].T
    for ref, (far, masks) in zip(refs, pieces):
        for i, mask in enumerate(masks):
            for z_hi in range(4):
                start = 384 * (place_ref[0] ^ mask) + 96 * z_hi + 48 * (place_ref[1] ^ far)
                first = 192 * i + 48 * z_hi
                ref[first : first + 48, :] = turned_ref[pl.ds(pl.multiple_of(start, 16), 48), :]


def turn(place, side, pieces):
    tokens, width = side.shape
    shapes = [(len(masks) * width // 8, tokens) for _, masks in pieces]
    return pl.pallas_call(
        functools.partial(turn_kernel, pieces),
        grid_spec=pltpu.PrefetchScalarGridSpec(
            num_scalar_prefetch=1,
            grid=(1,),
            in_specs=[pl.BlockSpec((tokens, width), lambda i, place: (0, 0))],
            out_specs=[pl.BlockSpec(shape, lambda i, place: (0, 0)) for shape in shapes],
            scratch_shapes=[pltpu.VMEM((width, tokens), side.dtype)],
        ),
        out_shape=[jax.ShapeDtypeStruct(shape, side.dtype) for shape in shapes],
        compiler_params=pltpu.CompilerParams(vmem_limit_bytes=12 * MIB),
        name="turn",
    )(place, side)


def attention_kernel(
    q_ref, da_ref, k_ref, v_ref, d_query_ref, attended_ref, dkv_ref, scores_ref, d_probs_ref, probs_ref, d_scores_ref
):
    bf = jnp.bfloat16
    blocks, _, tokens = dkv_ref.shape
    chunk = 16
    head_cols = lambda h: slice(h * HD, (h + 1) * HD)
    block_rows = lambda b: slice(b * tokens, (b + 1) * tokens)

    def ahead(h):
        def make(b, side_ref, other_ref, to_ref):
            def run():
                to_ref[h % 2, :, block_rows(b)] = dot(side_ref[:, head_cols(h)], other_ref[block_rows(b), :], ((1,), (1,)))

            return run

        return [
            make(b, *refs)
            for b in range(blocks)
            for refs in ((q_ref, k_ref, scores_ref), (da_ref, v_ref, d_probs_ref))
        ]

    def softmax(h, i):
        rows = slice(i * chunk, (i + 1) * chunk)
        scores = scores_ref[h % 2, rows, :]
        shifted = jnp.exp2((scores - jnp.max(scores, axis=1, keepdims=True)) * (SCALE * LOG2_E))
        probs = shifted * (1.0 / jnp.sum(shifted, axis=1, keepdims=True))
        d_probs = d_probs_ref[h % 2, rows, :]
        delta = jnp.sum(d_probs * probs, axis=1, keepdims=True)
        probs_ref[h % 2, rows, :] = probs.astype(bf)
        d_scores_ref[h % 2, rows, :] = (probs * (d_probs - delta)).astype(bf)

    def behind(h):
        sides = [ref[:, head_cols(h)].T for ref in (q_ref, da_ref)]

        def terms(b, i, from_ref):
            def run():
                term = dot(sides[i], from_ref[h % 2, :, block_rows(b)], ((1,), (0,)))
                rows = slice(i * HD, (i + 1) * HD)
                dkv_ref[b, rows, :] = term if h == 0 else dkv_ref[b, rows, :] + term

            return run

        def rows_of(from_ref, other_ref, to_ref, scale):
            def run():
                product = dot(from_ref[h % 2], other_ref[...], ((1,), (0,)))
                to_ref[:, head_cols(h)] = (product * scale if scale else product).astype(bf)

            return run

        work = [terms(b, i, ref) for b in range(blocks) for i, ref in enumerate((d_scores_ref, probs_ref))]
        work.insert(4, rows_of(probs_ref, v_ref, attended_ref, None))
        work.insert(13, rows_of(d_scores_ref, k_ref, d_query_ref, SCALE))
        return work

    for run in ahead(0):
        run()
    for h in range(HEADS):
        beside = []
        if h + 1 < HEADS:
            beside += [(n / 16, run) for n, run in enumerate(ahead(h + 1))]
        if h > 0:
            beside += [(n / 18, run) for n, run in enumerate(behind(h - 1))]
        beside.sort(key=lambda entry: entry[0])
        steps = tokens // chunk
        for i in range(steps):
            softmax(h, i)
            for at, run in beside:
                if i <= at * steps < i + 1:
                    run()
    for run in behind(HEADS - 1):
        run()

    for i, scale in enumerate((SCALE, 1.0)):
        rows = pl.ds(i * HD, HD)
        top = jnp.abs(dkv_ref[0, rows, :])
        for b in range(1, blocks):
            top = jnp.maximum(top, jnp.abs(dkv_ref[b, rows, :]))
        power = exponent(top * scale)
        factor = jnp.exp2(-power) * scale
        for b in range(blocks):
            dkv_ref[b, rows, :] = dkv_ref[b, rows, :] * factor
            dkv_ref[b, pl.ds(2 * HD + 8 * i, 8), :] = jnp.broadcast_to(power, (8, tokens))


def attention(queries, d_att, keys_values):
    tokens, inner = queries.shape
    length = keys_values.shape[0]
    whole = pl.BlockSpec((tokens, inner), lambda i: (0, 0))
    terms = (length // tokens, 2 * HD + 16, tokens)
    return pl.pallas_call(
        attention_kernel,
        grid=(1,),
        in_specs=[
            whole,
            whole,
            pl.BlockSpec((length, HD), lambda i: (0, 0)),
            pl.BlockSpec((length, HD), lambda i: (0, 1)),
        ],
        out_specs=[whole, whole, pl.BlockSpec(terms, lambda i: (0, 0, 0))],
        out_shape=[
            pltpu.HBM((tokens, inner), jnp.bfloat16),
            pltpu.HBM((tokens, inner), jnp.bfloat16),
            jax.ShapeDtypeStruct(terms, jnp.float32),
        ],
        scratch_shapes=[pltpu.VMEM((2, tokens, length), jnp.float32)] * 2 + [pltpu.VMEM((2, tokens, length), jnp.bfloat16)] * 2,
        compiler_params=pltpu.CompilerParams(vmem_limit_bytes=32 * MIB),
        cost_estimate=pl.CostEstimate(
            flops=12 * tokens * inner * length, bytes_accessed=4 << 20, transcendentals=tokens * HEADS * length
        ),
        name="attention",
    )(queries, d_att, keys_values, keys_values)


def store_scaled(values, ref):
    power = exponent(values)
    ref[:-8, :] = values * jnp.exp2(-power)
    ref[-8:, :] = jnp.broadcast_to(power, (8, values.shape[1]))


def wide_kernel(*refs):
    keep_ref, *send_refs = refs[16:]
    rows, cols = keep_ref.shape[0], send_refs[0].shape[1]
    for i in range(2):
        product = None
        for side_ref, factor_ref in zip(refs[8 * i : 8 * i + 4], refs[8 * i + 4 : 8 * i + 8]):
            term = dot(side_ref[: 2 * rows], factor_ref[...], ((1,), (0,)))
            product = term if product is None else product + term
        keep_ref[:, i * cols : (i + 1) * cols] = product[:rows]
        store_scaled(product[rows:], send_refs[i])


def wide_products(query, out):
    rows = out[0].shape[0] // 2
    cols = out[4].shape[1]
    query, out = (v[:4] + [pltpu.with_memory_space_constraint(f, pltpu.HBM) for f in v[4:]] for v in (query, out))
    return pl.pallas_call(
        wide_kernel,
        out_shape=[
            pltpu.HBM((rows, 2 * cols), jnp.float32),
            jax.ShapeDtypeStruct((rows + 8, cols), jnp.float32),
            jax.ShapeDtypeStruct((rows + 8, cols), jnp.float32),
        ],
        compiler_params=pltpu.CompilerParams(vmem_limit_bytes=20 * MIB),
        cost_estimate=pl.CostEstimate(flops=1 << 30, bytes_accessed=5 << 20, transcendentals=0),
        name="wide",
    )(*query, *out)


def narrow_kernel(mine_ref, theirs_ref, own_ref, other_ref, keep_ref, three_ref, one_ref, two_ref):
    product = None
    for side_ref, terms_ref in ((mine_ref, own_ref), (theirs_ref, other_ref)):
        side = side_ref[...]
        rest = terms_ref[...]
        for _ in range(2):
            piece = rest.astype(jnp.bfloat16)
            rest = rest - piece.astype(jnp.float32)
            term = dot(side, piece, ((1,), (1,)))
            product = term if product is None else product + term
    rows = keep_ref.shape[0]
    keep_ref[...] = product[:rows]
    powers = [jnp.broadcast_to(exponent(product[:, i * HD : (i + 1) * HD]), (8, HD)) for i in range(2)]
    power = jnp.concatenate(powers, axis=1)
    factor = jnp.exp2(-power[:1])
    for i, ref in enumerate((three_ref, one_ref, two_ref)):
        ref[:rows, :] = product[(i + 1) * rows : (i + 2) * rows] * factor
        ref[rows:, :] = power


def narrow_products(mine, theirs, own, other):
    rows = mine.shape[0] // 4
    cols = own.shape[0]
    sent = jax.ShapeDtypeStruct((rows + 8, cols), jnp.float32)
    return pl.pallas_call(
        narrow_kernel,
        out_shape=[pltpu.HBM((rows, cols), jnp.float32), sent, sent, sent],
        compiler_params=pltpu.CompilerParams(vmem_limit_bytes=16 * MIB),
        cost_estimate=pl.CostEstimate(flops=1, bytes_accessed=1, transcendentals=0),
        name="narrow",
    )(mine, theirs, own, other)


def own_terms_kernel(terms_ref, out_ref):
    for i in range(2):
        rows, powers = pl.ds(i * HD, HD), pl.ds(2 * HD + 8 * i, 1)
        total = unscaled(terms_ref, 0, rows, powers)
        for b in range(1, terms_ref.shape[0]):
            total = total + unscaled(terms_ref, b, rows, powers)
        out_ref[rows, :] = total


def own_terms(terms):
    return pl.pallas_call(
        own_terms_kernel,
        out_shape=jax.ShapeDtypeStruct((2 * HD, terms.shape[2]), jnp.float32),
        compiler_params=pltpu.CompilerParams(vmem_limit_bytes=8 * MIB),
        cost_estimate=pl.CostEstimate(flops=1, bytes_accessed=1, transcendentals=0),
        name="own_terms",
    )(terms)


def after_x_kernel(wide_ref, wide_got_ref, narrow_ref, narrow_got_ref, out_ref, total_ref):
    rows = wide_ref.shape[0]
    cols = 4 * HD
    scaled = lambda ref, i, here: ref[i, :rows, here] * jnp.exp2(ref[i, rows : rows + 1, here])
    for i, (first, width) in enumerate(((0, cols), (cols, cols), (2 * cols, HD), (2 * cols + HD, HD))):
        if i < 2:
            total = wide_ref[:, first : first + width] + scaled(wide_got_ref, i, pl.ds(0, cols))
        else:
            here = pl.ds(first - 2 * cols, HD)
            total = narrow_ref[:, here]
            for m in range(3):
                total = total + scaled(narrow_got_ref, m, here)
        top = exponent(total)
        total_ref[:, first : first + width] = total * jnp.exp2(-top)
        out_ref[:, 240 + i, :] = jnp.broadcast_to(top, (out_ref.shape[0], HD))
    out_ref[:, 244:, :] = jnp.zeros((out_ref.shape[0], 4, HD), jnp.float32)
    for k in range(out_ref.shape[0]):
        for j in range(10):
            for z_hi in range(4):
                to, start = 24 * j + 6 * z_hi, 48 * z_hi + 6 * k
                out_ref[k, to : to + 6, :] = total_ref[start : start + 6, j * HD : (j + 1) * HD]


def after_x(wide, wide_got, narrow, narrow_got):
    rows, cols = wide.shape
    shape = (rows // 24, 248, HD)
    return pl.pallas_call(
        after_x_kernel,
        out_shape=jax.ShapeDtypeStruct(shape, jnp.float32),
        scratch_shapes=[pltpu.VMEM((rows, cols + narrow.shape[1]), jnp.float32)],
        compiler_params=pltpu.CompilerParams(vmem_limit_bytes=16 * MIB),
        name="after_x",
    )(wide, wide_got, narrow, narrow_got)


def after_seq_kernel(got_ref, out_ref, total_ref):
    for i, (first, count) in enumerate(((0, 96), (96, 96), (192, 24), (216, 24))):
        rows = pl.ds(first, count)
        total = unscaled(got_ref, 0, rows, pl.ds(240 + i, 1))
        for b in range(1, got_ref.shape[0]):
            total = total + unscaled(got_ref, b, rows, pl.ds(240 + i, 1))
        total_ref[rows, :] = total
    for k in range(4):
        for j in range(10):
            out_ref[k, 6 * j : 6 * j + 6, :] = total_ref[24 * j + 6 * k : 24 * j + 6 * k + 6, :]
        out_ref[k, 60:, :] = jnp.zeros((4, HD), jnp.float32)


def after_seq(got):
    return pl.pallas_call(
        after_seq_kernel,
        out_shape=jax.ShapeDtypeStruct((4, 64, HD), jnp.float32),
        scratch_shapes=[pltpu.VMEM((240, HD), jnp.float32)],
        compiler_params=pltpu.CompilerParams(vmem_limit_bytes=8 * MIB),
        name="after_seq",
    )(got)


def last_sum_kernel(got_ref, query_ref, out_ref, key_ref, value_ref):
    total = (got_ref[0] + got_ref[1]) + (got_ref[2] + got_ref[3])
    first = 0
    for ref in (query_ref, out_ref, key_ref, value_ref):
        for j in range(ref.shape[1] // HD):
            ref[:, j * HD : (j + 1) * HD] = total[first : first + 6]
            first += 6


def last_sum(got):
    shape = lambda cols: jax.ShapeDtypeStruct((6, cols), jnp.float32)
    return pl.pallas_call(
        last_sum_kernel,
        out_shape=[shape(4 * HD), shape(4 * HD), shape(HD), shape(HD)],
        compiler_params=pltpu.CompilerParams(vmem_limit_bytes=8 * MIB),
        name="last_sum",
    )(got)


def local(normed, w_query, w_key, w_value, w_out, cotangent):
    hidden = normed[0]
    grads_in = cotangent[0]
    tokens = hidden.shape[0]
    bf, half = jnp.bfloat16, jnp.float16
    dp = lax.axis_index("dp")
    x, core = dp >> 3, dp & 1
    f32 = jnp.float32

    gathered = lax.all_to_all(project(hidden, w_key, w_value), "seq", 0, 0, tiled=True)

    queries = dot(hidden, w_query, ((1,), (0,))).astype(bf)
    d_att = dot(grads_in, w_out, ((1,), (0,))).astype(bf)
    place_now = jnp.stack([x, core])
    h, h_core, *h_far = turn(place_now, hidden, ((0, (0, 3, 1, 2)), (1, (0, 3, 1, 2)), (0, (1, 2)), (1, (1, 2))))
    g, g_core, *g_far = turn(place_now, grads_in, ((0, (0, 1)), (1, (0, 1)), (0, (3, 2)), (1, (3, 2))))
    h_from = [exchange(h_far[0], 1 << 6), exchange(h_far[1], (1 << 6) | 8)]
    g_from = [exchange(g_far[0], 3 << 6), exchange(g_far[1], (3 << 6) | 8)]
    h_core, g_core = from_other_core(h_core), from_other_core(g_core)

    queries, d_att = (pltpu.with_memory_space_constraint(v, pltpu.HBM) for v in (queries, d_att))
    d_query, attended, terms = attention(queries, d_att, gathered.reshape(8 * tokens, 2 * HD))
    terms, d_query, attended, h_from, g_from, h_core, g_core = lax.optimization_barrier(
        (terms, d_query, attended, h_from, g_from, h_core, g_core)
    )
    terms = lax.all_to_all(terms.astype(half), "seq", 0, 0, tiled=True)

    def factors(own, first):
        beside = exchange(own, first << 6)
        return [own, from_other_core(own), beside, from_other_core(beside)]

    keep, *sent = wide_products(
        [h, h_core, *h_from] + factors(d_query, 1),
        [g, g_core, *g_from] + factors(attended, 3),
    )
    sent = [block.astype(half) for block in sent]
    wide_got = [exchange(block, m << 6) for m, block in zip((3, 1), sent)]
    branch = dot(attended, w_out, ((1,), (1,))).astype(bf)

    terms, _, branch = lax.optimization_barrier((terms, sent, branch))
    d_kv = own_terms(terms.astype(f32))
    narrow, *sent = narrow_products(h, h_core, d_kv, from_other_core(d_kv))
    narrow_got = [exchange(block.astype(half), m << 6) for m, block in zip((3, 1, 2), sent)]

    part = after_x(keep, jnp.stack(wide_got).astype(f32), narrow, jnp.stack(narrow_got).astype(f32))
    part = after_seq(lax.all_to_all(part.astype(half), "seq", 0, 0, tiled=True).astype(f32))
    part = lax.all_to_all(part, AXES, 0, 0, axis_index_groups=Z_HI_GROUPS, tiled=True)
    grad_query, grad_out, grad_key, grad_value = last_sum(part)
    return branch[None], grad_query, grad_key, grad_value, grad_out


def solution(mesh):
    return jax.shard_map(
        local,
        mesh=mesh,
        in_specs=(P("dp", "seq", None), P(), P(), P(), P(), P("dp", "seq", None)),
        out_specs=(
            P("dp", "seq", None),
            P(("dp", "seq"), None),
            P(("dp", "seq"), None),
            P(("dp", "seq"), None),
            P(("dp", "seq"), None),
        ),
        check_vma=False,
    )
```

```python
import functools

import jax
import jax.numpy as jnp
from jax import lax
from jax.experimental import pallas as pl
from jax.experimental.pallas import tpu as pltpu
from jax.sharding import PartitionSpec as P

HEADS = 4
HD = 128
SCALE = HD ** (-0.5)
LOG2_E = 1.4426950408889634
AXES = ("dp", "seq")
MIB = 1024 * 1024


def place(x, y, z, core):
    return x * 64 + (z >> 1) * 16 + core * 8 + (z & 1) * 4 + y


Z_HI_GROUPS = [
    [place(x, y, 2 * z + low, c) for z in range(4)] for x in range(4) for y in range(4) for low in range(2) for c in range(2)
]


def dot(left, right, dims):
    return lax.dot_general(left, right, (dims, ((), ())), preferred_element_type=jnp.float32)


def exchange(value, mask):
    return lax.ppermute(value, AXES, [(i, i ^ mask) for i in range(256)])


def from_other_core(value):
    return exchange(value, 8)


def exponent(values):
    top = jnp.max(jnp.max(jnp.abs(values), axis=0, keepdims=True), axis=1, keepdims=True)
    return jnp.ceil(jnp.log2(jnp.maximum(top, 1e-30))) - 13.0


def unscaled(ref, block, values, exponents):
    return ref[block, values, :] * jnp.exp2(ref[block, exponents, :])


def project_kernel(hidden_hbm, w_key_hbm, w_value_hbm, out_hbm, hidden_ref, weight_ref, block_ref, in_sems, out_sems):
    chunks = in_sems.shape[0]
    depth = hidden_ref.shape[1] // chunks
    copies = []
    for c in range(chunks):
        part = pl.ds(c * depth, depth)
        copies.append(
            [
                pltpu.make_async_copy(hidden_hbm.at[:, part], hidden_ref.at[:, part], in_sems.at[c, 0]),
                pltpu.make_async_copy(w_key_hbm.at[part, :], weight_ref.at[part, pl.ds(0, HD)], in_sems.at[c, 1]),
                pltpu.make_async_copy(w_value_hbm.at[part, :], weight_ref.at[part, pl.ds(HD, HD)], in_sems.at[c, 2]),
            ]
        )
        for copy in copies[-1]:
            copy.start()
    total = None
    for c in range(chunks):
        for copy in copies[c]:
            copy.wait()
        term = dot(hidden_ref[:, c * depth : (c + 1) * depth], weight_ref[c * depth : (c + 1) * depth, :], ((1,), (0,)))
        total = term if total is None else total + term
    block_ref[...] = total.astype(jnp.bfloat16)
    copies = [pltpu.make_async_copy(block_ref, out_hbm.at[b], out_sems.at[b]) for b in range(out_hbm.shape[0])]
    for copy in copies:
        copy.start()
    for copy in copies:
        copy.wait()


def project(hidden, w_key, w_value):
    hidden, w_key, w_value = (pltpu.with_memory_space_constraint(v, pltpu.HBM) for v in (hidden, w_key, w_value))
    tokens, width = hidden.shape
    anywhere = pl.BlockSpec(memory_space=pl.ANY)
    return pl.pallas_call(
        project_kernel,
        in_specs=[anywhere] * 3,
        out_specs=anywhere,
        out_shape=pltpu.HBM((8, tokens, 2 * HD), jnp.bfloat16),
        scratch_shapes=[
            pltpu.VMEM((tokens, width), jnp.bfloat16),
            pltpu.VMEM((width, 2 * HD), jnp.bfloat16),
            pltpu.VMEM((tokens, 2 * HD), jnp.bfloat16),
            pltpu.SemaphoreType.DMA((3, 3)),
            pltpu.SemaphoreType.DMA((8,)),
        ],
        compiler_params=pltpu.CompilerParams(vmem_limit_bytes=16 * MIB),
        name="project",
    )(hidden, w_key, w_value)


def turn_kernel(pieces, place_ref, side_ref, *refs):
    turned_ref = refs[-1]
    turned_ref[...] = side_ref[...].T
    for ref, (far, masks) in zip(refs, pieces):
        for i, mask in enumerate(masks):
            for z_hi in range(4):
                start = 384 * (place_ref[0] ^ mask) + 96 * z_hi + 48 * (place_ref[1] ^ far)
                first = 192 * i + 48 * z_hi
                ref[first : first + 48, :] = turned_ref[pl.ds(pl.multiple_of(start, 16), 48), :]


def turn(place, side, pieces):
    tokens, width = side.shape
    shapes = [(len(masks) * width // 8, tokens) for _, masks in pieces]
    return pl.pallas_call(
        functools.partial(turn_kernel, pieces),
        grid_spec=pltpu.PrefetchScalarGridSpec(
            num_scalar_prefetch=1,
            grid=(1,),
            in_specs=[pl.BlockSpec((tokens, width), lambda i, place: (0, 0))],
            out_specs=[pl.BlockSpec(shape, lambda i, place: (0, 0)) for shape in shapes],
            scratch_shapes=[pltpu.VMEM((width, tokens), side.dtype)],
        ),
        out_shape=[jax.ShapeDtypeStruct(shape, side.dtype) for shape in shapes],
        compiler_params=pltpu.CompilerParams(vmem_limit_bytes=12 * MIB),
        name="turn",
    )(place, side)


def attention_kernel(
    q_hbm, da_hbm, kv_hbm, d_query_hbm, attended_hbm, dkv_ref,
    q_ref, da_ref, k_ref, v_ref, d_query_ref, attended_ref, scores_ref, d_probs_ref, probs_ref, d_scores_ref,
    side_sems, block_sems, out_sems,
):
    bf = jnp.bfloat16
    blocks, _, tokens = dkv_ref.shape
    chunk = 16
    head_cols = lambda h: slice(h * HD, (h + 1) * HD)
    block_rows = lambda b: slice(b * tokens, (b + 1) * tokens)
    sides_in = [
        pltpu.make_async_copy(source, ref, side_sems.at[i])
        for i, (source, ref) in enumerate(((q_hbm, q_ref), (da_hbm, da_ref)))
    ]
    blocks_in = [
        [
            pltpu.make_async_copy(
                kv_hbm.at[pl.ds(b * tokens, tokens), pl.ds(i * HD, HD)],
                ref.at[pl.ds(b * tokens, tokens), :],
                block_sems.at[i, b],
            )
            for b in range(blocks)
        ]
        for i, ref in enumerate((k_ref, v_ref))
    ]
    for copy in sides_in:
        copy.start()
    for b in range(blocks):
        for i in range(2):
            blocks_in[i][b].start()
    leaving = []

    def ahead(h):
        def make(b, i, side_ref, other_ref, to_ref):
            def run():
                if h == 0:
                    blocks_in[i][b].wait()
                    if b == 0:
                        sides_in[i].wait()
                to_ref[h % 2, :, block_rows(b)] = dot(side_ref[:, head_cols(h)], other_ref[block_rows(b), :], ((1,), (1,)))

            return run

        return [
            make(b, *refs)
            for b in range(blocks)
            for refs in ((0, q_ref, k_ref, scores_ref), (1, da_ref, v_ref, d_probs_ref))
        ]

    def softmax(h, i):
        rows = slice(i * chunk, (i + 1) * chunk)
        scores = scores_ref[h % 2, rows, :]
        shifted = jnp.exp2((scores - jnp.max(scores, axis=1, keepdims=True)) * (SCALE * LOG2_E))
        probs = shifted * (1.0 / jnp.sum(shifted, axis=1, keepdims=True))
        d_probs = d_probs_ref[h % 2, rows, :]
        delta = jnp.sum(d_probs * probs, axis=1, keepdims=True)
        probs_ref[h % 2, rows, :] = probs.astype(bf)
        d_scores_ref[h % 2, rows, :] = (probs * (d_probs - delta)).astype(bf)

    def behind(h):
        sides = [ref[:, head_cols(h)].T for ref in (q_ref, da_ref)]

        def terms(b, i, from_ref):
            def run():
                term = dot(sides[i], from_ref[h % 2, :, block_rows(b)], ((1,), (0,)))
                rows = slice(i * HD, (i + 1) * HD)
                dkv_ref[b, rows, :] = term if h == 0 else dkv_ref[b, rows, :] + term

            return run

        def rows_of(from_ref, other_ref, to_ref, scale, to_hbm, i):
            def run():
                product = dot(from_ref[h % 2], other_ref[...], ((1,), (0,)))
                to_ref[:, head_cols(h)] = (product * scale if scale else product).astype(bf)
                here = (slice(None), pl.ds(h * HD, HD))
                leaving.append(pltpu.make_async_copy(to_ref.at[here], to_hbm.at[here], out_sems.at[i, h]))
                leaving[-1].start()

            return run

        work = [terms(b, i, ref) for b in range(blocks) for i, ref in enumerate((d_scores_ref, probs_ref))]
        work.insert(4, rows_of(probs_ref, v_ref, attended_ref, None, attended_hbm, 0))
        work.insert(13, rows_of(d_scores_ref, k_ref, d_query_ref, SCALE, d_query_hbm, 1))
        return work

    for run in ahead(0):
        run()
    for h in range(HEADS):
        beside = []
        if h + 1 < HEADS:
            beside += [(n / 16, run) for n, run in enumerate(ahead(h + 1))]
        if h > 0:
            beside += [(n / 18, run) for n, run in enumerate(behind(h - 1))]
        beside.sort(key=lambda entry: entry[0])
        steps = tokens // chunk
        for i in range(steps):
            softmax(h, i)
            for at, run in beside:
                if i <= at * steps < i + 1:
                    run()
    for run in behind(HEADS - 1):
        run()

    for i, scale in enumerate((SCALE, 1.0)):
        rows = pl.ds(i * HD, HD)
        top = jnp.abs(dkv_ref[0, rows, :])
        for b in range(1, blocks):
            top = jnp.maximum(top, jnp.abs(dkv_ref[b, rows, :]))
        power = exponent(top * scale)
        factor = jnp.exp2(-power) * scale
        for b in range(blocks):
            dkv_ref[b, rows, :] = dkv_ref[b, rows, :] * factor
            dkv_ref[b, pl.ds(2 * HD + 4 * i, 4), :] = jnp.broadcast_to(power, (4, tokens))
    for copy in leaving:
        copy.wait()


def attention(queries, d_att, keys_values):
    tokens, inner = queries.shape
    length = keys_values.shape[0]
    blocks = length // tokens
    anywhere = pl.BlockSpec(memory_space=pl.ANY)
    small, large = pltpu.VMEM((tokens, inner), jnp.bfloat16), pltpu.VMEM((length, HD), jnp.bfloat16)
    wide, half = pltpu.VMEM((2, tokens, length), jnp.float32), pltpu.VMEM((2, tokens, length), jnp.bfloat16)
    operands = [pltpu.with_memory_space_constraint(v, pltpu.HBM) for v in (queries, d_att, keys_values)]
    return pl.pallas_call(
        attention_kernel,
        in_specs=[anywhere] * 3,
        out_specs=[anywhere, anywhere, pl.BlockSpec(memory_space=pltpu.VMEM)],
        out_shape=[
            pltpu.HBM((tokens, inner), jnp.bfloat16),
            pltpu.HBM((tokens, inner), jnp.bfloat16),
            jax.ShapeDtypeStruct((blocks, 2 * HD + 8, tokens), jnp.float32),
        ],
        scratch_shapes=[small, small, large, large, small, small, wide, wide, half, half]
        + [pltpu.SemaphoreType.DMA((2,)), pltpu.SemaphoreType.DMA((2, blocks)), pltpu.SemaphoreType.DMA((2, HEADS))],
        compiler_params=pltpu.CompilerParams(vmem_limit_bytes=32 * MIB),
        cost_estimate=pl.CostEstimate(
            flops=12 * tokens * inner * length, bytes_accessed=4 << 20, transcendentals=tokens * HEADS * length
        ),
        name="attention",
    )(*operands)


def store_scaled(values, ref):
    power = exponent(values)
    ref[:-8, :] = values * jnp.exp2(-power)
    ref[-8:, :] = jnp.broadcast_to(power, (8, values.shape[1]))


def wide_kernel(*refs):
    keep_ref, *send_refs = refs[16:]
    rows, cols = keep_ref.shape[0], send_refs[0].shape[1]
    for i in range(2):
        product = None
        for side_ref, factor_ref in zip(refs[8 * i : 8 * i + 4], refs[8 * i + 4 : 8 * i + 8]):
            term = dot(side_ref[: 2 * rows], factor_ref[...], ((1,), (0,)))
            product = term if product is None else product + term
        keep_ref[:, i * cols : (i + 1) * cols] = product[:rows]
        store_scaled(product[rows:], send_refs[i])


def wide_products(query, out):
    rows = out[0].shape[0] // 2
    cols = out[4].shape[1]
    query, out = (v[:4] + [pltpu.with_memory_space_constraint(f, pltpu.HBM) for f in v[4:]] for v in (query, out))
    return pl.pallas_call(
        wide_kernel,
        out_shape=[
            pltpu.HBM((rows, 2 * cols), jnp.float32),
            jax.ShapeDtypeStruct((rows + 8, cols), jnp.float32),
            jax.ShapeDtypeStruct((rows + 8, cols), jnp.float32),
        ],
        compiler_params=pltpu.CompilerParams(vmem_limit_bytes=20 * MIB),
        cost_estimate=pl.CostEstimate(flops=1 << 30, bytes_accessed=5 << 20, transcendentals=0),
        name="wide",
    )(*query, *out)


def narrow_kernel(mine_ref, theirs_ref, own_ref, other_ref, keep_ref, three_ref, one_ref, two_ref):
    product = None
    for side_ref, terms_ref in ((mine_ref, own_ref), (theirs_ref, other_ref)):
        side = side_ref[...]
        rest = terms_ref[...]
        for _ in range(2):
            piece = rest.astype(jnp.bfloat16)
            rest = rest - piece.astype(jnp.float32)
            term = dot(side, piece, ((1,), (1,)))
            product = term if product is None else product + term
    rows = keep_ref.shape[0]
    keep_ref[...] = product[:rows]
    powers = [jnp.broadcast_to(exponent(product[:, i * HD : (i + 1) * HD]), (8, HD)) for i in range(2)]
    power = jnp.concatenate(powers, axis=1)
    factor = jnp.exp2(-power[:1])
    for i, ref in enumerate((three_ref, one_ref, two_ref)):
        ref[:rows, :] = product[(i + 1) * rows : (i + 2) * rows] * factor
        ref[rows:, :] = power


def narrow_products(mine, theirs, own, other):
    rows = mine.shape[0] // 4
    cols = own.shape[0]
    sent = jax.ShapeDtypeStruct((rows + 8, cols), jnp.float32)
    return pl.pallas_call(
        narrow_kernel,
        out_shape=[pltpu.HBM((rows, cols), jnp.float32), sent, sent, sent],
        compiler_params=pltpu.CompilerParams(vmem_limit_bytes=16 * MIB),
        cost_estimate=pl.CostEstimate(flops=1, bytes_accessed=1, transcendentals=0),
        name="narrow",
    )(mine, theirs, own, other)


def own_terms_kernel(terms_ref, out_ref):
    for i in range(2):
        rows, powers = pl.ds(i * HD, HD), pl.ds(2 * HD + 4 * i, 1)
        total = unscaled(terms_ref, 0, rows, powers)
        for b in range(1, terms_ref.shape[0]):
            total = total + unscaled(terms_ref, b, rows, powers)
        out_ref[rows, :] = total


def own_terms(terms):
    return pl.pallas_call(
        own_terms_kernel,
        out_shape=jax.ShapeDtypeStruct((2 * HD, terms.shape[2]), jnp.float32),
        compiler_params=pltpu.CompilerParams(vmem_limit_bytes=8 * MIB),
        cost_estimate=pl.CostEstimate(flops=1, bytes_accessed=1, transcendentals=0),
        name="own_terms",
    )(terms)


def after_x_kernel(wide_ref, wide_got_ref, narrow_ref, narrow_got_ref, out_ref, total_ref):
    rows = wide_ref.shape[0]
    cols = 4 * HD
    scaled = lambda ref, i, here: ref[i, :rows, here] * jnp.exp2(ref[i, rows : rows + 1, here])
    for i, (first, width) in enumerate(((0, cols), (cols, cols), (2 * cols, HD), (2 * cols + HD, HD))):
        if i < 2:
            total = wide_ref[:, first : first + width] + scaled(wide_got_ref, i, pl.ds(0, cols))
        else:
            here = pl.ds(first - 2 * cols, HD)
            total = narrow_ref[:, here]
            for m in range(3):
                total = total + scaled(narrow_got_ref, m, here)
        top = exponent(total)
        total_ref[:, first : first + width] = total * jnp.exp2(-top)
        out_ref[:, 240 + i, :] = jnp.broadcast_to(top, (out_ref.shape[0], HD))
    out_ref[:, 244:, :] = jnp.zeros((out_ref.shape[0], 4, HD), jnp.float32)
    for k in range(out_ref.shape[0]):
        for j in range(10):
            for z_hi in range(4):
                to, start = 24 * j + 6 * z_hi, 48 * z_hi + 6 * k
                out_ref[k, to : to + 6, :] = total_ref[start : start + 6, j * HD : (j + 1) * HD]


def after_x(wide, wide_got, narrow, narrow_got):
    rows, cols = wide.shape
    shape = (rows // 24, 248, HD)
    return pl.pallas_call(
        after_x_kernel,
        out_shape=jax.ShapeDtypeStruct(shape, jnp.float32),
        scratch_shapes=[pltpu.VMEM((rows, cols + narrow.shape[1]), jnp.float32)],
        compiler_params=pltpu.CompilerParams(vmem_limit_bytes=16 * MIB),
        name="after_x",
    )(wide, wide_got, narrow, narrow_got)


def after_seq_kernel(got_ref, out_ref, total_ref):
    for i, (first, count) in enumerate(((0, 96), (96, 96), (192, 24), (216, 24))):
        rows = pl.ds(first, count)
        total = unscaled(got_ref, 0, rows, pl.ds(240 + i, 1))
        for b in range(1, got_ref.shape[0]):
            total = total + unscaled(got_ref, b, rows, pl.ds(240 + i, 1))
        total_ref[rows, :] = total
    for k in range(4):
        for j in range(10):
            out_ref[k, 6 * j : 6 * j + 6, :] = total_ref[24 * j + 6 * k : 24 * j + 6 * k + 6, :]
        out_ref[k, 60:, :] = jnp.zeros((4, HD), jnp.float32)


def after_seq(got):
    return pl.pallas_call(
        after_seq_kernel,
        out_shape=jax.ShapeDtypeStruct((4, 64, HD), jnp.float32),
        scratch_shapes=[pltpu.VMEM((240, HD), jnp.float32)],
        compiler_params=pltpu.CompilerParams(vmem_limit_bytes=8 * MIB),
        name="after_seq",
    )(got)


def last_sum_kernel(got_ref, query_ref, out_ref, key_ref, value_ref):
    total = (got_ref[0] + got_ref[1]) + (got_ref[2] + got_ref[3])
    first = 0
    for ref in (query_ref, out_ref, key_ref, value_ref):
        for j in range(ref.shape[1] // HD):
            ref[:, j * HD : (j + 1) * HD] = total[first : first + 6]
            first += 6


def last_sum(got):
    shape = lambda cols: jax.ShapeDtypeStruct((6, cols), jnp.float32)
    return pl.pallas_call(
        last_sum_kernel,
        out_shape=[shape(4 * HD), shape(4 * HD), shape(HD), shape(HD)],
        compiler_params=pltpu.CompilerParams(vmem_limit_bytes=8 * MIB),
        name="last_sum",
    )(got)


def local(normed, w_query, w_key, w_value, w_out, cotangent):
    hidden = normed[0]
    grads_in = cotangent[0]
    tokens = hidden.shape[0]
    bf, half = jnp.bfloat16, jnp.float16
    dp = lax.axis_index("dp")
    x, core = dp >> 3, dp & 1
    f32 = jnp.float32

    gathered = lax.all_to_all(project(hidden, w_key, w_value), "seq", 0, 0, tiled=True)

    queries = dot(hidden, w_query, ((1,), (0,))).astype(bf)
    d_att = dot(grads_in, w_out, ((1,), (0,))).astype(bf)
    place_now = jnp.stack([x, core])
    h, h_core, *h_far = turn(place_now, hidden, ((0, (0, 3, 1, 2)), (1, (0, 3, 1, 2)), (0, (1, 2)), (1, (1, 2))))
    g, g_core, *g_far = turn(place_now, grads_in, ((0, (0, 1)), (1, (0, 1)), (0, (3, 2)), (1, (3, 2))))
    h_from = [exchange(h_far[0], 1 << 6), exchange(h_far[1], (1 << 6) | 8)]
    g_from = [exchange(g_far[0], 3 << 6), exchange(g_far[1], (3 << 6) | 8)]
    h_core, g_core = from_other_core(h_core), from_other_core(g_core)

    d_query, attended, terms = attention(queries, d_att, gathered.reshape(8 * tokens, 2 * HD))
    terms, d_query, attended, h_from, g_from, h_core, g_core = lax.optimization_barrier(
        (terms, d_query, attended, h_from, g_from, h_core, g_core)
    )
    terms = lax.all_to_all(terms.astype(half), "seq", 0, 0, tiled=True)

    def factors(own, first):
        beside = exchange(own, first << 6)
        return [own, from_other_core(own), beside, from_other_core(beside)]

    keep, *sent = wide_products(
        [h, h_core, *h_from] + factors(d_query, 1),
        [g, g_core, *g_from] + factors(attended, 3),
    )
    sent = [block.astype(half) for block in sent]
    wide_got = [exchange(block, m << 6) for m, block in zip((3, 1), sent)]
    branch = dot(attended, w_out, ((1,), (1,))).astype(bf)

    terms, _, branch = lax.optimization_barrier((terms, sent, branch))
    d_kv = own_terms(terms.astype(f32))
    narrow, *sent = narrow_products(h, h_core, d_kv, from_other_core(d_kv))
    narrow_got = [exchange(block.astype(half), m << 6) for m, block in zip((3, 1, 2), sent)]

    part = after_x(keep, jnp.stack(wide_got).astype(f32), narrow, jnp.stack(narrow_got).astype(f32))
    part = after_seq(lax.all_to_all(part.astype(half), "seq", 0, 0, tiled=True).astype(f32))
    part = lax.all_to_all(part, AXES, 0, 0, axis_index_groups=Z_HI_GROUPS, tiled=True)
    grad_query, grad_out, grad_key, grad_value = last_sum(part)
    return branch[None], grad_query, grad_key, grad_value, grad_out


def solution(mesh):
    return jax.shard_map(
        local,
        mesh=mesh,
        in_specs=(P("dp", "seq", None), P(), P(), P(), P(), P("dp", "seq", None)),
        out_specs=(
            P("dp", "seq", None),
            P(("dp", "seq"), None),
            P(("dp", "seq"), None),
            P(("dp", "seq"), None),
            P(("dp", "seq"), None),
        ),
        check_vma=False,
    )
```

```python
import functools

import jax
import jax.numpy as jnp
from jax import lax
from jax.experimental import pallas as pl
from jax.experimental.pallas import tpu as pltpu
from jax.sharding import PartitionSpec as P

HEADS = 4
HD = 128
SCALE = HD ** (-0.5)
LOG2_E = 1.4426950408889634
AXES = ("dp", "seq")
MIB = 1024 * 1024


def place(x, y, z, core):
    return x * 64 + (z >> 1) * 16 + core * 8 + (z & 1) * 4 + y


YZ_GROUPS = [[place(x, y, z, c) for y in range(4) for z in range(8)] for x in range(4) for c in range(2)]


def dot(left, right, dims):
    return lax.dot_general(left, right, (dims, ((), ())), preferred_element_type=jnp.float32)


def exchange(value, mask):
    return lax.ppermute(value, AXES, [(i, i ^ mask) for i in range(256)])


def from_other_core(value):
    return exchange(value, 8)


def exponent(values):
    top = jnp.max(jnp.max(jnp.abs(values), axis=0, keepdims=True), axis=1, keepdims=True)
    return jnp.ceil(jnp.log2(jnp.maximum(top, 1e-30))) - 13.0


def unscaled(ref, block, values, exponents):
    return ref[block, values, :] * jnp.exp2(ref[block, exponents, :])


def project_kernel(hidden_ref, w_key_ref, w_value_ref, out_ref):
    hidden = hidden_ref[...]
    for i, ref in enumerate((w_key_ref, w_value_ref)):
        block = dot(hidden, ref[...], ((1,), (0,))).astype(jnp.bfloat16)
        for b in range(out_ref.shape[0]):
            out_ref[b, :, i * HD : (i + 1) * HD] = block


def project(hidden, w_key, w_value):
    hidden, w_key, w_value = (pltpu.with_memory_space_constraint(v, pltpu.HBM) for v in (hidden, w_key, w_value))
    return pl.pallas_call(
        project_kernel,
        out_shape=jax.ShapeDtypeStruct((8, hidden.shape[0], 2 * HD), jnp.bfloat16),
        compiler_params=pltpu.CompilerParams(vmem_limit_bytes=16 * MIB),
        name="project",
    )(hidden, w_key, w_value)


def turn_kernel(pieces, place_ref, side_ref, *refs):
    turned_ref = refs[-1]
    turned_ref[...] = side_ref[...].T
    for ref, (far, masks) in zip(refs, pieces):
        for i, mask in enumerate(masks):
            for z_hi in range(4):
                start = 384 * (place_ref[0] ^ mask) + 96 * z_hi + 48 * (place_ref[1] ^ far)
                first = 192 * i + 48 * z_hi
                ref[first : first + 48, :] = turned_ref[pl.ds(pl.multiple_of(start, 16), 48), :]


def turn(place, side, pieces):
    tokens, width = side.shape
    shapes = [(len(masks) * width // 8, tokens) for _, masks in pieces]
    return pl.pallas_call(
        functools.partial(turn_kernel, pieces),
        grid_spec=pltpu.PrefetchScalarGridSpec(
            num_scalar_prefetch=1,
            grid=(1,),
            in_specs=[pl.BlockSpec((tokens, width), lambda i, place: (0, 0))],
            out_specs=[pl.BlockSpec(shape, lambda i, place: (0, 0)) for shape in shapes],
            scratch_shapes=[pltpu.VMEM((width, tokens), side.dtype)],
        ),
        out_shape=[jax.ShapeDtypeStruct(shape, side.dtype) for shape in shapes],
        compiler_params=pltpu.CompilerParams(vmem_limit_bytes=12 * MIB),
        name="turn",
    )(place, side)


def attention_kernel(
    q_hbm, da_hbm, kv_hbm, d_query_hbm, attended_hbm, dkv_ref,
    q_ref, da_ref, k_ref, v_ref, d_query_ref, attended_ref, scores_ref, d_probs_ref, probs_ref, d_scores_ref,
    in_sems, out_sems,
):
    bf = jnp.bfloat16
    blocks, _, tokens = dkv_ref.shape
    chunk = 16
    head_cols = lambda h: slice(h * HD, (h + 1) * HD)
    block_rows = lambda b: slice(b * tokens, (b + 1) * tokens)
    arriving = [
        pltpu.make_async_copy(source, ref, in_sems.at[i])
        for i, (source, ref) in enumerate(
            (
                (kv_hbm.at[:, pl.ds(0, HD)], k_ref),
                (q_hbm, q_ref),
                (kv_hbm.at[:, pl.ds(HD, HD)], v_ref),
                (da_hbm, da_ref),
            )
        )
    ]
    for copy in arriving:
        copy.start()
    for copy in arriving:
        copy.wait()

    def ahead(h):
        def make(b, side_ref, other_ref, to_ref):
            def run():
                to_ref[h % 2, :, block_rows(b)] = dot(side_ref[:, head_cols(h)], other_ref[block_rows(b), :], ((1,), (1,)))

            return run

        return [
            make(b, *refs)
            for b in range(blocks)
            for refs in ((q_ref, k_ref, scores_ref), (da_ref, v_ref, d_probs_ref))
        ]

    def softmax(h, i):
        rows = slice(i * chunk, (i + 1) * chunk)
        scores = scores_ref[h % 2, rows, :]
        shifted = jnp.exp2((scores - jnp.max(scores, axis=1, keepdims=True)) * (SCALE * LOG2_E))
        probs = shifted * (1.0 / jnp.sum(shifted, axis=1, keepdims=True))
        d_probs = d_probs_ref[h % 2, rows, :]
        delta = jnp.sum(d_probs * probs, axis=1, keepdims=True)
        probs_ref[h % 2, rows, :] = probs.astype(bf)
        d_scores_ref[h % 2, rows, :] = (probs * (d_probs - delta)).astype(bf)

    def behind(h):
        sides = [ref[:, head_cols(h)].T for ref in (q_ref, da_ref)]

        def terms(b, i, from_ref):
            def run():
                term = dot(sides[i], from_ref[h % 2, :, block_rows(b)], ((1,), (0,)))
                rows = slice(i * HD, (i + 1) * HD)
                dkv_ref[b, rows, :] = term if h == 0 else dkv_ref[b, rows, :] + term

            return run

        def rows_of(from_ref, other_ref, to_ref, scale):
            def run():
                product = dot(from_ref[h % 2], other_ref[...], ((1,), (0,)))
                to_ref[:, head_cols(h)] = (product * scale if scale else product).astype(bf)

            return run

        work = [terms(b, i, ref) for b in range(blocks) for i, ref in enumerate((d_scores_ref, probs_ref))]
        work.insert(4, rows_of(probs_ref, v_ref, attended_ref, None))
        work.insert(13, rows_of(d_scores_ref, k_ref, d_query_ref, SCALE))
        return work

    for run in ahead(0):
        run()
    for h in range(HEADS):
        beside = []
        if h + 1 < HEADS:
            beside += [(n / 16, run) for n, run in enumerate(ahead(h + 1))]
        if h > 0:
            beside += [(n / 18, run) for n, run in enumerate(behind(h - 1))]
        beside.sort(key=lambda entry: entry[0])
        steps = tokens // chunk
        for i in range(steps):
            softmax(h, i)
            for at, run in beside:
                if i <= at * steps < i + 1:
                    run()
    for run in behind(HEADS - 1):
        run()

    leaving = [
        pltpu.make_async_copy(ref, target, out_sems.at[i])
        for i, (ref, target) in enumerate(((d_query_ref, d_query_hbm), (attended_ref, attended_hbm)))
    ]
    for copy in leaving:
        copy.start()
    for i, scale in enumerate((SCALE, 1.0)):
        rows = pl.ds(i * HD, HD)
        top = jnp.abs(dkv_ref[0, rows, :])
        for b in range(1, blocks):
            top = jnp.maximum(top, jnp.abs(dkv_ref[b, rows, :]))
        power = exponent(top * scale)
        factor = jnp.exp2(-power) * scale
        for b in range(blocks):
            dkv_ref[b, rows, :] = dkv_ref[b, rows, :] * factor
            dkv_ref[b, pl.ds(2 * HD + 4 * i, 4), :] = jnp.broadcast_to(power, (4, tokens))
    for copy in leaving:
        copy.wait()


def attention(queries, d_att, keys_values):
    tokens, inner = queries.shape
    length = keys_values.shape[0]
    blocks = length // tokens
    anywhere = pl.BlockSpec(memory_space=pl.ANY)
    small, large = pltpu.VMEM((tokens, inner), jnp.bfloat16), pltpu.VMEM((length, HD), jnp.bfloat16)
    wide, half = pltpu.VMEM((2, tokens, length), jnp.float32), pltpu.VMEM((2, tokens, length), jnp.bfloat16)
    operands = [pltpu.with_memory_space_constraint(v, pltpu.HBM) for v in (queries, d_att, keys_values)]
    return pl.pallas_call(
        attention_kernel,
        in_specs=[anywhere] * 3,
        out_specs=[anywhere, anywhere, pl.BlockSpec(memory_space=pltpu.VMEM)],
        out_shape=[
            pltpu.HBM((tokens, inner), jnp.bfloat16),
            pltpu.HBM((tokens, inner), jnp.bfloat16),
            jax.ShapeDtypeStruct((blocks, 2 * HD + 8, tokens), jnp.float32),
        ],
        scratch_shapes=[small, small, large, large, small, small, wide, wide, half, half]
        + [pltpu.SemaphoreType.DMA((4,)), pltpu.SemaphoreType.DMA((2,))],
        compiler_params=pltpu.CompilerParams(vmem_limit_bytes=32 * MIB),
        cost_estimate=pl.CostEstimate(
            flops=12 * tokens * inner * length, bytes_accessed=4 << 20, transcendentals=tokens * HEADS * length
        ),
        name="attention",
    )(*operands)


def store_scaled(values, ref):
    power = exponent(values)
    ref[:-8, :] = values * jnp.exp2(-power)
    ref[-8:, :] = jnp.broadcast_to(power, (8, values.shape[1]))


def wide_kernel(*refs):
    keep_ref, *send_refs = refs[16:]
    rows, cols = keep_ref.shape[0], send_refs[0].shape[1]
    for i in range(2):
        product = None
        for side_ref, factor_ref in zip(refs[8 * i : 8 * i + 4], refs[8 * i + 4 : 8 * i + 8]):
            term = dot(side_ref[: 2 * rows], factor_ref[...], ((1,), (0,)))
            product = term if product is None else product + term
        keep_ref[:, i * cols : (i + 1) * cols] = product[:rows]
        store_scaled(product[rows:], send_refs[i])


def wide_products(query, out):
    rows = out[0].shape[0] // 2
    cols = out[4].shape[1]
    query, out = (v[:4] + [pltpu.with_memory_space_constraint(f, pltpu.HBM) for f in v[4:]] for v in (query, out))
    return pl.pallas_call(
        wide_kernel,
        out_shape=[
            pltpu.HBM((rows, 2 * cols), jnp.float32),
            jax.ShapeDtypeStruct((rows + 8, cols), jnp.float32),
            jax.ShapeDtypeStruct((rows + 8, cols), jnp.float32),
        ],
        compiler_params=pltpu.CompilerParams(vmem_limit_bytes=20 * MIB),
        cost_estimate=pl.CostEstimate(flops=1 << 30, bytes_accessed=5 << 20, transcendentals=0),
        name="wide",
    )(*query, *out)


def narrow_kernel(mine_ref, theirs_ref, own_ref, other_ref, keep_ref, three_ref, one_ref, two_ref):
    product = None
    for side_ref, terms_ref in ((mine_ref, own_ref), (theirs_ref, other_ref)):
        side = side_ref[...]
        rest = terms_ref[...]
        for _ in range(2):
            piece = rest.astype(jnp.bfloat16)
            rest = rest - piece.astype(jnp.float32)
            term = dot(side, piece, ((1,), (1,)))
            product = term if product is None else product + term
    rows = keep_ref.shape[0]
    keep_ref[...] = product[:rows]
    powers = [jnp.broadcast_to(exponent(product[:, i * HD : (i + 1) * HD]), (8, HD)) for i in range(2)]
    power = jnp.concatenate(powers, axis=1)
    factor = jnp.exp2(-power[:1])
    for i, ref in enumerate((three_ref, one_ref, two_ref)):
        ref[:rows, :] = product[(i + 1) * rows : (i + 2) * rows] * factor
        ref[rows:, :] = power


def narrow_products(mine, theirs, own, other):
    rows = mine.shape[0] // 4
    cols = own.shape[0]
    sent = jax.ShapeDtypeStruct((rows + 8, cols), jnp.float32)
    return pl.pallas_call(
        narrow_kernel,
        out_shape=[pltpu.HBM((rows, cols), jnp.float32), sent, sent, sent],
        compiler_params=pltpu.CompilerParams(vmem_limit_bytes=16 * MIB),
        cost_estimate=pl.CostEstimate(flops=1, bytes_accessed=1, transcendentals=0),
        name="narrow",
    )(mine, theirs, own, other)


def own_terms_kernel(terms_ref, out_ref):
    for i in range(2):
        rows, powers = pl.ds(i * HD, HD), pl.ds(2 * HD + 4 * i, 1)
        total = unscaled(terms_ref, 0, rows, powers)
        for b in range(1, terms_ref.shape[0]):
            total = total + unscaled(terms_ref, b, rows, powers)
        out_ref[rows, :] = total


def own_terms(terms):
    return pl.pallas_call(
        own_terms_kernel,
        out_shape=jax.ShapeDtypeStruct((2 * HD, terms.shape[2]), jnp.float32),
        compiler_params=pltpu.CompilerParams(vmem_limit_bytes=8 * MIB),
        cost_estimate=pl.CostEstimate(flops=1, bytes_accessed=1, transcendentals=0),
        name="own_terms",
    )(terms)


def after_x_kernel(wide_ref, wide_got_ref, narrow_ref, narrow_got_ref, out_ref, total_ref):
    rows = wide_ref.shape[0]
    cols = 4 * HD
    scaled = lambda ref, i, here: ref[i, :rows, here] * jnp.exp2(ref[i, rows : rows + 1, here])
    for i, (first, width) in enumerate(((0, cols), (cols, cols), (2 * cols, HD), (2 * cols + HD, HD))):
        if i < 2:
            total = wide_ref[:, first : first + width] + scaled(wide_got_ref, i, pl.ds(0, cols))
        else:
            here = pl.ds(first - 2 * cols, HD)
            total = narrow_ref[:, here]
            for m in range(3):
                total = total + scaled(narrow_got_ref, m, here)
        top = exponent(total)
        total_ref[:, first : first + width] = total * jnp.exp2(-top)
        out_ref[:, 60 + i, :] = jnp.broadcast_to(top, (out_ref.shape[0], HD))
    for k in range(out_ref.shape[0]):
        y, z = k // 8, k % 8
        start = 48 * (z // 2) + 6 * (4 * (z % 2) + y)
        for j in range(10):
            out_ref[k, 6 * j : 6 * j + 6, :] = total_ref[start : start + 6, j * HD : (j + 1) * HD]


def after_x(wide, wide_got, narrow, narrow_got):
    rows, cols = wide.shape
    shape = (rows // 6, 64, HD)
    return pl.pallas_call(
        after_x_kernel,
        out_shape=jax.ShapeDtypeStruct(shape, jnp.float32),
        scratch_shapes=[pltpu.VMEM((rows, cols + narrow.shape[1]), jnp.float32)],
        compiler_params=pltpu.CompilerParams(vmem_limit_bytes=16 * MIB),
        name="after_x",
    )(wide, wide_got, narrow, narrow_got)


def last_sum_kernel(got_ref, query_ref, out_ref, key_ref, value_ref):
    first = 0
    for i, ref in enumerate((query_ref, out_ref, key_ref, value_ref)):
        tiles = ref.shape[1] // HD
        rows = pl.ds(first, 6 * tiles)
        total = unscaled(got_ref, 0, rows, pl.ds(60 + i, 1))
        for b in range(1, got_ref.shape[0]):
            total = total + unscaled(got_ref, b, rows, pl.ds(60 + i, 1))
        for j in range(tiles):
            ref[:, j * HD : (j + 1) * HD] = total[6 * j : 6 * j + 6]
        first += 6 * tiles


def last_sum(got):
    shape = lambda cols: jax.ShapeDtypeStruct((6, cols), jnp.float32)
    return pl.pallas_call(
        last_sum_kernel,
        out_shape=[shape(4 * HD), shape(4 * HD), shape(HD), shape(HD)],
        compiler_params=pltpu.CompilerParams(vmem_limit_bytes=8 * MIB),
        name="last_sum",
    )(got)


def local(normed, w_query, w_key, w_value, w_out, cotangent):
    hidden = normed[0]
    grads_in = cotangent[0]
    tokens = hidden.shape[0]
    bf, half = jnp.bfloat16, jnp.float16
    dp = lax.axis_index("dp")
    x, core = dp >> 3, dp & 1
    f32 = jnp.float32

    gathered = lax.all_to_all(project(hidden, w_key, w_value), "seq", 0, 0, tiled=True)

    queries = dot(hidden, w_query, ((1,), (0,))).astype(bf)
    d_att = dot(grads_in, w_out, ((1,), (0,))).astype(bf)
    place_now = jnp.stack([x, core])
    h, h_core, *h_far = turn(place_now, hidden, ((0, (0, 3, 1, 2)), (1, (0, 3, 1, 2)), (0, (1, 2)), (1, (1, 2))))
    g, g_core, *g_far = turn(place_now, grads_in, ((0, (0, 1)), (1, (0, 1)), (0, (3, 2)), (1, (3, 2))))
    h_from = [exchange(h_far[0], 1 << 6), exchange(h_far[1], (1 << 6) | 8)]
    g_from = [exchange(g_far[0], 3 << 6), exchange(g_far[1], (3 << 6) | 8)]
    h_core, g_core = from_other_core(h_core), from_other_core(g_core)

    d_query, attended, terms = attention(queries, d_att, gathered.reshape(8 * tokens, 2 * HD))
    terms, d_query, attended, h_from, g_from, h_core, g_core = lax.optimization_barrier(
        (terms, d_query, attended, h_from, g_from, h_core, g_core)
    )
    terms = lax.all_to_all(terms.astype(half), "seq", 0, 0, tiled=True)

    def factors(own, first):
        beside = exchange(own, first << 6)
        return [own, from_other_core(own), beside, from_other_core(beside)]

    keep, *sent = wide_products(
        [h, h_core, *h_from] + factors(d_query, 1),
        [g, g_core, *g_from] + factors(attended, 3),
    )
    sent = [block.astype(half) for block in sent]
    wide_got = [exchange(block, m << 6) for m, block in zip((3, 1), sent)]
    branch = dot(attended, w_out, ((1,), (1,))).astype(bf)

    terms, _, branch = lax.optimization_barrier((terms, sent, branch))
    d_kv = own_terms(terms.astype(f32))
    narrow, *sent = narrow_products(h, h_core, d_kv, from_other_core(d_kv))
    narrow_got = [exchange(block.astype(half), m << 6) for m, block in zip((3, 1, 2), sent)]

    part = after_x(keep, jnp.stack(wide_got).astype(f32), narrow, jnp.stack(narrow_got).astype(f32))
    part = lax.all_to_all(part.astype(half), AXES, 0, 0, axis_index_groups=YZ_GROUPS, tiled=True)
    grad_query, grad_out, grad_key, grad_value = last_sum(part.astype(f32))
    return branch[None], grad_query, grad_key, grad_value, grad_out


def solution(mesh):
    return jax.shard_map(
        local,
        mesh=mesh,
        in_specs=(P("dp", "seq", None), P(), P(), P(), P(), P("dp", "seq", None)),
        out_specs=(
            P("dp", "seq", None),
            P(("dp", "seq"), None),
            P(("dp", "seq"), None),
            P(("dp", "seq"), None),
            P(("dp", "seq"), None),
        ),
        check_vma=False,
    )
```

```python
import functools

import jax
import jax.numpy as jnp
from jax import lax
from jax.experimental import pallas as pl
from jax.experimental.pallas import tpu as pltpu
from jax.sharding import PartitionSpec as P

HEADS = 4
HD = 128
SCALE = HD ** (-0.5)
LOG2_E = 1.4426950408889634
AXES = ("dp", "seq")
MIB = 1024 * 1024


def place(x, y, z, core):
    return x * 64 + (z >> 1) * 16 + core * 8 + (z & 1) * 4 + y


SEQ_GROUPS = [
    [place(x, y, 2 * z + low, c) for y in range(4) for low in range(2)] for x in range(4) for z in range(4) for c in range(2)
]
YZ_GROUPS = [[place(x, y, z, c) for y in range(4) for z in range(8)] for x in range(4) for c in range(2)]


def dot(left, right, dims):
    return lax.dot_general(left, right, (dims, ((), ())), preferred_element_type=jnp.float32)


def exchange(value, mask):
    return lax.ppermute(value, AXES, [(i, i ^ mask) for i in range(256)])


def from_other_core(value):
    return exchange(value, 8)


def exponent(values):
    top = jnp.max(jnp.max(jnp.abs(values), axis=0, keepdims=True), axis=1, keepdims=True)
    return jnp.ceil(jnp.log2(jnp.maximum(top, 1e-30))) - 13.0


def unscaled(ref, block, values, exponents):
    return ref[block, values, :] * jnp.exp2(ref[block, exponents, :])


def project_kernel(hidden_ref, w_key_ref, w_value_ref, out_ref):
    hidden = hidden_ref[...]
    for i, ref in enumerate((w_key_ref, w_value_ref)):
        block = dot(hidden, ref[...], ((1,), (0,))).astype(jnp.bfloat16)
        for b in range(out_ref.shape[0]):
            out_ref[b, :, i * HD : (i + 1) * HD] = block


def project(hidden, w_key, w_value):
    hidden, w_key, w_value = (pltpu.with_memory_space_constraint(v, pltpu.HBM) for v in (hidden, w_key, w_value))
    return pl.pallas_call(
        project_kernel,
        out_shape=jax.ShapeDtypeStruct((8, hidden.shape[0], 2 * HD), jnp.bfloat16),
        compiler_params=pltpu.CompilerParams(vmem_limit_bytes=16 * MIB),
        name="project",
    )(hidden, w_key, w_value)


def turn_kernel(pieces, place_ref, side_ref, *refs):
    turned_ref = refs[-1]
    turned_ref[...] = side_ref[...].T
    for ref, (far, masks) in zip(refs, pieces):
        for i, mask in enumerate(masks):
            for z_hi in range(4):
                start = 384 * (place_ref[0] ^ mask) + 96 * z_hi + 48 * (place_ref[1] ^ far)
                first = 192 * i + 48 * z_hi
                ref[first : first + 48, :] = turned_ref[pl.ds(pl.multiple_of(start, 16), 48), :]


def turn(place, side, pieces):
    tokens, width = side.shape
    shapes = [(len(masks) * width // 8, tokens) for _, masks in pieces]
    return pl.pallas_call(
        functools.partial(turn_kernel, pieces),
        grid_spec=pltpu.PrefetchScalarGridSpec(
            num_scalar_prefetch=1,
            grid=(1,),
            in_specs=[pl.BlockSpec((tokens, width), lambda i, place: (0, 0))],
            out_specs=[pl.BlockSpec(shape, lambda i, place: (0, 0)) for shape in shapes],
            scratch_shapes=[pltpu.VMEM((width, tokens), side.dtype)],
        ),
        out_shape=[jax.ShapeDtypeStruct(shape, side.dtype) for shape in shapes],
        compiler_params=pltpu.CompilerParams(vmem_limit_bytes=12 * MIB),
        name="turn",
    )(place, side)


def attention_kernel(
    q_hbm, da_hbm, kv_hbm, d_query_hbm, attended_hbm, dkv_ref,
    q_ref, da_ref, k_ref, v_ref, d_query_ref, attended_ref, scores_ref, d_probs_ref, probs_ref, d_scores_ref,
    in_sems, out_sems,
):
    bf = jnp.bfloat16
    blocks, _, tokens = dkv_ref.shape
    chunk = 16
    head_cols = lambda h: slice(h * HD, (h + 1) * HD)
    block_rows = lambda b: slice(b * tokens, (b + 1) * tokens)
    arriving = [
        pltpu.make_async_copy(source, ref, in_sems.at[i])
        for i, (source, ref) in enumerate(
            (
                (kv_hbm.at[:, pl.ds(0, HD)], k_ref),
                (q_hbm, q_ref),
                (kv_hbm.at[:, pl.ds(HD, HD)], v_ref),
                (da_hbm, da_ref),
            )
        )
    ]
    for copy in arriving:
        copy.start()
    for copy in arriving:
        copy.wait()

    def ahead(h):
        def make(b, side_ref, other_ref, to_ref):
            def run():
                to_ref[h % 2, :, block_rows(b)] = dot(side_ref[:, head_cols(h)], other_ref[block_rows(b), :], ((1,), (1,)))

            return run

        return [
            make(b, *refs)
            for b in range(blocks)
            for refs in ((q_ref, k_ref, scores_ref), (da_ref, v_ref, d_probs_ref))
        ]

    def softmax(h, i):
        rows = slice(i * chunk, (i + 1) * chunk)
        scores = scores_ref[h % 2, rows, :]
        shifted = jnp.exp2((scores - jnp.max(scores, axis=1, keepdims=True)) * (SCALE * LOG2_E))
        probs = shifted * (1.0 / jnp.sum(shifted, axis=1, keepdims=True))
        d_probs = d_probs_ref[h % 2, rows, :]
        delta = jnp.sum(d_probs * probs, axis=1, keepdims=True)
        probs_ref[h % 2, rows, :] = probs.astype(bf)
        d_scores_ref[h % 2, rows, :] = (probs * (d_probs - delta)).astype(bf)

    def behind(h):
        sides = [ref[:, head_cols(h)].T for ref in (q_ref, da_ref)]

        def terms(b, i, from_ref):
            def run():
                term = dot(sides[i], from_ref[h % 2, :, block_rows(b)], ((1,), (0,)))
                rows = slice(i * HD, (i + 1) * HD)
                dkv_ref[b, rows, :] = term if h == 0 else dkv_ref[b, rows, :] + term

            return run

        def rows_of(from_ref, other_ref, to_ref, scale):
            def run():
                product = dot(from_ref[h % 2], other_ref[...], ((1,), (0,)))
                to_ref[:, head_cols(h)] = (product * scale if scale else product).astype(bf)

            return run

        work = [terms(b, i, ref) for b in range(blocks) for i, ref in enumerate((d_scores_ref, probs_ref))]
        work.insert(4, rows_of(probs_ref, v_ref, attended_ref, None))
        work.insert(13, rows_of(d_scores_ref, k_ref, d_query_ref, SCALE))
        return work

    for run in ahead(0):
        run()
    for h in range(HEADS):
        beside = []
        if h + 1 < HEADS:
            beside += [(n / 16, run) for n, run in enumerate(ahead(h + 1))]
        if h > 0:
            beside += [(n / 18, run) for n, run in enumerate(behind(h - 1))]
        beside.sort(key=lambda entry: entry[0])
        steps = tokens // chunk
        for i in range(steps):
            softmax(h, i)
            for at, run in beside:
                if i <= at * steps < i + 1:
                    run()
    for run in behind(HEADS - 1):
        run()

    leaving = [
        pltpu.make_async_copy(ref, target, out_sems.at[i])
        for i, (ref, target) in enumerate(((d_query_ref, d_query_hbm), (attended_ref, attended_hbm)))
    ]
    for copy in leaving:
        copy.start()
    for i, scale in enumerate((SCALE, 1.0)):
        rows = pl.ds(i * HD, HD)
        top = jnp.abs(dkv_ref[0, rows, :])
        for b in range(1, blocks):
            top = jnp.maximum(top, jnp.abs(dkv_ref[b, rows, :]))
        power = exponent(top * scale)
        factor = jnp.exp2(-power) * scale
        for b in range(blocks):
            dkv_ref[b, rows, :] = dkv_ref[b, rows, :] * factor
            dkv_ref[b, pl.ds(2 * HD + 4 * i, 4), :] = jnp.broadcast_to(power, (4, tokens))
    for copy in leaving:
        copy.wait()


def attention(queries, d_att, keys_values):
    tokens, inner = queries.shape
    length = keys_values.shape[0]
    blocks = length // tokens
    anywhere = pl.BlockSpec(memory_space=pl.ANY)
    small, large = pltpu.VMEM((tokens, inner), jnp.bfloat16), pltpu.VMEM((length, HD), jnp.bfloat16)
    wide, half = pltpu.VMEM((2, tokens, length), jnp.float32), pltpu.VMEM((2, tokens, length), jnp.bfloat16)
    operands = [pltpu.with_memory_space_constraint(v, pltpu.HBM) for v in (queries, d_att, keys_values)]
    return pl.pallas_call(
        attention_kernel,
        in_specs=[anywhere] * 3,
        out_specs=[anywhere, anywhere, pl.BlockSpec(memory_space=pltpu.VMEM)],
        out_shape=[
            pltpu.HBM((tokens, inner), jnp.bfloat16),
            pltpu.HBM((tokens, inner), jnp.bfloat16),
            jax.ShapeDtypeStruct((blocks, 2 * HD + 8, tokens), jnp.float32),
        ],
        scratch_shapes=[small, small, large, large, small, small, wide, wide, half, half]
        + [pltpu.SemaphoreType.DMA((4,)), pltpu.SemaphoreType.DMA((2,))],
        compiler_params=pltpu.CompilerParams(vmem_limit_bytes=32 * MIB),
        cost_estimate=pl.CostEstimate(
            flops=12 * tokens * inner * length, bytes_accessed=4 << 20, transcendentals=tokens * HEADS * length
        ),
        name="attention",
    )(*operands)


def store_scaled(values, ref):
    power = exponent(values)
    ref[:-8, :] = values * jnp.exp2(-power)
    ref[-8:, :] = jnp.broadcast_to(power, (8, values.shape[1]))


def wide_kernel(*refs):
    keep_hbm, *send_refs = refs[16:19]
    sides_ref, factors_ref, keep_ref, in_sems, out_sems = refs[19:]
    rows, cols = keep_ref.shape[0], send_refs[0].shape[1]
    arriving = []
    for i in range(2):
        arriving.append([])
        for n in range(4):
            side, factor = refs[8 * i + n], refs[8 * i + 4 + n]
            copies = (
                pltpu.make_async_copy(side.at[pl.ds(0, 2 * rows), :], sides_ref.at[i, n], in_sems.at[i, n, 0]),
                pltpu.make_async_copy(factor, factors_ref.at[i, n], in_sems.at[i, n, 1]),
            )
            for copy in copies:
                copy.start()
            arriving[i].extend(copies)
    leaving = []
    for i in range(2):
        for copy in arriving[i]:
            copy.wait()
        product = None
        for n in range(4):
            term = dot(sides_ref[i, n], factors_ref[i, n], ((1,), (0,)))
            product = term if product is None else product + term
        here = (slice(None), pl.ds(i * cols, cols))
        keep_ref[:, i * cols : (i + 1) * cols] = product[:rows]
        leaving.append(pltpu.make_async_copy(keep_ref.at[here], keep_hbm.at[here], out_sems.at[i]))
        leaving[i].start()
        store_scaled(product[rows:], send_refs[i])
    for copy in leaving:
        copy.wait()


def wide_products(query, out):
    rows, tokens = out[0].shape[0] // 2, out[0].shape[1]
    cols = out[4].shape[1]
    anywhere, fast = pl.BlockSpec(memory_space=pl.ANY), pl.BlockSpec(memory_space=pltpu.VMEM)
    return pl.pallas_call(
        wide_kernel,
        in_specs=[anywhere] * 16,
        out_specs=[anywhere, fast, fast],
        out_shape=[
            pltpu.HBM((rows, 2 * cols), jnp.float32),
            jax.ShapeDtypeStruct((rows + 8, cols), jnp.float32),
            jax.ShapeDtypeStruct((rows + 8, cols), jnp.float32),
        ],
        scratch_shapes=[
            pltpu.VMEM((2, 4, 2 * rows, tokens), jnp.bfloat16),
            pltpu.VMEM((2, 4, tokens, cols), jnp.bfloat16),
            pltpu.VMEM((rows, 2 * cols), jnp.float32),
            pltpu.SemaphoreType.DMA((2, 4, 2)),
            pltpu.SemaphoreType.DMA((2,)),
        ],
        compiler_params=pltpu.CompilerParams(vmem_limit_bytes=20 * MIB),
        cost_estimate=pl.CostEstimate(flops=1 << 30, bytes_accessed=5 << 20, transcendentals=0),
        name="wide",
    )(*query, *out)


def narrow_kernel(mine_ref, theirs_ref, own_ref, other_ref, keep_ref, three_ref, one_ref, two_ref):
    product = None
    for side_ref, terms_ref in ((mine_ref, own_ref), (theirs_ref, other_ref)):
        side = side_ref[...]
        rest = terms_ref[...]
        for _ in range(2):
            piece = rest.astype(jnp.bfloat16)
            rest = rest - piece.astype(jnp.float32)
            term = dot(side, piece, ((1,), (1,)))
            product = term if product is None else product + term
    rows = keep_ref.shape[0]
    keep_ref[...] = product[:rows]
    powers = [jnp.broadcast_to(exponent(product[:, i * HD : (i + 1) * HD]), (8, HD)) for i in range(2)]
    power = jnp.concatenate(powers, axis=1)
    factor = jnp.exp2(-power[:1])
    for i, ref in enumerate((three_ref, one_ref, two_ref)):
        ref[:rows, :] = product[(i + 1) * rows : (i + 2) * rows] * factor
        ref[rows:, :] = power


def narrow_products(mine, theirs, own, other):
    rows = mine.shape[0] // 4
    cols = own.shape[0]
    sent = jax.ShapeDtypeStruct((rows + 8, cols), jnp.float32)
    return pl.pallas_call(
        narrow_kernel,
        out_shape=[pltpu.HBM((rows, cols), jnp.float32), sent, sent, sent],
        compiler_params=pltpu.CompilerParams(vmem_limit_bytes=16 * MIB),
        cost_estimate=pl.CostEstimate(flops=1, bytes_accessed=1, transcendentals=0),
        name="narrow",
    )(mine, theirs, own, other)


def own_terms_kernel(terms_ref, out_ref):
    for i in range(2):
        rows, powers = pl.ds(i * HD, HD), pl.ds(2 * HD + 4 * i, 1)
        total = unscaled(terms_ref, 0, rows, powers)
        for b in range(1, terms_ref.shape[0]):
            total = total + unscaled(terms_ref, b, rows, powers)
        out_ref[rows, :] = total


def own_terms(terms):
    return pl.pallas_call(
        own_terms_kernel,
        out_shape=jax.ShapeDtypeStruct((2 * HD, terms.shape[2]), jnp.float32),
        compiler_params=pltpu.CompilerParams(vmem_limit_bytes=8 * MIB),
        cost_estimate=pl.CostEstimate(flops=1, bytes_accessed=1, transcendentals=0),
        name="own_terms",
    )(terms)


def after_x_kernel(wide_ref, wide_got_ref, narrow_ref, narrow_got_ref, out_ref, total_ref):
    rows = wide_ref.shape[0]
    cols = 4 * HD
    scaled = lambda ref, i, here: ref[i, :rows, here] * jnp.exp2(ref[i, rows : rows + 1, here])
    for i, (first, width) in enumerate(((0, cols), (cols, cols), (2 * cols, HD), (2 * cols + HD, HD))):
        if i < 2:
            total = wide_ref[:, first : first + width] + scaled(wide_got_ref, i, pl.ds(0, cols))
        else:
            here = pl.ds(first - 2 * cols, HD)
            total = narrow_ref[:, here]
            for m in range(3):
                total = total + scaled(narrow_got_ref, m, here)
        top = exponent(total)
        total_ref[:, first : first + width] = total * jnp.exp2(-top)
        out_ref[:, 60 + i, :] = jnp.broadcast_to(top, (out_ref.shape[0], HD))
    for k in range(out_ref.shape[0]):
        y, z = k // 8, k % 8
        start = 48 * (z // 2) + 6 * (4 * (z % 2) + y)
        for j in range(10):
            out_ref[k, 6 * j : 6 * j + 6, :] = total_ref[start : start + 6, j * HD : (j + 1) * HD]


def after_x(wide, wide_got, narrow, narrow_got):
    rows, cols = wide.shape
    shape = (rows // 6, 64, HD)
    return pl.pallas_call(
        after_x_kernel,
        out_shape=jax.ShapeDtypeStruct(shape, jnp.float32),
        scratch_shapes=[pltpu.VMEM((rows, cols + narrow.shape[1]), jnp.float32)],
        compiler_params=pltpu.CompilerParams(vmem_limit_bytes=16 * MIB),
        name="after_x",
    )(wide, wide_got, narrow, narrow_got)


def last_sum_kernel(got_ref, query_ref, out_ref, key_ref, value_ref):
    first = 0
    for i, ref in enumerate((query_ref, out_ref, key_ref, value_ref)):
        tiles = ref.shape[1] // HD
        rows = pl.ds(first, 6 * tiles)
        total = unscaled(got_ref, 0, rows, pl.ds(60 + i, 1))
        for b in range(1, got_ref.shape[0]):
            total = total + unscaled(got_ref, b, rows, pl.ds(60 + i, 1))
        for j in range(tiles):
            ref[:, j * HD : (j + 1) * HD] = total[6 * j : 6 * j + 6]
        first += 6 * tiles


def last_sum(got):
    shape = lambda cols: jax.ShapeDtypeStruct((6, cols), jnp.float32)
    return pl.pallas_call(
        last_sum_kernel,
        out_shape=[shape(4 * HD), shape(4 * HD), shape(HD), shape(HD)],
        compiler_params=pltpu.CompilerParams(vmem_limit_bytes=8 * MIB),
        name="last_sum",
    )(got)


def local(normed, w_query, w_key, w_value, w_out, cotangent):
    hidden = normed[0]
    grads_in = cotangent[0]
    tokens = hidden.shape[0]
    bf, half = jnp.bfloat16, jnp.float16
    dp = lax.axis_index("dp")
    x, core = dp >> 3, dp & 1
    f32 = jnp.float32

    gathered = lax.all_to_all(project(hidden, w_key, w_value), AXES, 0, 0, axis_index_groups=SEQ_GROUPS, tiled=True)

    queries = dot(hidden, w_query, ((1,), (0,))).astype(bf)
    d_att = dot(grads_in, w_out, ((1,), (0,))).astype(bf)
    place_now = jnp.stack([x, core])
    h, h_core, *h_far = turn(place_now, hidden, ((0, (0, 3, 1, 2)), (1, (0, 3, 1, 2)), (0, (1, 2)), (1, (1, 2))))
    g, g_core, *g_far = turn(place_now, grads_in, ((0, (0, 1)), (1, (0, 1)), (0, (3, 2)), (1, (3, 2))))
    h_from = [exchange(h_far[0], 1 << 6), exchange(h_far[1], (1 << 6) | 8)]
    g_from = [exchange(g_far[0], 3 << 6), exchange(g_far[1], (3 << 6) | 8)]
    h_core, g_core = from_other_core(h_core), from_other_core(g_core)

    d_query, attended, terms = attention(queries, d_att, gathered.reshape(8 * tokens, 2 * HD))
    terms, d_query, attended, h_from, g_from, h_core, g_core = lax.optimization_barrier(
        (terms, d_query, attended, h_from, g_from, h_core, g_core)
    )
    terms = lax.all_to_all(terms.astype(half), AXES, 0, 0, axis_index_groups=SEQ_GROUPS, tiled=True)

    def factors(own, first):
        beside = exchange(own, first << 6)
        here = pltpu.with_memory_space_constraint(own, pltpu.HBM)
        return [here, from_other_core(own), beside, from_other_core(beside)]

    keep, *sent = wide_products(
        [h, h_core, *h_from] + factors(d_query, 1),
        [g, g_core, *g_from] + factors(attended, 3),
    )
    sent = [block.astype(half) for block in sent]
    wide_got = [exchange(block, m << 6) for m, block in zip((3, 1), sent)]
    branch = dot(attended, w_out, ((1,), (1,))).astype(bf)

    terms, _, branch = lax.optimization_barrier((terms, sent, branch))
    d_kv = own_terms(terms.astype(f32))
    narrow, *sent = narrow_products(h, h_core, d_kv, from_other_core(d_kv))
    narrow_got = [exchange(block.astype(half), m << 6) for m, block in zip((3, 1, 2), sent)]

    part = after_x(keep, jnp.stack(wide_got).astype(f32), narrow, jnp.stack(narrow_got).astype(f32))
    part = lax.all_to_all(part.astype(half), AXES, 0, 0, axis_index_groups=YZ_GROUPS, tiled=True)
    grad_query, grad_out, grad_key, grad_value = last_sum(part.astype(f32))
    return branch[None], grad_query, grad_key, grad_value, grad_out


def solution(mesh):
    return jax.shard_map(
        local,
        mesh=mesh,
        in_specs=(P("dp", "seq", None), P(), P(), P(), P(), P("dp", "seq", None)),
        out_specs=(
            P("dp", "seq", None),
            P(("dp", "seq"), None),
            P(("dp", "seq"), None),
            P(("dp", "seq"), None),
            P(("dp", "seq"), None),
        ),
        check_vma=False,
    )
```

```python
import functools

import jax
import jax.numpy as jnp
from jax import lax
from jax.experimental import pallas as pl
from jax.experimental.pallas import tpu as pltpu
from jax.sharding import PartitionSpec as P

HEADS = 4
HD = 128
SCALE = HD ** (-0.5)
LOG2_E = 1.4426950408889634
AXES = ("dp", "seq")
MIB = 1024 * 1024


def place(x, y, z, core):
    return x * 64 + (z >> 1) * 16 + core * 8 + (z & 1) * 4 + y


SEQ_GROUPS = [
    [place(x, y, 2 * z + low, c) for y in range(4) for low in range(2)] for x in range(4) for z in range(4) for c in range(2)
]
YZ_ORDER = [(y, (i + 2 * y) % 8) for i in range(8) for y in range(4)]
YZ_GROUPS = [[place(x, y, z, c) for y, z in YZ_ORDER] for x in range(4) for c in range(2)]


def dot(left, right, dims):
    return lax.dot_general(left, right, (dims, ((), ())), preferred_element_type=jnp.float32)


def exchange(value, mask):
    return lax.ppermute(value, AXES, [(i, i ^ mask) for i in range(256)])


def from_other_core(value):
    return exchange(value, 8)


def exponent(values):
    top = jnp.max(jnp.max(jnp.abs(values), axis=0, keepdims=True), axis=1, keepdims=True)
    return jnp.ceil(jnp.log2(jnp.maximum(top, 1e-30))) - 13.0


def unscaled(ref, block, values, exponents):
    return ref[block, values, :] * jnp.exp2(ref[block, exponents, :])


def project_kernel(hidden_ref, w_key_ref, w_value_ref, out_ref):
    hidden = hidden_ref[...]
    for i, ref in enumerate((w_key_ref, w_value_ref)):
        block = dot(hidden, ref[...], ((1,), (0,))).astype(jnp.bfloat16)
        for b in range(out_ref.shape[0]):
            out_ref[b, :, i * HD : (i + 1) * HD] = block


def project(hidden, w_key, w_value):
    hidden, w_key, w_value = (pltpu.with_memory_space_constraint(v, pltpu.HBM) for v in (hidden, w_key, w_value))
    return pl.pallas_call(
        project_kernel,
        out_shape=jax.ShapeDtypeStruct((8, hidden.shape[0], 2 * HD), jnp.bfloat16),
        compiler_params=pltpu.CompilerParams(vmem_limit_bytes=16 * MIB),
        name="project",
    )(hidden, w_key, w_value)


def turn_kernel(pieces, place_ref, side_ref, *refs):
    turned_ref = refs[-1]
    turned_ref[...] = side_ref[...].T
    for ref, (far, masks) in zip(refs, pieces):
        for i, mask in enumerate(masks):
            for z_hi in range(4):
                start = 384 * (place_ref[0] ^ mask) + 96 * z_hi + 48 * (place_ref[1] ^ far)
                first = 192 * i + 48 * z_hi
                ref[first : first + 48, :] = turned_ref[pl.ds(pl.multiple_of(start, 16), 48), :]


def turn(place, side, pieces):
    tokens, width = side.shape
    shapes = [(len(masks) * width // 8, tokens) for _, masks in pieces]
    return pl.pallas_call(
        functools.partial(turn_kernel, pieces),
        grid_spec=pltpu.PrefetchScalarGridSpec(
            num_scalar_prefetch=1,
            grid=(1,),
            in_specs=[pl.BlockSpec((tokens, width), lambda i, place: (0, 0))],
            out_specs=[pl.BlockSpec(shape, lambda i, place: (0, 0)) for shape in shapes],
            scratch_shapes=[pltpu.VMEM((width, tokens), side.dtype)],
        ),
        out_shape=[jax.ShapeDtypeStruct(shape, side.dtype) for shape in shapes],
        compiler_params=pltpu.CompilerParams(vmem_limit_bytes=12 * MIB),
        name="turn",
    )(place, side)


def attention_kernel(
    q_hbm, da_hbm, kv_hbm, d_query_hbm, attended_hbm, dkv_ref,
    q_ref, da_ref, k_ref, v_ref, d_query_ref, attended_ref, scores_ref, d_probs_ref, probs_ref, d_scores_ref,
    in_sems, out_sems,
):
    bf = jnp.bfloat16
    blocks, _, tokens = dkv_ref.shape
    chunk = 16
    head_cols = lambda h: slice(h * HD, (h + 1) * HD)
    block_rows = lambda b: slice(b * tokens, (b + 1) * tokens)
    arriving = [
        pltpu.make_async_copy(source, ref, in_sems.at[i])
        for i, (source, ref) in enumerate(
            (
                (kv_hbm.at[:, pl.ds(0, HD)], k_ref),
                (q_hbm, q_ref),
                (kv_hbm.at[:, pl.ds(HD, HD)], v_ref),
                (da_hbm, da_ref),
            )
        )
    ]
    for copy in arriving:
        copy.start()
    for copy in arriving:
        copy.wait()

    def ahead(h):
        def make(b, side_ref, other_ref, to_ref):
            def run():
                to_ref[h % 2, :, block_rows(b)] = dot(side_ref[:, head_cols(h)], other_ref[block_rows(b), :], ((1,), (1,)))

            return run

        return [
            make(b, *refs)
            for b in range(blocks)
            for refs in ((q_ref, k_ref, scores_ref), (da_ref, v_ref, d_probs_ref))
        ]

    def softmax(h, i):
        rows = slice(i * chunk, (i + 1) * chunk)
        scores = scores_ref[h % 2, rows, :]
        shifted = jnp.exp2((scores - jnp.max(scores, axis=1, keepdims=True)) * (SCALE * LOG2_E))
        probs = shifted * (1.0 / jnp.sum(shifted, axis=1, keepdims=True))
        d_probs = d_probs_ref[h % 2, rows, :]
        delta = jnp.sum(d_probs * probs, axis=1, keepdims=True)
        probs_ref[h % 2, rows, :] = probs.astype(bf)
        d_scores_ref[h % 2, rows, :] = (probs * (d_probs - delta)).astype(bf)

    def behind(h):
        sides = [ref[:, head_cols(h)].T for ref in (q_ref, da_ref)]

        def terms(b, i, from_ref):
            def run():
                term = dot(sides[i], from_ref[h % 2, :, block_rows(b)], ((1,), (0,)))
                rows = slice(i * HD, (i + 1) * HD)
                dkv_ref[b, rows, :] = term if h == 0 else dkv_ref[b, rows, :] + term

            return run

        def rows_of(from_ref, other_ref, to_ref, scale):
            def run():
                product = dot(from_ref[h % 2], other_ref[...], ((1,), (0,)))
                to_ref[:, head_cols(h)] = (product * scale if scale else product).astype(bf)

            return run

        work = [terms(b, i, ref) for b in range(blocks) for i, ref in enumerate((d_scores_ref, probs_ref))]
        work.insert(4, rows_of(probs_ref, v_ref, attended_ref, None))
        work.insert(13, rows_of(d_scores_ref, k_ref, d_query_ref, SCALE))
        return work

    for run in ahead(0):
        run()
    for h in range(HEADS):
        beside = []
        if h + 1 < HEADS:
            beside += [(n / 16, run) for n, run in enumerate(ahead(h + 1))]
        if h > 0:
            beside += [(n / 18, run) for n, run in enumerate(behind(h - 1))]
        beside.sort(key=lambda entry: entry[0])
        steps = tokens // chunk
        for i in range(steps):
            softmax(h, i)
            for at, run in beside:
                if i <= at * steps < i + 1:
                    run()
    for run in behind(HEADS - 1):
        run()

    leaving = [
        pltpu.make_async_copy(ref, target, out_sems.at[i])
        for i, (ref, target) in enumerate(((d_query_ref, d_query_hbm), (attended_ref, attended_hbm)))
    ]
    for copy in leaving:
        copy.start()
    for i, scale in enumerate((SCALE, 1.0)):
        rows = pl.ds(i * HD, HD)
        top = jnp.abs(dkv_ref[0, rows, :])
        for b in range(1, blocks):
            top = jnp.maximum(top, jnp.abs(dkv_ref[b, rows, :]))
        power = exponent(top * scale)
        factor = jnp.exp2(-power) * scale
        for b in range(blocks):
            dkv_ref[b, rows, :] = dkv_ref[b, rows, :] * factor
            dkv_ref[b, pl.ds(2 * HD + 4 * i, 4), :] = jnp.broadcast_to(power, (4, tokens))
    for copy in leaving:
        copy.wait()


def attention(queries, d_att, keys_values):
    tokens, inner = queries.shape
    length = keys_values.shape[0]
    blocks = length // tokens
    anywhere = pl.BlockSpec(memory_space=pl.ANY)
    small, large = pltpu.VMEM((tokens, inner), jnp.bfloat16), pltpu.VMEM((length, HD), jnp.bfloat16)
    wide, half = pltpu.VMEM((2, tokens, length), jnp.float32), pltpu.VMEM((2, tokens, length), jnp.bfloat16)
    operands = [pltpu.with_memory_space_constraint(v, pltpu.HBM) for v in (queries, d_att, keys_values)]
    return pl.pallas_call(
        attention_kernel,
        in_specs=[anywhere] * 3,
        out_specs=[anywhere, anywhere, pl.BlockSpec(memory_space=pltpu.VMEM)],
        out_shape=[
            pltpu.HBM((tokens, inner), jnp.bfloat16),
            pltpu.HBM((tokens, inner), jnp.bfloat16),
            jax.ShapeDtypeStruct((blocks, 2 * HD + 8, tokens), jnp.float32),
        ],
        scratch_shapes=[small, small, large, large, small, small, wide, wide, half, half]
        + [pltpu.SemaphoreType.DMA((4,)), pltpu.SemaphoreType.DMA((2,))],
        compiler_params=pltpu.CompilerParams(vmem_limit_bytes=32 * MIB),
        cost_estimate=pl.CostEstimate(
            flops=12 * tokens * inner * length, bytes_accessed=4 << 20, transcendentals=tokens * HEADS * length
        ),
        name="attention",
    )(*operands)


def store_scaled(values, ref):
    power = exponent(values)
    ref[:-8, :] = values * jnp.exp2(-power)
    ref[-8:, :] = jnp.broadcast_to(power, (8, values.shape[1]))


def wide_kernel(*refs):
    keep_hbm, *send_refs = refs[16:19]
    sides_ref, factors_ref, keep_ref, in_sems, out_sems = refs[19:]
    rows, cols = keep_ref.shape[0], send_refs[0].shape[1]
    arriving = []
    for i in range(2):
        arriving.append([])
        for n in range(4):
            side, factor = refs[8 * i + n], refs[8 * i + 4 + n]
            copies = (
                pltpu.make_async_copy(side.at[pl.ds(0, 2 * rows), :], sides_ref.at[i, n], in_sems.at[i, n, 0]),
                pltpu.make_async_copy(factor, factors_ref.at[i, n], in_sems.at[i, n, 1]),
            )
            for copy in copies:
                copy.start()
            arriving[i].extend(copies)
    leaving = []
    for i in range(2):
        for copy in arriving[i]:
            copy.wait()
        product = None
        for n in range(4):
            term = dot(sides_ref[i, n], factors_ref[i, n], ((1,), (0,)))
            product = term if product is None else product + term
        here = (slice(None), pl.ds(i * cols, cols))
        keep_ref[:, i * cols : (i + 1) * cols] = product[:rows]
        leaving.append(pltpu.make_async_copy(keep_ref.at[here], keep_hbm.at[here], out_sems.at[i]))
        leaving[i].start()
        store_scaled(product[rows:], send_refs[i])
    for copy in leaving:
        copy.wait()


def wide_products(query, out):
    rows, tokens = out[0].shape[0] // 2, out[0].shape[1]
    cols = out[4].shape[1]
    anywhere, fast = pl.BlockSpec(memory_space=pl.ANY), pl.BlockSpec(memory_space=pltpu.VMEM)
    return pl.pallas_call(
        wide_kernel,
        in_specs=[anywhere] * 16,
        out_specs=[anywhere, fast, fast],
        out_shape=[
            pltpu.HBM((rows, 2 * cols), jnp.float32),
            jax.ShapeDtypeStruct((rows + 8, cols), jnp.float32),
            jax.ShapeDtypeStruct((rows + 8, cols), jnp.float32),
        ],
        scratch_shapes=[
            pltpu.VMEM((2, 4, 2 * rows, tokens), jnp.bfloat16),
            pltpu.VMEM((2, 4, tokens, cols), jnp.bfloat16),
            pltpu.VMEM((rows, 2 * cols), jnp.float32),
            pltpu.SemaphoreType.DMA((2, 4, 2)),
            pltpu.SemaphoreType.DMA((2,)),
        ],
        compiler_params=pltpu.CompilerParams(vmem_limit_bytes=20 * MIB),
        cost_estimate=pl.CostEstimate(flops=1 << 30, bytes_accessed=5 << 20, transcendentals=0),
        name="wide",
    )(*query, *out)


def narrow_kernel(mine_ref, theirs_ref, own_ref, other_ref, keep_ref, three_ref, one_ref, two_ref):
    product = None
    for side_ref, terms_ref in ((mine_ref, own_ref), (theirs_ref, other_ref)):
        side = side_ref[...]
        rest = terms_ref[...]
        for _ in range(2):
            piece = rest.astype(jnp.bfloat16)
            rest = rest - piece.astype(jnp.float32)
            term = dot(side, piece, ((1,), (1,)))
            product = term if product is None else product + term
    rows = keep_ref.shape[0]
    keep_ref[...] = product[:rows]
    powers = [jnp.broadcast_to(exponent(product[:, i * HD : (i + 1) * HD]), (8, HD)) for i in range(2)]
    power = jnp.concatenate(powers, axis=1)
    factor = jnp.exp2(-power[:1])
    for i, ref in enumerate((three_ref, one_ref, two_ref)):
        ref[:rows, :] = product[(i + 1) * rows : (i + 2) * rows] * factor
        ref[rows:, :] = power


def narrow_products(mine, theirs, own, other):
    rows = mine.shape[0] // 4
    cols = own.shape[0]
    sent = jax.ShapeDtypeStruct((rows + 8, cols), jnp.float32)
    return pl.pallas_call(
        narrow_kernel,
        out_shape=[pltpu.HBM((rows, cols), jnp.float32), sent, sent, sent],
        compiler_params=pltpu.CompilerParams(vmem_limit_bytes=16 * MIB),
        cost_estimate=pl.CostEstimate(flops=1, bytes_accessed=1, transcendentals=0),
        name="narrow",
    )(mine, theirs, own, other)


def own_terms_kernel(terms_ref, out_ref):
    for i in range(2):
        rows, powers = pl.ds(i * HD, HD), pl.ds(2 * HD + 4 * i, 1)
        total = unscaled(terms_ref, 0, rows, powers)
        for b in range(1, terms_ref.shape[0]):
            total = total + unscaled(terms_ref, b, rows, powers)
        out_ref[rows, :] = total


def own_terms(terms):
    return pl.pallas_call(
        own_terms_kernel,
        out_shape=jax.ShapeDtypeStruct((2 * HD, terms.shape[2]), jnp.float32),
        compiler_params=pltpu.CompilerParams(vmem_limit_bytes=8 * MIB),
        cost_estimate=pl.CostEstimate(flops=1, bytes_accessed=1, transcendentals=0),
        name="own_terms",
    )(terms)


def after_x_kernel(wide_ref, wide_got_ref, narrow_ref, narrow_got_ref, out_ref, total_ref):
    rows = wide_ref.shape[0]
    cols = 4 * HD
    scaled = lambda ref, i, here: ref[i, :rows, here] * jnp.exp2(ref[i, rows : rows + 1, here])
    for i, (first, width) in enumerate(((0, cols), (cols, cols), (2 * cols, HD), (2 * cols + HD, HD))):
        if i < 2:
            total = wide_ref[:, first : first + width] + scaled(wide_got_ref, i, pl.ds(0, cols))
        else:
            here = pl.ds(first - 2 * cols, HD)
            total = narrow_ref[:, here]
            for m in range(3):
                total = total + scaled(narrow_got_ref, m, here)
        top = exponent(total)
        total_ref[:, first : first + width] = total * jnp.exp2(-top)
        out_ref[:, 60 + i, :] = jnp.broadcast_to(top, (out_ref.shape[0], HD))
    for k, (y, z) in enumerate(YZ_ORDER):
        start = 48 * (z // 2) + 6 * (4 * (z % 2) + y)
        for j in range(10):
            out_ref[k, 6 * j : 6 * j + 6, :] = total_ref[start : start + 6, j * HD : (j + 1) * HD]


def after_x(wide, wide_got, narrow, narrow_got):
    rows, cols = wide.shape
    shape = (rows // 6, 64, HD)
    return pl.pallas_call(
        after_x_kernel,
        out_shape=jax.ShapeDtypeStruct(shape, jnp.float32),
        scratch_shapes=[pltpu.VMEM((rows, cols + narrow.shape[1]), jnp.float32)],
        compiler_params=pltpu.CompilerParams(vmem_limit_bytes=16 * MIB),
        name="after_x",
    )(wide, wide_got, narrow, narrow_got)


def last_sum_kernel(got_ref, query_ref, out_ref, key_ref, value_ref):
    first = 0
    for i, ref in enumerate((query_ref, out_ref, key_ref, value_ref)):
        tiles = ref.shape[1] // HD
        rows = pl.ds(first, 6 * tiles)
        total = unscaled(got_ref, 0, rows, pl.ds(60 + i, 1))
        for b in range(1, got_ref.shape[0]):
            total = total + unscaled(got_ref, b, rows, pl.ds(60 + i, 1))
        for j in range(tiles):
            ref[:, j * HD : (j + 1) * HD] = total[6 * j : 6 * j + 6]
        first += 6 * tiles


def last_sum(got):
    shape = lambda cols: jax.ShapeDtypeStruct((6, cols), jnp.float32)
    return pl.pallas_call(
        last_sum_kernel,
        out_shape=[shape(4 * HD), shape(4 * HD), shape(HD), shape(HD)],
        compiler_params=pltpu.CompilerParams(vmem_limit_bytes=8 * MIB),
        name="last_sum",
    )(got)


def local(normed, w_query, w_key, w_value, w_out, cotangent):
    hidden = normed[0]
    grads_in = cotangent[0]
    tokens = hidden.shape[0]
    bf, half = jnp.bfloat16, jnp.float16
    dp = lax.axis_index("dp")
    x, core = dp >> 3, dp & 1
    f32 = jnp.float32

    gathered = lax.all_to_all(project(hidden, w_key, w_value), AXES, 0, 0, axis_index_groups=SEQ_GROUPS, tiled=True)

    queries = dot(hidden, w_query, ((1,), (0,))).astype(bf)
    d_att = dot(grads_in, w_out, ((1,), (0,))).astype(bf)
    place_now = jnp.stack([x, core])
    h, h_core, *h_far = turn(place_now, hidden, ((0, (0, 3, 1, 2)), (1, (0, 3, 1, 2)), (0, (1, 2)), (1, (1, 2))))
    g, g_core, *g_far = turn(place_now, grads_in, ((0, (0, 1)), (1, (0, 1)), (0, (3, 2)), (1, (3, 2))))
    h_from = [exchange(h_far[0], 1 << 6), exchange(h_far[1], (1 << 6) | 8)]
    g_from = [exchange(g_far[0], 3 << 6), exchange(g_far[1], (3 << 6) | 8)]
    h_core, g_core = from_other_core(h_core), from_other_core(g_core)

    d_query, attended, terms = attention(queries, d_att, gathered.reshape(8 * tokens, 2 * HD))
    terms, d_query, attended, h_from, g_from, h_core, g_core = lax.optimization_barrier(
        (terms, d_query, attended, h_from, g_from, h_core, g_core)
    )
    terms = lax.all_to_all(terms.astype(half), AXES, 0, 0, axis_index_groups=SEQ_GROUPS, tiled=True)

    def factors(own, first):
        beside = exchange(own, first << 6)
        here = pltpu.with_memory_space_constraint(own, pltpu.HBM)
        return [here, from_other_core(own), beside, from_other_core(beside)]

    keep, *sent = wide_products(
        [h, h_core, *h_from] + factors(d_query, 1),
        [g, g_core, *g_from] + factors(attended, 3),
    )
    sent = [block.astype(half) for block in sent]
    wide_got = [exchange(block, m << 6) for m, block in zip((3, 1), sent)]
    branch = dot(attended, w_out, ((1,), (1,))).astype(bf)

    terms, _ = lax.optimization_barrier((terms, sent))
    d_kv = own_terms(terms.astype(f32))
    narrow, *sent = narrow_products(h, h_core, d_kv, from_other_core(d_kv))
    narrow_got = [exchange(block.astype(half), m << 6) for m, block in zip((3, 1, 2), sent)]

    part = after_x(keep, jnp.stack(wide_got).astype(f32), narrow, jnp.stack(narrow_got).astype(f32))
    part = lax.all_to_all(part.astype(half), AXES, 0, 0, axis_index_groups=YZ_GROUPS, tiled=True)
    grad_query, grad_out, grad_key, grad_value = last_sum(part.astype(f32))
    return branch[None], grad_query, grad_key, grad_value, grad_out


def solution(mesh):
    return jax.shard_map(
        local,
        mesh=mesh,
        in_specs=(P("dp", "seq", None), P(), P(), P(), P(), P("dp", "seq", None)),
        out_specs=(
            P("dp", "seq", None),
            P(("dp", "seq"), None),
            P(("dp", "seq"), None),
            P(("dp", "seq"), None),
            P(("dp", "seq"), None),
        ),
        check_vma=False,
    )
```

```python
import functools

import jax
import jax.numpy as jnp
from jax import lax
from jax.experimental import pallas as pl
from jax.experimental.pallas import tpu as pltpu
from jax.sharding import PartitionSpec as P

HEADS = 4
HD = 128
SCALE = HD ** (-0.5)
LOG2_E = 1.4426950408889634
AXES = ("dp", "seq")
MIB = 1024 * 1024


def place(x, y, z, core):
    return x * 64 + (z >> 1) * 16 + core * 8 + (z & 1) * 4 + y


SEQ_GROUPS = [
    [place(x, y, 2 * z + low, c) for y in range(4) for low in range(2)] for x in range(4) for z in range(4) for c in range(2)
]
YZ_ORDER = [(y, (i + 2 * y) % 8) for i in range(8) for y in range(4)]
YZ_GROUPS = [[place(x, y, z, c) for y, z in YZ_ORDER] for x in range(4) for c in range(2)]


def dot(left, right, dims):
    return lax.dot_general(left, right, (dims, ((), ())), preferred_element_type=jnp.float32)


def exchange(value, mask):
    return lax.ppermute(value, AXES, [(i, i ^ mask) for i in range(256)])


def from_other_core(value):
    return exchange(value, 8)


def exponent(values):
    top = jnp.max(jnp.max(jnp.abs(values), axis=0, keepdims=True), axis=1, keepdims=True)
    return jnp.ceil(jnp.log2(jnp.maximum(top, 1e-30))) - 13.0


def unscaled(ref, block, values, exponents):
    return ref[block, values, :] * jnp.exp2(ref[block, exponents, :])


def project_kernel(hidden_ref, w_key_ref, w_value_ref, out_ref):
    hidden = hidden_ref[...]
    for i, ref in enumerate((w_key_ref, w_value_ref)):
        block = dot(hidden, ref[...], ((1,), (0,))).astype(jnp.bfloat16)
        for b in range(out_ref.shape[0]):
            out_ref[b, :, i * HD : (i + 1) * HD] = block


def project(hidden, w_key, w_value):
    hidden, w_key, w_value = (pltpu.with_memory_space_constraint(v, pltpu.HBM) for v in (hidden, w_key, w_value))
    return pl.pallas_call(
        project_kernel,
        out_shape=jax.ShapeDtypeStruct((8, hidden.shape[0], 2 * HD), jnp.bfloat16),
        compiler_params=pltpu.CompilerParams(vmem_limit_bytes=16 * MIB),
        name="project",
    )(hidden, w_key, w_value)


def turn_kernel(pieces, place_ref, side_ref, *refs):
    turned_ref = refs[-1]
    turned_ref[...] = side_ref[...].T
    for ref, (far, masks) in zip(refs, pieces):
        for i, mask in enumerate(masks):
            for z_hi in range(4):
                start = 384 * (place_ref[0] ^ mask) + 96 * z_hi + 48 * (place_ref[1] ^ far)
                first = 192 * i + 48 * z_hi
                ref[first : first + 48, :] = turned_ref[pl.ds(pl.multiple_of(start, 16), 48), :]


def turn(place, side, pieces):
    tokens, width = side.shape
    shapes = [(len(masks) * width // 8, tokens) for _, masks in pieces]
    return pl.pallas_call(
        functools.partial(turn_kernel, pieces),
        grid_spec=pltpu.PrefetchScalarGridSpec(
            num_scalar_prefetch=1,
            grid=(1,),
            in_specs=[pl.BlockSpec((tokens, width), lambda i, place: (0, 0))],
            out_specs=[pl.BlockSpec(shape, lambda i, place: (0, 0)) for shape in shapes],
            scratch_shapes=[pltpu.VMEM((width, tokens), side.dtype)],
        ),
        out_shape=[jax.ShapeDtypeStruct(shape, side.dtype) for shape in shapes],
        compiler_params=pltpu.CompilerParams(vmem_limit_bytes=12 * MIB),
        name="turn",
    )(place, side)


def attention_kernel(
    q_hbm, da_hbm, kv_hbm, d_query_hbm, attended_hbm, dkv_ref,
    q_ref, da_ref, k_ref, v_ref, d_query_ref, attended_ref, scores_ref, d_probs_ref, probs_ref, d_scores_ref,
    in_sems, out_sems,
):
    bf = jnp.bfloat16
    blocks, _, tokens = dkv_ref.shape
    chunk = 16
    head_cols = lambda h: slice(h * HD, (h + 1) * HD)
    block_rows = lambda b: slice(b * tokens, (b + 1) * tokens)
    arriving = [
        pltpu.make_async_copy(source, ref, in_sems.at[i])
        for i, (source, ref) in enumerate(
            (
                (kv_hbm.at[:, pl.ds(0, HD)], k_ref),
                (q_hbm, q_ref),
                (kv_hbm.at[:, pl.ds(HD, HD)], v_ref),
                (da_hbm, da_ref),
            )
        )
    ]
    for copy in arriving:
        copy.start()
    for copy in arriving:
        copy.wait()

    def ahead(h):
        def make(b, side_ref, other_ref, to_ref):
            def run():
                to_ref[h % 2, :, block_rows(b)] = dot(side_ref[:, head_cols(h)], other_ref[block_rows(b), :], ((1,), (1,)))

            return run

        return [
            make(b, *refs)
            for b in range(blocks)
            for refs in ((q_ref, k_ref, scores_ref), (da_ref, v_ref, d_probs_ref))
        ]

    def softmax(h, i):
        rows = slice(i * chunk, (i + 1) * chunk)
        scores = scores_ref[h % 2, rows, :]
        shifted = jnp.exp2((scores - jnp.max(scores, axis=1, keepdims=True)) * (SCALE * LOG2_E))
        probs = shifted * (1.0 / jnp.sum(shifted, axis=1, keepdims=True))
        d_probs = d_probs_ref[h % 2, rows, :]
        delta = jnp.sum(d_probs * probs, axis=1, keepdims=True)
        probs_ref[h % 2, rows, :] = probs.astype(bf)
        d_scores_ref[h % 2, rows, :] = (probs * (d_probs - delta)).astype(bf)

    def behind(h):
        sides = [ref[:, head_cols(h)].T for ref in (q_ref, da_ref)]

        def terms(b, i, from_ref):
            def run():
                term = dot(sides[i], from_ref[h % 2, :, block_rows(b)], ((1,), (0,)))
                rows = slice(i * HD, (i + 1) * HD)
                dkv_ref[b, rows, :] = term if h == 0 else dkv_ref[b, rows, :] + term

            return run

        def rows_of(from_ref, other_ref, to_ref, scale):
            def run():
                product = dot(from_ref[h % 2], other_ref[...], ((1,), (0,)))
                to_ref[:, head_cols(h)] = (product * scale if scale else product).astype(bf)

            return run

        work = [terms(b, i, ref) for b in range(blocks) for i, ref in enumerate((d_scores_ref, probs_ref))]
        work.insert(4, rows_of(probs_ref, v_ref, attended_ref, None))
        work.insert(13, rows_of(d_scores_ref, k_ref, d_query_ref, SCALE))
        return work

    for run in ahead(0):
        run()
    for h in range(HEADS):
        beside = []
        if h + 1 < HEADS:
            beside += [(n / 16, run) for n, run in enumerate(ahead(h + 1))]
        if h > 0:
            beside += [(n / 18, run) for n, run in enumerate(behind(h - 1))]
        beside.sort(key=lambda entry: entry[0])
        steps = tokens // chunk
        for i in range(steps):
            softmax(h, i)
            for at, run in beside:
                if i <= at * steps < i + 1:
                    run()
    for run in behind(HEADS - 1):
        run()

    leaving = [
        pltpu.make_async_copy(ref, target, out_sems.at[i])
        for i, (ref, target) in enumerate(((d_query_ref, d_query_hbm), (attended_ref, attended_hbm)))
    ]
    for copy in leaving:
        copy.start()
    for i, scale in enumerate((SCALE, 1.0)):
        rows = pl.ds(i * HD, HD)
        top = jnp.abs(dkv_ref[0, rows, :])
        for b in range(1, blocks):
            top = jnp.maximum(top, jnp.abs(dkv_ref[b, rows, :]))
        power = exponent(top * scale)
        factor = jnp.exp2(-power) * scale
        for b in range(blocks):
            dkv_ref[b, rows, :] = dkv_ref[b, rows, :] * factor
            dkv_ref[b, pl.ds(2 * HD + 4 * i, 4), :] = jnp.broadcast_to(power, (4, tokens))
    for copy in leaving:
        copy.wait()


def attention(queries, d_att, keys_values):
    tokens, inner = queries.shape
    length = keys_values.shape[0]
    blocks = length // tokens
    anywhere = pl.BlockSpec(memory_space=pl.ANY)
    small, large = pltpu.VMEM((tokens, inner), jnp.bfloat16), pltpu.VMEM((length, HD), jnp.bfloat16)
    wide, half = pltpu.VMEM((2, tokens, length), jnp.float32), pltpu.VMEM((2, tokens, length), jnp.bfloat16)
    operands = [pltpu.with_memory_space_constraint(v, pltpu.HBM) for v in (queries, d_att, keys_values)]
    return pl.pallas_call(
        attention_kernel,
        in_specs=[anywhere] * 3,
        out_specs=[anywhere, anywhere, pl.BlockSpec(memory_space=pltpu.VMEM)],
        out_shape=[
            pltpu.HBM((tokens, inner), jnp.bfloat16),
            pltpu.HBM((tokens, inner), jnp.bfloat16),
            jax.ShapeDtypeStruct((blocks, 2 * HD + 8, tokens), jnp.float32),
        ],
        scratch_shapes=[small, small, large, large, small, small, wide, wide, half, half]
        + [pltpu.SemaphoreType.DMA((4,)), pltpu.SemaphoreType.DMA((2,))],
        compiler_params=pltpu.CompilerParams(vmem_limit_bytes=32 * MIB),
        cost_estimate=pl.CostEstimate(
            flops=12 * tokens * inner * length, bytes_accessed=4 << 20, transcendentals=tokens * HEADS * length
        ),
        name="attention",
    )(*operands)


def store_scaled(values, ref):
    power = exponent(values)
    ref[:-8, :] = values * jnp.exp2(-power)
    ref[-8:, :] = jnp.broadcast_to(power, (8, values.shape[1]))


def wide_kernel(*refs):
    keep_hbm, *send_refs = refs[16:19]
    sides_ref, factors_ref, keep_ref, in_sems, out_sems = refs[19:]
    rows, cols = keep_ref.shape[0], send_refs[0].shape[1]
    arriving = []
    for i in range(2):
        arriving.append([])
        for n in range(4):
            side, factor = refs[8 * i + n], refs[8 * i + 4 + n]
            copies = (
                pltpu.make_async_copy(side.at[pl.ds(0, 2 * rows), :], sides_ref.at[i, n], in_sems.at[i, n, 0]),
                pltpu.make_async_copy(factor, factors_ref.at[i, n], in_sems.at[i, n, 1]),
            )
            for copy in copies:
                copy.start()
            arriving[i].extend(copies)
    leaving = []
    for i in range(2):
        for copy in arriving[i]:
            copy.wait()
        product = None
        for n in range(4):
            term = dot(sides_ref[i, n], factors_ref[i, n], ((1,), (0,)))
            product = term if product is None else product + term
        here = (slice(None), pl.ds(i * cols, cols))
        keep_ref[:, i * cols : (i + 1) * cols] = product[:rows]
        leaving.append(pltpu.make_async_copy(keep_ref.at[here], keep_hbm.at[here], out_sems.at[i]))
        leaving[i].start()
        store_scaled(product[rows:], send_refs[i])
    for copy in leaving:
        copy.wait()


def wide_products(query, out):
    rows, tokens = out[0].shape[0] // 2, out[0].shape[1]
    cols = out[4].shape[1]
    anywhere, fast = pl.BlockSpec(memory_space=pl.ANY), pl.BlockSpec(memory_space=pltpu.VMEM)
    return pl.pallas_call(
        wide_kernel,
        in_specs=[anywhere] * 16,
        out_specs=[anywhere, fast, fast],
        out_shape=[
            pltpu.HBM((rows, 2 * cols), jnp.float32),
            jax.ShapeDtypeStruct((rows + 8, cols), jnp.float32),
            jax.ShapeDtypeStruct((rows + 8, cols), jnp.float32),
        ],
        scratch_shapes=[
            pltpu.VMEM((2, 4, 2 * rows, tokens), jnp.bfloat16),
            pltpu.VMEM((2, 4, tokens, cols), jnp.bfloat16),
            pltpu.VMEM((rows, 2 * cols), jnp.float32),
            pltpu.SemaphoreType.DMA((2, 4, 2)),
            pltpu.SemaphoreType.DMA((2,)),
        ],
        compiler_params=pltpu.CompilerParams(vmem_limit_bytes=20 * MIB),
        cost_estimate=pl.CostEstimate(flops=1 << 30, bytes_accessed=5 << 20, transcendentals=0),
        name="wide",
    )(*query, *out)


def narrow_kernel(mine_ref, theirs_ref, own_ref, other_ref, keep_ref, three_ref, one_ref, two_ref):
    product = None
    for side_ref, terms_ref in ((mine_ref, own_ref), (theirs_ref, other_ref)):
        side = side_ref[...]
        rest = terms_ref[...]
        for _ in range(2):
            piece = rest.astype(jnp.bfloat16)
            rest = rest - piece.astype(jnp.float32)
            term = dot(side, piece, ((1,), (1,)))
            product = term if product is None else product + term
    rows = keep_ref.shape[0]
    keep_ref[...] = product[:rows]
    powers = [jnp.broadcast_to(exponent(product[:, i * HD : (i + 1) * HD]), (8, HD)) for i in range(2)]
    power = jnp.concatenate(powers, axis=1)
    factor = jnp.exp2(-power[:1])
    for i, ref in enumerate((three_ref, one_ref, two_ref)):
        ref[:rows, :] = product[(i + 1) * rows : (i + 2) * rows] * factor
        ref[rows:, :] = power


def narrow_products(mine, theirs, own, other):
    rows = mine.shape[0] // 4
    cols = own.shape[0]
    sent = jax.ShapeDtypeStruct((rows + 8, cols), jnp.float32)
    return pl.pallas_call(
        narrow_kernel,
        out_shape=[pltpu.HBM((rows, cols), jnp.float32), sent, sent, sent],
        compiler_params=pltpu.CompilerParams(vmem_limit_bytes=16 * MIB),
        cost_estimate=pl.CostEstimate(flops=1, bytes_accessed=1, transcendentals=0),
        name="narrow",
    )(mine, theirs, own, other)


def own_terms_kernel(terms_ref, out_ref):
    for i in range(2):
        rows, powers = pl.ds(i * HD, HD), pl.ds(2 * HD + 4 * i, 1)
        total = unscaled(terms_ref, 0, rows, powers)
        for b in range(1, terms_ref.shape[0]):
            total = total + unscaled(terms_ref, b, rows, powers)
        out_ref[rows, :] = total


def own_terms(terms):
    return pl.pallas_call(
        own_terms_kernel,
        out_shape=jax.ShapeDtypeStruct((2 * HD, terms.shape[2]), jnp.float32),
        compiler_params=pltpu.CompilerParams(vmem_limit_bytes=8 * MIB),
        cost_estimate=pl.CostEstimate(flops=1, bytes_accessed=1, transcendentals=0),
        name="own_terms",
    )(terms)


def after_x_kernel(wide_ref, wide_got_ref, narrow_ref, narrow_got_ref, out_ref, total_ref):
    rows = wide_ref.shape[0]
    cols = 4 * HD
    scaled = lambda ref, i, here: ref[i, :rows, here] * jnp.exp2(ref[i, rows : rows + 1, here])
    for i, (first, width) in enumerate(((0, cols), (cols, cols), (2 * cols, HD), (2 * cols + HD, HD))):
        if i < 2:
            total = wide_ref[:, first : first + width] + scaled(wide_got_ref, i, pl.ds(0, cols))
        else:
            here = pl.ds(first - 2 * cols, HD)
            total = narrow_ref[:, here]
            for m in range(3):
                total = total + scaled(narrow_got_ref, m, here)
        top = exponent(total)
        total_ref[:, first : first + width] = total * jnp.exp2(-top)
        out_ref[:, 60 + i, :] = jnp.broadcast_to(top, (out_ref.shape[0], HD))
    for k, (y, z) in enumerate(YZ_ORDER):
        start = 48 * (z // 2) + 6 * (4 * (z % 2) + y)
        for j in range(10):
            out_ref[k, 6 * j : 6 * j + 6, :] = total_ref[start : start + 6, j * HD : (j + 1) * HD]


def after_x(wide, wide_got, narrow, narrow_got):
    rows, cols = wide.shape
    shape = (rows // 6, 64, HD)
    return pl.pallas_call(
        after_x_kernel,
        out_shape=jax.ShapeDtypeStruct(shape, jnp.float32),
        scratch_shapes=[pltpu.VMEM((rows, cols + narrow.shape[1]), jnp.float32)],
        compiler_params=pltpu.CompilerParams(vmem_limit_bytes=16 * MIB),
        name="after_x",
    )(wide, wide_got, narrow, narrow_got)


def last_sum_kernel(got_ref, query_ref, out_ref, key_ref, value_ref):
    first = 0
    for i, ref in enumerate((query_ref, out_ref, key_ref, value_ref)):
        tiles = ref.shape[1] // HD
        rows = pl.ds(first, 6 * tiles)
        total = unscaled(got_ref, 0, rows, pl.ds(60 + i, 1))
        for b in range(1, got_ref.shape[0]):
            total = total + unscaled(got_ref, b, rows, pl.ds(60 + i, 1))
        for j in range(tiles):
            ref[:, j * HD : (j + 1) * HD] = total[6 * j : 6 * j + 6]
        first += 6 * tiles


def last_sum(got):
    shape = lambda cols: jax.ShapeDtypeStruct((6, cols), jnp.float32)
    return pl.pallas_call(
        last_sum_kernel,
        out_shape=[shape(4 * HD), shape(4 * HD), shape(HD), shape(HD)],
        compiler_params=pltpu.CompilerParams(vmem_limit_bytes=8 * MIB),
        name="last_sum",
    )(got)


def local(normed, w_query, w_key, w_value, w_out, cotangent):
    hidden = normed[0]
    grads_in = cotangent[0]
    tokens = hidden.shape[0]
    bf, half = jnp.bfloat16, jnp.float16
    dp = lax.axis_index("dp")
    x, core = dp >> 3, dp & 1
    f32 = jnp.float32

    gathered = lax.all_to_all(project(hidden, w_key, w_value), AXES, 0, 0, axis_index_groups=SEQ_GROUPS, tiled=True)

    queries = dot(hidden, w_query, ((1,), (0,))).astype(bf)
    d_att = dot(grads_in, w_out, ((1,), (0,))).astype(bf)
    place_now = jnp.stack([x, core])
    h, h_core, *h_far = turn(place_now, hidden, ((0, (0, 3, 1, 2)), (1, (0, 3, 1, 2)), (0, (1, 2)), (1, (1, 2))))
    g, g_core, *g_far = turn(place_now, grads_in, ((0, (0, 1)), (1, (0, 1)), (0, (3, 2)), (1, (3, 2))))
    h_from = [exchange(h_far[0], 1 << 6), exchange(h_far[1], (1 << 6) | 8)]
    g_from = [exchange(g_far[0], 3 << 6), exchange(g_far[1], (3 << 6) | 8)]
    h_core, g_core = from_other_core(h_core), from_other_core(g_core)

    d_query, attended, terms = attention(queries, d_att, gathered.reshape(8 * tokens, 2 * HD))
    terms, d_query, attended, h_from, g_from, h_core, g_core = lax.optimization_barrier(
        (terms, d_query, attended, h_from, g_from, h_core, g_core)
    )
    terms = lax.all_to_all(terms.astype(half), AXES, 0, 0, axis_index_groups=SEQ_GROUPS, tiled=True)

    def factors(own, first):
        beside = exchange(own, first << 6)
        here = pltpu.with_memory_space_constraint(own, pltpu.HBM)
        return [here, from_other_core(own), beside, from_other_core(beside)]

    keep, *sent = wide_products(
        [h, h_core, *h_from] + factors(d_query, 1),
        [g, g_core, *g_from] + factors(attended, 3),
    )
    sent = [block.astype(half) for block in sent]
    wide_got = [exchange(block, m << 6) for m, block in zip((3, 1), sent)]
    branch = dot(attended, w_out, ((1,), (1,))).astype(bf)

    terms, _, branch = lax.optimization_barrier((terms, sent, branch))
    d_kv = own_terms(terms.astype(f32))
    narrow, *sent = narrow_products(h, h_core, d_kv, from_other_core(d_kv))
    narrow_got = [exchange(block.astype(half), m << 6) for m, block in zip((3, 1, 2), sent)]

    part = after_x(keep, jnp.stack(wide_got).astype(f32), narrow, jnp.stack(narrow_got).astype(f32))
    part = lax.all_to_all(part.astype(half), AXES, 0, 0, axis_index_groups=YZ_GROUPS, tiled=True)
    grad_query, grad_out, grad_key, grad_value = last_sum(part.astype(f32))
    return branch[None], grad_query, grad_key, grad_value, grad_out


def solution(mesh):
    return jax.shard_map(
        local,
        mesh=mesh,
        in_specs=(P("dp", "seq", None), P(), P(), P(), P(), P("dp", "seq", None)),
        out_specs=(
            P("dp", "seq", None),
            P(("dp", "seq"), None),
            P(("dp", "seq"), None),
            P(("dp", "seq"), None),
            P(("dp", "seq"), None),
        ),
        check_vma=False,
    )
```

```python
import functools

import jax
import jax.numpy as jnp
from jax import lax
from jax.experimental import pallas as pl
from jax.experimental.pallas import tpu as pltpu
from jax.sharding import PartitionSpec as P

HEADS = 4
HD = 128
SCALE = HD ** (-0.5)
LOG2_E = 1.4426950408889634
AXES = ("dp", "seq")
MIB = 1024 * 1024


def place(x, y, z, core):
    return x * 64 + (z >> 1) * 16 + core * 8 + (z & 1) * 4 + y


SEQ_GROUPS = [
    [place(x, y, 2 * z + low, c) for y in range(4) for low in range(2)] for x in range(4) for z in range(4) for c in range(2)
]
YZ_ORDER = [(y, (i + 2 * y) % 8) for i in range(8) for y in range(4)]
YZ_GROUPS = [[place(x, y, z, c) for y, z in YZ_ORDER] for x in range(4) for c in range(2)]


def dot(left, right, dims):
    return lax.dot_general(left, right, (dims, ((), ())), preferred_element_type=jnp.float32)


def exchange(value, mask):
    return lax.ppermute(value, AXES, [(i, i ^ mask) for i in range(256)])


def from_other_core(value):
    return exchange(value, 8)


def exponent(values):
    top = jnp.max(jnp.max(jnp.abs(values), axis=0, keepdims=True), axis=1, keepdims=True)
    return jnp.ceil(jnp.log2(jnp.maximum(top, 1e-30))) - 13.0


def unscaled(ref, block, values, exponents):
    return ref[block, values, :] * jnp.exp2(ref[block, exponents, :])


def project_kernel(hidden_ref, w_key_ref, w_value_ref, out_ref):
    hidden = hidden_ref[...]
    for i, ref in enumerate((w_key_ref, w_value_ref)):
        block = dot(hidden, ref[...], ((1,), (0,))).astype(jnp.bfloat16)
        for b in range(out_ref.shape[0]):
            out_ref[b, :, i * HD : (i + 1) * HD] = block


def project(hidden, w_key, w_value):
    hidden, w_key, w_value = (pltpu.with_memory_space_constraint(v, pltpu.HBM) for v in (hidden, w_key, w_value))
    return pl.pallas_call(
        project_kernel,
        out_shape=jax.ShapeDtypeStruct((8, hidden.shape[0], 2 * HD), jnp.bfloat16),
        compiler_params=pltpu.CompilerParams(vmem_limit_bytes=16 * MIB),
        name="project",
    )(hidden, w_key, w_value)


def turn_kernel(pieces, place_ref, side_ref, *refs):
    turned_ref = refs[-1]
    turned_ref[...] = side_ref[...].T
    for ref, (far, masks) in zip(refs, pieces):
        for i, mask in enumerate(masks):
            for z_hi in range(4):
                start = 384 * (place_ref[0] ^ mask) + 96 * z_hi + 48 * (place_ref[1] ^ far)
                first = 192 * i + 48 * z_hi
                ref[first : first + 48, :] = turned_ref[pl.ds(pl.multiple_of(start, 16), 48), :]


def turn(place, side, pieces):
    tokens, width = side.shape
    shapes = [(len(masks) * width // 8, tokens) for _, masks in pieces]
    return pl.pallas_call(
        functools.partial(turn_kernel, pieces),
        grid_spec=pltpu.PrefetchScalarGridSpec(
            num_scalar_prefetch=1,
            grid=(1,),
            in_specs=[pl.BlockSpec((tokens, width), lambda i, place: (0, 0))],
            out_specs=[pl.BlockSpec(shape, lambda i, place: (0, 0)) for shape in shapes],
            scratch_shapes=[pltpu.VMEM((width, tokens), side.dtype)],
        ),
        out_shape=[jax.ShapeDtypeStruct(shape, side.dtype) for shape in shapes],
        compiler_params=pltpu.CompilerParams(vmem_limit_bytes=12 * MIB),
        name="turn",
    )(place, side)


def attention_kernel(
    q_hbm, da_hbm, kv_hbm, d_query_hbm, attended_hbm, dkv_ref,
    q_ref, da_ref, k_ref, v_ref, d_query_ref, attended_ref, scores_ref, d_probs_ref, probs_ref, d_scores_ref,
    in_sems, out_sems,
):
    bf = jnp.bfloat16
    blocks, _, tokens = dkv_ref.shape
    chunk = 16
    head_cols = lambda h: slice(h * HD, (h + 1) * HD)
    block_rows = lambda b: slice(b * tokens, (b + 1) * tokens)
    arriving = [
        pltpu.make_async_copy(source, ref, in_sems.at[i])
        for i, (source, ref) in enumerate(
            (
                (kv_hbm.at[:, pl.ds(0, HD)], k_ref),
                (q_hbm, q_ref),
                (kv_hbm.at[:, pl.ds(HD, HD)], v_ref),
                (da_hbm, da_ref),
            )
        )
    ]
    for copy in arriving:
        copy.start()
    for copy in arriving:
        copy.wait()

    def ahead(h):
        def make(b, side_ref, other_ref, to_ref):
            def run():
                to_ref[h % 2, :, block_rows(b)] = dot(side_ref[:, head_cols(h)], other_ref[block_rows(b), :], ((1,), (1,)))

            return run

        return [
            make(b, *refs)
            for b in range(blocks)
            for refs in ((q_ref, k_ref, scores_ref), (da_ref, v_ref, d_probs_ref))
        ]

    def softmax(h, i):
        rows = slice(i * chunk, (i + 1) * chunk)
        scores = scores_ref[h % 2, rows, :]
        shifted = jnp.exp2((scores - jnp.max(scores, axis=1, keepdims=True)) * (SCALE * LOG2_E))
        probs = shifted * (1.0 / jnp.sum(shifted, axis=1, keepdims=True))
        d_probs = d_probs_ref[h % 2, rows, :]
        delta = jnp.sum(d_probs * probs, axis=1, keepdims=True)
        probs_ref[h % 2, rows, :] = probs.astype(bf)
        d_scores_ref[h % 2, rows, :] = (probs * (d_probs - delta)).astype(bf)

    def behind(h):
        sides = [ref[:, head_cols(h)].T for ref in (q_ref, da_ref)]

        def terms(b, i, from_ref):
            def run():
                term = dot(sides[i], from_ref[h % 2, :, block_rows(b)], ((1,), (0,)))
                rows = slice(i * HD, (i + 1) * HD)
                total = term if h == 0 else dkv_ref[b, rows, :] + term
                if h == HEADS - 1:
                    total = total * (SCALE, 1.0)[i]
                    power = exponent(total)
                    total = total * jnp.exp2(-power)
                    dkv_ref[b, pl.ds(2 * HD + 4 * i, 4), :] = jnp.broadcast_to(power, (4, tokens))
                dkv_ref[b, rows, :] = total

            return run

        def rows_of(from_ref, other_ref, to_ref, scale):
            def run():
                product = dot(from_ref[h % 2], other_ref[...], ((1,), (0,)))
                to_ref[:, head_cols(h)] = (product * scale if scale else product).astype(bf)

            return run

        work = [terms(b, i, ref) for b in range(blocks) for i, ref in enumerate((d_scores_ref, probs_ref))]
        rows = [rows_of(probs_ref, v_ref, attended_ref, None), rows_of(d_scores_ref, k_ref, d_query_ref, SCALE)]
        if h == HEADS - 1:
            return rows + [copy.start for copy in leaving] + work
        work.insert(4, rows[0])
        work.insert(13, rows[1])
        return work

    leaving = [
        pltpu.make_async_copy(ref, target, out_sems.at[i])
        for i, (ref, target) in enumerate(((d_query_ref, d_query_hbm), (attended_ref, attended_hbm)))
    ]
    for run in ahead(0):
        run()
    for h in range(HEADS):
        beside = []
        if h + 1 < HEADS:
            beside += [(n / 16, run) for n, run in enumerate(ahead(h + 1))]
        if h > 0:
            beside += [(n / 18, run) for n, run in enumerate(behind(h - 1))]
        beside.sort(key=lambda entry: entry[0])
        steps = tokens // chunk
        for i in range(steps):
            softmax(h, i)
            for at, run in beside:
                if i <= at * steps < i + 1:
                    run()
    for run in behind(HEADS - 1):
        run()

    for copy in leaving:
        copy.wait()


def attention(queries, d_att, keys_values):
    tokens, inner = queries.shape
    length = keys_values.shape[0]
    blocks = length // tokens
    anywhere = pl.BlockSpec(memory_space=pl.ANY)
    small, large = pltpu.VMEM((tokens, inner), jnp.bfloat16), pltpu.VMEM((length, HD), jnp.bfloat16)
    wide, half = pltpu.VMEM((2, tokens, length), jnp.float32), pltpu.VMEM((2, tokens, length), jnp.bfloat16)
    operands = [pltpu.with_memory_space_constraint(v, pltpu.HBM) for v in (queries, d_att, keys_values)]
    return pl.pallas_call(
        attention_kernel,
        in_specs=[anywhere] * 3,
        out_specs=[anywhere, anywhere, pl.BlockSpec(memory_space=pltpu.VMEM)],
        out_shape=[
            pltpu.HBM((tokens, inner), jnp.bfloat16),
            pltpu.HBM((tokens, inner), jnp.bfloat16),
            jax.ShapeDtypeStruct((blocks, 2 * HD + 8, tokens), jnp.float32),
        ],
        scratch_shapes=[small, small, large, large, small, small, wide, wide, half, half]
        + [pltpu.SemaphoreType.DMA((4,)), pltpu.SemaphoreType.DMA((2,))],
        compiler_params=pltpu.CompilerParams(vmem_limit_bytes=32 * MIB),
        cost_estimate=pl.CostEstimate(
            flops=12 * tokens * inner * length, bytes_accessed=4 << 20, transcendentals=tokens * HEADS * length
        ),
        name="attention",
    )(*operands)


def store_scaled(values, ref):
    power = exponent(values)
    ref[:-8, :] = values * jnp.exp2(-power)
    ref[-8:, :] = jnp.broadcast_to(power, (8, values.shape[1]))


def wide_kernel(*refs):
    keep_hbm, *send_refs = refs[16:19]
    sides_ref, factors_ref, keep_ref, in_sems, out_sems = refs[19:]
    rows, cols = keep_ref.shape[0], send_refs[0].shape[1]
    arriving = []
    for i in range(2):
        arriving.append([])
        for n in range(4):
            side, factor = refs[8 * i + n], refs[8 * i + 4 + n]
            copies = (
                pltpu.make_async_copy(side.at[pl.ds(0, 2 * rows), :], sides_ref.at[i, n], in_sems.at[i, n, 0]),
                pltpu.make_async_copy(factor, factors_ref.at[i, n], in_sems.at[i, n, 1]),
            )
            for copy in copies:
                copy.start()
            arriving[i].extend(copies)
    leaving = []
    for i in range(2):
        for copy in arriving[i]:
            copy.wait()
        product = None
        for n in range(4):
            term = dot(sides_ref[i, n], factors_ref[i, n], ((1,), (0,)))
            product = term if product is None else product + term
        here = (slice(None), pl.ds(i * cols, cols))
        keep_ref[:, i * cols : (i + 1) * cols] = product[:rows]
        leaving.append(pltpu.make_async_copy(keep_ref.at[here], keep_hbm.at[here], out_sems.at[i]))
        leaving[i].start()
        store_scaled(product[rows:], send_refs[i])
    for copy in leaving:
        copy.wait()


def wide_products(query, out):
    rows, tokens = out[0].shape[0] // 2, out[0].shape[1]
    cols = out[4].shape[1]
    anywhere, fast = pl.BlockSpec(memory_space=pl.ANY), pl.BlockSpec(memory_space=pltpu.VMEM)
    return pl.pallas_call(
        wide_kernel,
        in_specs=[anywhere] * 16,
        out_specs=[anywhere, fast, fast],
        out_shape=[
            pltpu.HBM((rows, 2 * cols), jnp.float32),
            jax.ShapeDtypeStruct((rows + 8, cols), jnp.float32),
            jax.ShapeDtypeStruct((rows + 8, cols), jnp.float32),
        ],
        scratch_shapes=[
            pltpu.VMEM((2, 4, 2 * rows, tokens), jnp.bfloat16),
            pltpu.VMEM((2, 4, tokens, cols), jnp.bfloat16),
            pltpu.VMEM((rows, 2 * cols), jnp.float32),
            pltpu.SemaphoreType.DMA((2, 4, 2)),
            pltpu.SemaphoreType.DMA((2,)),
        ],
        compiler_params=pltpu.CompilerParams(vmem_limit_bytes=20 * MIB),
        cost_estimate=pl.CostEstimate(flops=1 << 30, bytes_accessed=5 << 20, transcendentals=0),
        name="wide",
    )(*query, *out)


def narrow_kernel(mine_ref, theirs_ref, own_ref, other_ref, keep_ref, three_ref, one_ref, two_ref):
    product = None
    for side_ref, terms_ref in ((mine_ref, own_ref), (theirs_ref, other_ref)):
        side = side_ref[...]
        rest = terms_ref[...]
        for _ in range(2):
            piece = rest.astype(jnp.bfloat16)
            rest = rest - piece.astype(jnp.float32)
            term = dot(side, piece, ((1,), (1,)))
            product = term if product is None else product + term
    rows = keep_ref.shape[0]
    keep_ref[...] = product[:rows]
    powers = [jnp.broadcast_to(exponent(product[:, i * HD : (i + 1) * HD]), (8, HD)) for i in range(2)]
    power = jnp.concatenate(powers, axis=1)
    factor = jnp.exp2(-power[:1])
    for i, ref in enumerate((three_ref, one_ref, two_ref)):
        ref[:rows, :] = product[(i + 1) * rows : (i + 2) * rows] * factor
        ref[rows:, :] = power


def narrow_products(mine, theirs, own, other):
    rows = mine.shape[0] // 4
    cols = own.shape[0]
    sent = jax.ShapeDtypeStruct((rows + 8, cols), jnp.float32)
    return pl.pallas_call(
        narrow_kernel,
        out_shape=[pltpu.HBM((rows, cols), jnp.float32), sent, sent, sent],
        compiler_params=pltpu.CompilerParams(vmem_limit_bytes=16 * MIB),
        cost_estimate=pl.CostEstimate(flops=1, bytes_accessed=1, transcendentals=0),
        name="narrow",
    )(mine, theirs, own, other)


def own_terms_kernel(terms_ref, out_ref):
    for i in range(2):
        rows, powers = pl.ds(i * HD, HD), pl.ds(2 * HD + 4 * i, 1)
        total = unscaled(terms_ref, 0, rows, powers)
        for b in range(1, terms_ref.shape[0]):
            total = total + unscaled(terms_ref, b, rows, powers)
        out_ref[rows, :] = total


def own_terms(terms):
    return pl.pallas_call(
        own_terms_kernel,
        out_shape=jax.ShapeDtypeStruct((2 * HD, terms.shape[2]), jnp.float32),
        compiler_params=pltpu.CompilerParams(vmem_limit_bytes=8 * MIB),
        cost_estimate=pl.CostEstimate(flops=1, bytes_accessed=1, transcendentals=0),
        name="own_terms",
    )(terms)


def after_x_kernel(wide_ref, wide_got_ref, narrow_ref, narrow_got_ref, out_ref, total_ref):
    rows = wide_ref.shape[0]
    cols = 4 * HD
    scaled = lambda ref, i, here: ref[i, :rows, here] * jnp.exp2(ref[i, rows : rows + 1, here])
    for i, (first, width) in enumerate(((0, cols), (cols, cols), (2 * cols, HD), (2 * cols + HD, HD))):
        if i < 2:
            total = wide_ref[:, first : first + width] + scaled(wide_got_ref, i, pl.ds(0, cols))
        else:
            here = pl.ds(first - 2 * cols, HD)
            total = narrow_ref[:, here]
            for m in range(3):
                total = total + scaled(narrow_got_ref, m, here)
        top = exponent(total)
        total_ref[:, first : first + width] = total * jnp.exp2(-top)
        out_ref[:, 60 + i, :] = jnp.broadcast_to(top, (out_ref.shape[0], HD))
    for k, (y, z) in enumerate(YZ_ORDER):
        start = 48 * (z // 2) + 6 * (4 * (z % 2) + y)
        for j in range(10):
            out_ref[k, 6 * j : 6 * j + 6, :] = total_ref[start : start + 6, j * HD : (j + 1) * HD]


def after_x(wide, wide_got, narrow, narrow_got):
    rows, cols = wide.shape
    shape = (rows // 6, 64, HD)
    return pl.pallas_call(
        after_x_kernel,
        out_shape=jax.ShapeDtypeStruct(shape, jnp.float32),
        scratch_shapes=[pltpu.VMEM((rows, cols + narrow.shape[1]), jnp.float32)],
        compiler_params=pltpu.CompilerParams(vmem_limit_bytes=16 * MIB),
        name="after_x",
    )(wide, wide_got, narrow, narrow_got)


def last_sum_kernel(got_ref, query_ref, out_ref, key_ref, value_ref):
    first = 0
    for i, ref in enumerate((query_ref, out_ref, key_ref, value_ref)):
        tiles = ref.shape[1] // HD
        rows = pl.ds(first, 6 * tiles)
        total = unscaled(got_ref, 0, rows, pl.ds(60 + i, 1))
        for b in range(1, got_ref.shape[0]):
            total = total + unscaled(got_ref, b, rows, pl.ds(60 + i, 1))
        for j in range(tiles):
            ref[:, j * HD : (j + 1) * HD] = total[6 * j : 6 * j + 6]
        first += 6 * tiles


def last_sum(got):
    shape = lambda cols: jax.ShapeDtypeStruct((6, cols), jnp.float32)
    return pl.pallas_call(
        last_sum_kernel,
        out_shape=[shape(4 * HD), shape(4 * HD), shape(HD), shape(HD)],
        compiler_params=pltpu.CompilerParams(vmem_limit_bytes=8 * MIB),
        name="last_sum",
    )(got)


def local(normed, w_query, w_key, w_value, w_out, cotangent):
    hidden = normed[0]
    grads_in = cotangent[0]
    tokens = hidden.shape[0]
    bf, half = jnp.bfloat16, jnp.float16
    dp = lax.axis_index("dp")
    x, core = dp >> 3, dp & 1
    f32 = jnp.float32

    gathered = lax.all_to_all(project(hidden, w_key, w_value), AXES, 0, 0, axis_index_groups=SEQ_GROUPS, tiled=True)

    queries = dot(hidden, w_query, ((1,), (0,))).astype(bf)
    d_att = dot(grads_in, w_out, ((1,), (0,))).astype(bf)
    place_now = jnp.stack([x, core])
    h, h_core, *h_far = turn(place_now, hidden, ((0, (0, 3, 1, 2)), (1, (0, 3, 1, 2)), (0, (1, 2)), (1, (1, 2))))
    g, g_core, *g_far = turn(place_now, grads_in, ((0, (0, 1)), (1, (0, 1)), (0, (3, 2)), (1, (3, 2))))
    h_from = [exchange(h_far[0], 1 << 6), exchange(h_far[1], (1 << 6) | 8)]
    g_from = [exchange(g_far[0], 3 << 6), exchange(g_far[1], (3 << 6) | 8)]
    h_core, g_core = from_other_core(h_core), from_other_core(g_core)

    d_query, attended, terms = attention(queries, d_att, gathered.reshape(8 * tokens, 2 * HD))
    terms, d_query, attended, h_from, g_from, h_core, g_core = lax.optimization_barrier(
        (terms, d_query, attended, h_from, g_from, h_core, g_core)
    )
    terms = lax.all_to_all(terms.astype(half), AXES, 0, 0, axis_index_groups=SEQ_GROUPS, tiled=True)

    def factors(own, first):
        beside = exchange(own, first << 6)
        here = pltpu.with_memory_space_constraint(own, pltpu.HBM)
        return [here, from_other_core(own), beside, from_other_core(beside)]

    keep, *sent = wide_products(
        [h, h_core, *h_from] + factors(d_query, 1),
        [g, g_core, *g_from] + factors(attended, 3),
    )
    sent = [block.astype(half) for block in sent]
    wide_got = [exchange(block, m << 6) for m, block in zip((3, 1), sent)]
    branch = dot(attended, w_out, ((1,), (1,))).astype(bf)

    terms, _, branch = lax.optimization_barrier((terms, sent, branch))
    d_kv = own_terms(terms.astype(f32))
    narrow, *sent = narrow_products(h, h_core, d_kv, from_other_core(d_kv))
    narrow_got = [exchange(block.astype(half), m << 6) for m, block in zip((3, 1, 2), sent)]

    part = after_x(keep, jnp.stack(wide_got).astype(f32), narrow, jnp.stack(narrow_got).astype(f32))
    part = lax.all_to_all(part.astype(half), AXES, 0, 0, axis_index_groups=YZ_GROUPS, tiled=True)
    grad_query, grad_out, grad_key, grad_value = last_sum(part.astype(f32))
    return branch[None], grad_query, grad_key, grad_value, grad_out


def solution(mesh):
    return jax.shard_map(
        local,
        mesh=mesh,
        in_specs=(P("dp", "seq", None), P(), P(), P(), P(), P("dp", "seq", None)),
        out_specs=(
            P("dp", "seq", None),
            P(("dp", "seq"), None),
            P(("dp", "seq"), None),
            P(("dp", "seq"), None),
            P(("dp", "seq"), None),
        ),
        check_vma=False,
    )
```

```python
import functools

import jax
import jax.numpy as jnp
from jax import lax
from jax.experimental import pallas as pl
from jax.experimental.pallas import tpu as pltpu
from jax.sharding import PartitionSpec as P

HEADS = 4
HD = 128
SCALE = HD ** (-0.5)
LOG2_E = 1.4426950408889634
AXES = ("dp", "seq")
MIB = 1024 * 1024


def place(x, y, z, core):
    return x * 64 + (z >> 1) * 16 + core * 8 + (z & 1) * 4 + y


SEQ_GROUPS = [
    [place(x, y, 2 * z + low, c) for y in range(4) for low in range(2)] for x in range(4) for z in range(4) for c in range(2)
]
YZ_ORDER = [(y, (i + 2 * y) % 8) for i in range(8) for y in range(4)]
YZ_GROUPS = [[place(x, y, z, c) for y, z in YZ_ORDER] for x in range(4) for c in range(2)]


def dot(left, right, dims):
    return lax.dot_general(left, right, (dims, ((), ())), preferred_element_type=jnp.float32)


def exchange(value, mask):
    return lax.ppermute(value, AXES, [(i, i ^ mask) for i in range(256)])


def from_other_core(value):
    return exchange(value, 8)


def exponent(values):
    top = jnp.max(jnp.max(jnp.abs(values), axis=0, keepdims=True), axis=1, keepdims=True)
    return jnp.ceil(jnp.log2(jnp.maximum(top, 1e-30))) - 13.0


def unscaled(ref, block, values, exponents):
    return ref[block, values, :] * jnp.exp2(ref[block, exponents, :])


def project_kernel(hidden_ref, w_key_ref, w_value_ref, out_ref):
    hidden = hidden_ref[...]
    for i, ref in enumerate((w_key_ref, w_value_ref)):
        block = dot(hidden, ref[...], ((1,), (0,))).astype(jnp.bfloat16)
        for b in range(out_ref.shape[0]):
            out_ref[b, :, i * HD : (i + 1) * HD] = block


def project(hidden, w_key, w_value):
    hidden, w_key, w_value = (pltpu.with_memory_space_constraint(v, pltpu.HBM) for v in (hidden, w_key, w_value))
    return pl.pallas_call(
        project_kernel,
        out_shape=jax.ShapeDtypeStruct((8, hidden.shape[0], 2 * HD), jnp.bfloat16),
        compiler_params=pltpu.CompilerParams(vmem_limit_bytes=16 * MIB),
        name="project",
    )(hidden, w_key, w_value)


def turn_kernel(pieces, place_ref, side_ref, *refs):
    turned_ref = refs[-1]
    turned_ref[...] = side_ref[...].T
    for ref, (far, masks) in zip(refs, pieces):
        for i, mask in enumerate(masks):
            for z_hi in range(4):
                start = 384 * (place_ref[0] ^ mask) + 96 * z_hi + 48 * (place_ref[1] ^ far)
                first = 192 * i + 48 * z_hi
                ref[first : first + 48, :] = turned_ref[pl.ds(pl.multiple_of(start, 16), 48), :]


def turn(place, side, pieces):
    tokens, width = side.shape
    shapes = [(len(masks) * width // 8, tokens) for _, masks in pieces]
    return pl.pallas_call(
        functools.partial(turn_kernel, pieces),
        grid_spec=pltpu.PrefetchScalarGridSpec(
            num_scalar_prefetch=1,
            grid=(1,),
            in_specs=[pl.BlockSpec((tokens, width), lambda i, place: (0, 0))],
            out_specs=[pl.BlockSpec(shape, lambda i, place: (0, 0)) for shape in shapes],
            scratch_shapes=[pltpu.VMEM((width, tokens), side.dtype)],
        ),
        out_shape=[jax.ShapeDtypeStruct(shape, side.dtype) for shape in shapes],
        compiler_params=pltpu.CompilerParams(vmem_limit_bytes=12 * MIB),
        name="turn",
    )(place, side)


def attention_kernel(
    q_hbm, da_hbm, kv_hbm, d_query_hbm, attended_hbm, dkv_ref,
    q_ref, da_ref, k_ref, v_ref, d_query_ref, attended_ref, scores_ref, d_probs_ref, probs_ref, d_scores_ref,
    in_sems, out_sems,
):
    bf = jnp.bfloat16
    blocks, _, tokens = dkv_ref.shape
    chunk = 16
    head_cols = lambda h: slice(h * HD, (h + 1) * HD)
    block_rows = lambda b: slice(b * tokens, (b + 1) * tokens)
    arriving = [
        pltpu.make_async_copy(source, ref, in_sems.at[i])
        for i, (source, ref) in enumerate(
            (
                (kv_hbm.at[:, pl.ds(0, HD)], k_ref),
                (q_hbm, q_ref),
                (kv_hbm.at[:, pl.ds(HD, HD)], v_ref),
                (da_hbm, da_ref),
            )
        )
    ]
    for copy in arriving:
        copy.start()
    for copy in arriving:
        copy.wait()

    def ahead(h):
        def make(b, side_ref, other_ref, to_ref):
            def run():
                to_ref[h % 2, :, block_rows(b)] = dot(side_ref[:, head_cols(h)], other_ref[block_rows(b), :], ((1,), (1,)))

            return run

        return [
            make(b, *refs)
            for b in range(blocks)
            for refs in ((q_ref, k_ref, scores_ref), (da_ref, v_ref, d_probs_ref))
        ]

    def softmax(h, i):
        rows = slice(i * chunk, (i + 1) * chunk)
        scores = scores_ref[h % 2, rows, :]
        shifted = jnp.exp2((scores - jnp.max(scores, axis=1, keepdims=True)) * (SCALE * LOG2_E))
        probs = shifted * (1.0 / jnp.sum(shifted, axis=1, keepdims=True))
        d_probs = d_probs_ref[h % 2, rows, :]
        delta = jnp.sum(d_probs * probs, axis=1, keepdims=True)
        probs_ref[h % 2, rows, :] = probs.astype(bf)
        d_scores_ref[h % 2, rows, :] = (probs * (d_probs - delta)).astype(bf)

    def behind(h):
        sides = [ref[:, head_cols(h)].T for ref in (q_ref, da_ref)]

        def terms(b, i, from_ref):
            def run():
                term = dot(sides[i], from_ref[h % 2, :, block_rows(b)], ((1,), (0,)))
                rows = slice(i * HD, (i + 1) * HD)
                total = term if h == 0 else dkv_ref[b, rows, :] + term
                if h == HEADS - 1:
                    total = total * (SCALE, 1.0)[i]
                    power = exponent(total)
                    total = total * jnp.exp2(-power)
                    dkv_ref[b, pl.ds(2 * HD + 4 * i, 4), :] = jnp.broadcast_to(power, (4, tokens))
                dkv_ref[b, rows, :] = total

            return run

        def rows_of(from_ref, other_ref, to_ref, scale):
            def run():
                product = dot(from_ref[h % 2], other_ref[...], ((1,), (0,)))
                to_ref[:, head_cols(h)] = (product * scale if scale else product).astype(bf)

            return run

        work = [terms(b, i, ref) for b in range(blocks) for i, ref in enumerate((d_scores_ref, probs_ref))]
        rows = [rows_of(probs_ref, v_ref, attended_ref, None), rows_of(d_scores_ref, k_ref, d_query_ref, SCALE)]
        if h == HEADS - 1:
            return rows + [copy.start for copy in leaving] + work
        work.insert(4, rows[0])
        work.insert(13, rows[1])
        return work

    leaving = [
        pltpu.make_async_copy(ref, target, out_sems.at[i])
        for i, (ref, target) in enumerate(((d_query_ref, d_query_hbm), (attended_ref, attended_hbm)))
    ]
    for run in ahead(0):
        run()
    for h in range(HEADS):
        beside = []
        if h + 1 < HEADS:
            beside += [(n / 16, run) for n, run in enumerate(ahead(h + 1))]
        if h > 0:
            beside += [(n / 18, run) for n, run in enumerate(behind(h - 1))]
        beside.sort(key=lambda entry: entry[0])
        steps = tokens // chunk
        for i in range(steps):
            softmax(h, i)
            for at, run in beside:
                if i <= at * steps < i + 1:
                    run()
    for run in behind(HEADS - 1):
        run()

    for copy in leaving:
        copy.wait()


def attention(queries, d_att, keys_values):
    tokens, inner = queries.shape
    length = keys_values.shape[0]
    blocks = length // tokens
    anywhere = pl.BlockSpec(memory_space=pl.ANY)
    small, large = pltpu.VMEM((tokens, inner), jnp.bfloat16), pltpu.VMEM((length, HD), jnp.bfloat16)
    wide, half = pltpu.VMEM((2, tokens, length), jnp.float32), pltpu.VMEM((2, tokens, length), jnp.bfloat16)
    operands = [pltpu.with_memory_space_constraint(v, pltpu.HBM) for v in (queries, d_att, keys_values)]
    return pl.pallas_call(
        attention_kernel,
        in_specs=[anywhere] * 3,
        out_specs=[anywhere, anywhere, pl.BlockSpec(memory_space=pltpu.VMEM)],
        out_shape=[
            pltpu.HBM((tokens, inner), jnp.bfloat16),
            pltpu.HBM((tokens, inner), jnp.bfloat16),
            jax.ShapeDtypeStruct((blocks, 2 * HD + 8, tokens), jnp.float32),
        ],
        scratch_shapes=[small, small, large, large, small, small, wide, wide, half, half]
        + [pltpu.SemaphoreType.DMA((4,)), pltpu.SemaphoreType.DMA((2,))],
        compiler_params=pltpu.CompilerParams(vmem_limit_bytes=32 * MIB),
        cost_estimate=pl.CostEstimate(
            flops=12 * tokens * inner * length, bytes_accessed=4 << 20, transcendentals=tokens * HEADS * length
        ),
        name="attention",
    )(*operands)


def store_scaled(values, ref):
    power = exponent(values)
    ref[:-8, :] = values * jnp.exp2(-power)
    ref[-8:, :] = jnp.broadcast_to(power, (8, values.shape[1]))


def wide_kernel(*refs):
    keep_hbm, *send_refs = refs[16:19]
    sides_ref, factors_ref, keep_ref, in_sems, out_sems = refs[19:]
    rows, cols = keep_ref.shape[0], send_refs[0].shape[1]
    tokens = factors_ref.shape[1] // 4
    arriving = []
    for i in range(2):
        arriving.append([])
        for n in range(4):
            side, factor = refs[8 * i + n], refs[8 * i + 4 + n]
            copies = (
                pltpu.make_async_copy(side.at[pl.ds(0, 2 * rows), :], sides_ref.at[i, :, pl.ds(n * tokens, tokens)], in_sems.at[i, n, 0]),
                pltpu.make_async_copy(factor, factors_ref.at[i, pl.ds(n * tokens, tokens), :], in_sems.at[i, n, 1]),
            )
            for copy in copies:
                copy.start()
            arriving[i].extend(copies)
    leaving = []
    for i in range(2):
        for copy in arriving[i]:
            copy.wait()
        product = dot(sides_ref[i], factors_ref[i], ((1,), (0,)))
        here = (slice(None), pl.ds(i * cols, cols))
        keep_ref[:, i * cols : (i + 1) * cols] = product[:rows]
        leaving.append(pltpu.make_async_copy(keep_ref.at[here], keep_hbm.at[here], out_sems.at[i]))
        leaving[i].start()
        store_scaled(product[rows:], send_refs[i])
    for copy in leaving:
        copy.wait()


def wide_products(query, out):
    rows, tokens = out[0].shape[0] // 2, out[0].shape[1]
    cols = out[4].shape[1]
    anywhere, fast = pl.BlockSpec(memory_space=pl.ANY), pl.BlockSpec(memory_space=pltpu.VMEM)
    return pl.pallas_call(
        wide_kernel,
        in_specs=[anywhere] * 16,
        out_specs=[anywhere, fast, fast],
        out_shape=[
            pltpu.HBM((rows, 2 * cols), jnp.float32),
            jax.ShapeDtypeStruct((rows + 8, cols), jnp.float32),
            jax.ShapeDtypeStruct((rows + 8, cols), jnp.float32),
        ],
        scratch_shapes=[
            pltpu.VMEM((2, 2 * rows, 4 * tokens), jnp.bfloat16),
            pltpu.VMEM((2, 4 * tokens, cols), jnp.bfloat16),
            pltpu.VMEM((rows, 2 * cols), jnp.float32),
            pltpu.SemaphoreType.DMA((2, 4, 2)),
            pltpu.SemaphoreType.DMA((2,)),
        ],
        compiler_params=pltpu.CompilerParams(vmem_limit_bytes=20 * MIB),
        cost_estimate=pl.CostEstimate(flops=1 << 30, bytes_accessed=5 << 20, transcendentals=0),
        name="wide",
    )(*query, *out)


def narrow_kernel(mine_ref, theirs_ref, own_ref, other_ref, keep_ref, three_ref, one_ref, two_ref):
    product = None
    for side_ref, terms_ref in ((mine_ref, own_ref), (theirs_ref, other_ref)):
        side = side_ref[...]
        rest = terms_ref[...]
        for _ in range(2):
            piece = rest.astype(jnp.bfloat16)
            rest = rest - piece.astype(jnp.float32)
            term = dot(side, piece, ((1,), (1,)))
            product = term if product is None else product + term
    rows = keep_ref.shape[0]
    keep_ref[...] = product[:rows]
    powers = [jnp.broadcast_to(exponent(product[:, i * HD : (i + 1) * HD]), (8, HD)) for i in range(2)]
    power = jnp.concatenate(powers, axis=1)
    factor = jnp.exp2(-power[:1])
    for i, ref in enumerate((three_ref, one_ref, two_ref)):
        ref[:rows, :] = product[(i + 1) * rows : (i + 2) * rows] * factor
        ref[rows:, :] = power


def narrow_products(mine, theirs, own, other):
    rows = mine.shape[0] // 4
    cols = own.shape[0]
    sent = jax.ShapeDtypeStruct((rows + 8, cols), jnp.float32)
    return pl.pallas_call(
        narrow_kernel,
        out_shape=[pltpu.HBM((rows, cols), jnp.float32), sent, sent, sent],
        compiler_params=pltpu.CompilerParams(vmem_limit_bytes=16 * MIB),
        cost_estimate=pl.CostEstimate(flops=1, bytes_accessed=1, transcendentals=0),
        name="narrow",
    )(mine, theirs, own, other)


def own_terms_kernel(terms_ref, out_ref):
    for i in range(2):
        rows, powers = pl.ds(i * HD, HD), pl.ds(2 * HD + 4 * i, 1)
        total = unscaled(terms_ref, 0, rows, powers)
        for b in range(1, terms_ref.shape[0]):
            total = total + unscaled(terms_ref, b, rows, powers)
        out_ref[rows, :] = total


def own_terms(terms):
    return pl.pallas_call(
        own_terms_kernel,
        out_shape=jax.ShapeDtypeStruct((2 * HD, terms.shape[2]), jnp.float32),
        compiler_params=pltpu.CompilerParams(vmem_limit_bytes=8 * MIB),
        cost_estimate=pl.CostEstimate(flops=1, bytes_accessed=1, transcendentals=0),
        name="own_terms",
    )(terms)


def after_x_kernel(wide_ref, wide_got_ref, narrow_ref, narrow_got_ref, out_ref, total_ref):
    rows = wide_ref.shape[0]
    cols = 4 * HD
    scaled = lambda ref, i, here: ref[i, :rows, here] * jnp.exp2(ref[i, rows : rows + 1, here])
    for i, (first, width) in enumerate(((0, cols), (cols, cols), (2 * cols, HD), (2 * cols + HD, HD))):
        if i < 2:
            total = wide_ref[:, first : first + width] + scaled(wide_got_ref, i, pl.ds(0, cols))
        else:
            here = pl.ds(first - 2 * cols, HD)
            total = narrow_ref[:, here]
            for m in range(3):
                total = total + scaled(narrow_got_ref, m, here)
        top = exponent(total)
        total_ref[:, first : first + width] = total * jnp.exp2(-top)
        out_ref[:, 60 + i, :] = jnp.broadcast_to(top, (out_ref.shape[0], HD))
    for k, (y, z) in enumerate(YZ_ORDER):
        start = 48 * (z // 2) + 6 * (4 * (z % 2) + y)
        for j in range(10):
            out_ref[k, 6 * j : 6 * j + 6, :] = total_ref[start : start + 6, j * HD : (j + 1) * HD]


def after_x(wide, wide_got, narrow, narrow_got):
    rows, cols = wide.shape
    shape = (rows // 6, 64, HD)
    return pl.pallas_call(
        after_x_kernel,
        out_shape=jax.ShapeDtypeStruct(shape, jnp.float32),
        scratch_shapes=[pltpu.VMEM((rows, cols + narrow.shape[1]), jnp.float32)],
        compiler_params=pltpu.CompilerParams(vmem_limit_bytes=16 * MIB),
        name="after_x",
    )(wide, wide_got, narrow, narrow_got)


def last_sum_kernel(got_ref, query_ref, out_ref, key_ref, value_ref):
    first = 0
    for i, ref in enumerate((query_ref, out_ref, key_ref, value_ref)):
        tiles = ref.shape[1] // HD
        rows = pl.ds(first, 6 * tiles)
        total = unscaled(got_ref, 0, rows, pl.ds(60 + i, 1))
        for b in range(1, got_ref.shape[0]):
            total = total + unscaled(got_ref, b, rows, pl.ds(60 + i, 1))
        for j in range(tiles):
            ref[:, j * HD : (j + 1) * HD] = total[6 * j : 6 * j + 6]
        first += 6 * tiles


def last_sum(got):
    shape = lambda cols: jax.ShapeDtypeStruct((6, cols), jnp.float32)
    return pl.pallas_call(
        last_sum_kernel,
        out_shape=[shape(4 * HD), shape(4 * HD), shape(HD), shape(HD)],
        compiler_params=pltpu.CompilerParams(vmem_limit_bytes=8 * MIB),
        name="last_sum",
    )(got)


def local(normed, w_query, w_key, w_value, w_out, cotangent):
    hidden = normed[0]
    grads_in = cotangent[0]
    tokens = hidden.shape[0]
    bf, half = jnp.bfloat16, jnp.float16
    dp = lax.axis_index("dp")
    x, core = dp >> 3, dp & 1
    f32 = jnp.float32

    gathered = lax.all_to_all(project(hidden, w_key, w_value), AXES, 0, 0, axis_index_groups=SEQ_GROUPS, tiled=True)

    queries = dot(hidden, w_query, ((1,), (0,))).astype(bf)
    d_att = dot(grads_in, w_out, ((1,), (0,))).astype(bf)
    place_now = jnp.stack([x, core])
    h, h_core, *h_far = turn(place_now, hidden, ((0, (0, 3, 1, 2)), (1, (0, 3, 1, 2)), (0, (1, 2)), (1, (1, 2))))
    g, g_core, *g_far = turn(place_now, grads_in, ((0, (0, 1)), (1, (0, 1)), (0, (3, 2)), (1, (3, 2))))
    h_from = [exchange(h_far[0], 1 << 6), exchange(h_far[1], (1 << 6) | 8)]
    g_from = [exchange(g_far[0], 3 << 6), exchange(g_far[1], (3 << 6) | 8)]
    h_core, g_core = from_other_core(h_core), from_other_core(g_core)

    d_query, attended, terms = attention(queries, d_att, gathered.reshape(8 * tokens, 2 * HD))
    terms, d_query, attended, h_from, g_from, h_core, g_core = lax.optimization_barrier(
        (terms, d_query, attended, h_from, g_from, h_core, g_core)
    )
    terms = lax.all_to_all(terms.astype(half), AXES, 0, 0, axis_index_groups=SEQ_GROUPS, tiled=True)

    def factors(own, first):
        beside = exchange(own, first << 6)
        here = pltpu.with_memory_space_constraint(own, pltpu.HBM)
        return [here, from_other_core(own), beside, from_other_core(beside)]

    keep, *sent = wide_products(
        [h, h_core, *h_from] + factors(d_query, 1),
        [g, g_core, *g_from] + factors(attended, 3),
    )
    sent = [block.astype(half) for block in sent]
    wide_got = [exchange(block, m << 6) for m, block in zip((3, 1), sent)]
    branch = dot(attended, w_out, ((1,), (1,))).astype(bf)

    terms, _, branch = lax.optimization_barrier((terms, sent, branch))
    d_kv = own_terms(terms.astype(f32))
    narrow, *sent = narrow_products(h, h_core, d_kv, from_other_core(d_kv))
    narrow_got = [exchange(block.astype(half), m << 6) for m, block in zip((3, 1, 2), sent)]

    part = after_x(keep, jnp.stack(wide_got).astype(f32), narrow, jnp.stack(narrow_got).astype(f32))
    part = lax.all_to_all(part.astype(half), AXES, 0, 0, axis_index_groups=YZ_GROUPS, tiled=True)
    grad_query, grad_out, grad_key, grad_value = last_sum(part.astype(f32))
    return branch[None], grad_query, grad_key, grad_value, grad_out


def solution(mesh):
    return jax.shard_map(
        local,
        mesh=mesh,
        in_specs=(P("dp", "seq", None), P(), P(), P(), P(), P("dp", "seq", None)),
        out_specs=(
            P("dp", "seq", None),
            P(("dp", "seq"), None),
            P(("dp", "seq"), None),
            P(("dp", "seq"), None),
            P(("dp", "seq"), None),
        ),
        check_vma=False,
    )
```
